32 devices in a mesh: grp: 4 (over z), dat: 4 (over y, x), mdl: 2 (over core).
Axes of the slice: x: 2, y: 2, z: 4, core: 2. Of those that a mesh axis runs over, the one named last changes fastest.
Arguments:
- token_ids: int32 [64, 512], P(('grp', 'dat')), may hold values from 0 to 32127
- item_lengths: int32 [64], P(('grp', 'dat')), may hold values from 128 to 512
- prefix_lengths: int32 [64], P(('grp', 'dat')), may hold values from 1 to 64
- group_live: int32 [4], replicated, may hold values from 2 to 16, as said below
- partner: int32 [64], P(('grp', 'dat')), may hold values from 0 to 15, as said below
- embedding: float32 [768, 32128], P('dat'), may hold values from -6 to 6
- qkv_weight: float32 [768, 3, 768], P('dat', None, 'mdl'), may hold values from -0.21875 to 0.21875
- out_weight: float32 [768, 768], P('mdl', 'dat'), may hold values from -1.25 to 1.25
- up_weight: float32 [768, 3072], P('dat', 'mdl'), may hold values from -0.21875 to 0.21875
- down_weight: float32 [768, 3072], P('dat', 'mdl'), may hold values from -0.109375 to 0.109375
- bias_table: float32 [32, 12], P(None, 'mdl'), may hold values from -6 to 6
- norm_gains: float32 [3, 768], replicated, may hold values from 0.5 to 1.5
- embedding_first: float32 [768, 32128], P('dat')
- embedding_second: float32 [768, 32128], P('dat'), as said below
- qkv_first: float32 [768, 3, 768], P('dat', None, 'mdl')
- qkv_second: float32 [768, 3, 768], P('dat', None, 'mdl'), as said below
- out_first: float32 [768, 768], P('mdl', 'dat')
- out_second: float32 [768, 768], P('mdl', 'dat'), as said below
- up_first: float32 [768, 3072], P('dat', 'mdl')
- up_second: float32 [768, 3072], P('dat', 'mdl'), as said below
- down_first: float32 [768, 3072], P('dat', 'mdl')
- down_second: float32 [768, 3072], P('dat', 'mdl'), as said below
- bias_first: float32 [32, 12], P(None, 'mdl')
- bias_second: float32 [32, 12], P(None, 'mdl'), as said below
- gains_first: float32 [3, 768], replicated
- gains_second: float32 [3, 768], replicated, as said below
Outputs:
- loss_pair: float32 [2], replicated
- matrix_norms: float32 [9, 2], replicated
- embedding_momentum: float32 [768, 32128], P('dat')
- embedding_variance: float32 [768, 32128], P('dat')
- embedding_updated: float32 [768, 32128], P('dat')
- qkv_momentum: float32 [768, 3, 768], P('dat', None, 'mdl')
- qkv_variance: float32 [768, 3, 768], P('dat', None, 'mdl')
- qkv_updated: float32 [768, 3, 768], P('dat', None, 'mdl')
- out_momentum: float32 [768, 768], P('mdl', 'dat')
- out_variance: float32 [768, 768], P('mdl', 'dat')
- out_updated: float32 [768, 768], P('mdl', 'dat')
- up_momentum: float32 [768, 3072], P('dat', 'mdl')
- up_variance: float32 [768, 3072], P('dat', 'mdl')
- up_updated: float32 [768, 3072], P('dat', 'mdl')
- down_momentum: float32 [768, 3072], P('dat', 'mdl')
- down_variance: float32 [768, 3072], P('dat', 'mdl')
- down_updated: float32 [768, 3072], P('dat', 'mdl')
- bias_momentum: float32 [32, 12], P(None, 'mdl')
- bias_variance: float32 [32, 12], P(None, 'mdl')
- bias_updated: float32 [32, 12], P(None, 'mdl')
- gains_momentum: float32 [3, 768], replicated
- gains_variance: float32 [3, 768], replicated
- gains_updated: float32 [3, 768], replicated
The draws below stay inside these ranges and needn't reach their ends.
Inputs may be any that keep to these rules, and one draw needn't show every extreme that they name: `group_live`: Even; the items of a group at slots below it are live, the rest are dead; the last group is full. `partner`: for a live item, the slot of another live item of the same group whose partner is this item; a dead item names its own slot. `embedding_second`: positive. `qkv_second`: positive. `out_second`: positive. `up_second`: positive. `down_second`: positive. `bias_second`: positive. `gains_second`: positive.
All inputs are finite; a program needn't handle non-finite values.
Results may differ from the reference program's by a relative error of at most 0.012.
The reference program's roundings to bfloat16 on the way count: a program that leaves them out, or rounds other values in their place, can miss the bound.
Values may be sent and summed in bfloat16 or wider, within the bound.
A program may use at most 512 MiB of HBM per device.

```python
import math
import jax
import jax.numpy as jnp
from jax import lax

D = 768
HEADS = 12
HEAD = 64
FF = 3072
VOCAB = 32128
BUCKETS = 32
LENGTH = 512
STEP = 10
ITEM_GRP = 16
ITEMS = 64
N_GRP = 4


BETA_ONE = 0.9


BETA_TWO = 0.999


def grad_size(factor):
    items_live = max(ITEMS * 2 // 3, 2)
    return factor * 5.0 / math.sqrt(items_live * D)


def first_moment(key, array_shape, grad_rms):
    return grad_rms * (1.0 - BETA_ONE) / BETA_ONE * jax.random.normal(key, array_shape, jnp.float32)


def second_moment(key, array_shape, grad_rms):
    spread = jnp.exp(jax.random.uniform(key, array_shape, jnp.float32, math.log(0.5), math.log(4.0)))
    return grad_rms * grad_rms * (1.0 - BETA_TWO) / BETA_TWO * spread


def group_layout(key):
    live_key, order_key = jax.random.split(key)
    groups = jnp.arange(N_GRP)
    half_count = ITEM_GRP // 2
    lowest_pair = 1 + (half_count - 1) * groups // N_GRP
    pair_count = jax.random.randint(live_key, (N_GRP,), lowest_pair, half_count + 1)
    live_counts = jnp.where(groups == N_GRP - 1, ITEM_GRP, 2 * pair_count).astype(jnp.int32)

    def one_group(group_key, live_now):
        shuffled = jax.random.permutation(group_key, ITEM_GRP)
        slot_index = jnp.arange(ITEM_GRP)
        ranking = jnp.where(slot_index < live_now, shuffled, ITEM_GRP + slot_index)
        ordering = jnp.argsort(ranking, stable=True)
        mate_slots = jnp.where(slot_index < live_now, ordering[jnp.bitwise_xor(slot_index, 1)], ordering)
        return jnp.zeros((ITEM_GRP,), jnp.int32).at[ordering].set(mate_slots.astype(jnp.int32))
    group_keys = jax.random.split(order_key, N_GRP)
    partners = jax.vmap(one_group)(group_keys, live_counts).reshape(-1)
    return (live_counts, partners)


def draw_group_live(key, part):
    return group_layout(key)[0]


def draw_partner(key, part):
    return group_layout(key)[1]


def draw_item_lengths(key, part):
    key = jax.random.fold_in(key, 3)
    first_key, second_key = jax.random.split(key)
    drawn_lengths = jax.random.randint(first_key, (ITEMS,), LENGTH // 4, LENGTH + 1)
    full_slot = jax.random.randint(second_key, (), 0, ITEMS)
    indices = jnp.arange(ITEMS)
    drawn_lengths = jnp.where(indices == full_slot, LENGTH, drawn_lengths)
    return jnp.where(indices == (full_slot + 1) % ITEMS, LENGTH // 4, drawn_lengths).astype(jnp.int32)


def draw_embedding_first(key, part):
    return first_moment(jax.random.fold_in(key, 11), (D, VOCAB), grad_size(1.0) / math.sqrt(VOCAB))


def draw_embedding_second(key, part):
    return second_moment(jax.random.fold_in(key, 12), (D, VOCAB), grad_size(1.0) / math.sqrt(VOCAB))


def draw_qkv_first(key, part):
    return first_moment(jax.random.fold_in(key, 13), (D, 3, D), grad_size(0.3))


def draw_qkv_second(key, part):
    return second_moment(jax.random.fold_in(key, 14), (D, 3, D), grad_size(0.3))


def draw_out_first(key, part):
    return first_moment(jax.random.fold_in(key, 15), (D, D), grad_size(0.2))


def draw_out_second(key, part):
    return second_moment(jax.random.fold_in(key, 16), (D, D), grad_size(0.2))


def draw_up_first(key, part):
    return first_moment(jax.random.fold_in(key, 17), (D, FF), grad_size(0.2))


def draw_up_second(key, part):
    return second_moment(jax.random.fold_in(key, 18), (D, FF), grad_size(0.2))


def draw_down_first(key, part):
    return first_moment(jax.random.fold_in(key, 19), (D, FF), grad_size(0.5))


def draw_down_second(key, part):
    return second_moment(jax.random.fold_in(key, 20), (D, FF), grad_size(0.5))


def draw_bias_first(key, part):
    return first_moment(jax.random.fold_in(key, 21), (BUCKETS, HEADS), grad_size(1.0))


def draw_bias_second(key, part):
    return second_moment(jax.random.fold_in(key, 22), (BUCKETS, HEADS), grad_size(1.0))


def draw_gains_first(key, part):
    return first_moment(jax.random.fold_in(key, 23), (3, D), grad_size(2.0))


def draw_gains_second(key, part):
    return second_moment(jax.random.fold_in(key, 24), (3, D), grad_size(2.0))


def with_ends(result, rng, least, largest):
    longest = result.shape.index(max(result.shape))
    spots = []
    for shift in (0, 1):
        where = [jax.random.randint(jax.random.fold_in(rng, axis), (), 0, length) for axis, length in enumerate(result.shape)]
        where[longest] = (where[longest] + shift) % result.shape[longest]
        spots.append(tuple(where))
    return result.at[spots[0]].set(least).at[spots[1]].set(largest)


def level_of(stream_key, shape, shards, least, top_value):
    level = 1.0
    for axis_at, shards_of in shards:
        heights = jax.random.uniform(jax.random.fold_in(jax.random.fold_in(stream_key, 6), axis_at), (shards_of,), jnp.float32, least / len(shards), top_value / len(shards))
        level = level * jnp.repeat(jnp.exp(heights), shape[axis_at] // shards_of).reshape((-1,) + (1,) * (len(shape) - 1 - axis_at))
    return level


def bell_draw(key, dims, width, bound, cuts=(), kind=jnp.bfloat16):
    drawn = jax.random.normal(key, dims, jnp.float32) * width
    if len(cuts) > 0:
        drawn = level_of(key, dims, cuts, -0.22, 0.18) * drawn
    return jnp.clip(drawn, min=-bound, max=bound).astype(kind)


def setup_inputs(seed: int = 0) -> dict:
    keys = jax.random.split(jax.random.key(seed), 27)
    token_ids = with_ends(jax.random.randint(keys[0], (ITEMS, LENGTH), 0, VOCAB), jax.random.fold_in(keys[0], 1), 0, VOCAB - 1).astype(jnp.int32)
    item_lengths = draw_item_lengths(jax.random.fold_in(keys[26], 71), 0)
    prefix_lengths = with_ends(jax.random.randint(keys[2], (ITEMS,), 1, LENGTH // 8 + 1), jax.random.fold_in(keys[2], 1), 1, (LENGTH // 8 + 1) - 1).astype(jnp.int32)
    group_live = draw_group_live(jax.random.fold_in(keys[26], 71), 0)
    partner = draw_partner(jax.random.fold_in(keys[26], 71), 0)
    embedding = bell_draw(keys[5], (D, VOCAB), 1.0, 6.0, ((0, 4),), jnp.float32)
    qkv_weight = bell_draw(keys[6], (D, 3, D), D ** -0.5, 0.21875, ((0, 4), (2, 2)), jnp.float32)
    out_weight = bell_draw(keys[7], (D, D), (D // 32) ** -0.5, 1.25, ((0, 2), (1, 4)), jnp.float32)
    up_weight = bell_draw(keys[8], (D, FF), D ** -0.5, 0.21875, ((0, 4), (1, 2)), jnp.float32)
    down_weight = bell_draw(keys[9], (D, FF), FF ** -0.5, 0.109375, ((0, 4), (1, 2)), jnp.float32)
    bias_table = bell_draw(keys[10], (BUCKETS, HEADS), 1.0, 6.0, ((1, 2),), jnp.float32)
    norm_gains = jnp.clip(1.0 + 0.1 * jax.random.normal(keys[11], (3, D), jnp.float32), 0.5, 1.5)
    embedding_first = draw_embedding_first(jax.random.fold_in(keys[26], 71), 0)
    embedding_second = draw_embedding_second(jax.random.fold_in(keys[26], 71), 0)
    qkv_first = draw_qkv_first(jax.random.fold_in(keys[26], 71), 0)
    qkv_second = draw_qkv_second(jax.random.fold_in(keys[26], 71), 0)
    out_first = draw_out_first(jax.random.fold_in(keys[26], 71), 0)
    out_second = draw_out_second(jax.random.fold_in(keys[26], 71), 0)
    up_first = draw_up_first(jax.random.fold_in(keys[26], 71), 0)
    up_second = draw_up_second(jax.random.fold_in(keys[26], 71), 0)
    down_first = draw_down_first(jax.random.fold_in(keys[26], 71), 0)
    down_second = draw_down_second(jax.random.fold_in(keys[26], 71), 0)
    bias_first = draw_bias_first(jax.random.fold_in(keys[26], 71), 0)
    bias_second = draw_bias_second(jax.random.fold_in(keys[26], 71), 0)
    gains_first = draw_gains_first(jax.random.fold_in(keys[26], 71), 0)
    gains_second = draw_gains_second(jax.random.fold_in(keys[26], 71), 0)
    return dict(token_ids=token_ids, item_lengths=item_lengths, prefix_lengths=prefix_lengths, group_live=group_live, partner=partner, embedding=embedding, qkv_weight=qkv_weight, out_weight=out_weight, up_weight=up_weight, down_weight=down_weight, bias_table=bias_table, norm_gains=norm_gains, embedding_first=embedding_first, embedding_second=embedding_second, qkv_first=qkv_first, qkv_second=qkv_second, out_first=out_first, out_second=out_second, up_first=up_first, up_second=up_second, down_first=down_first, down_second=down_second, bias_first=bias_first, bias_second=bias_second, gains_first=gains_first, gains_second=gains_second)


SOFTMAX_WARMTH = 0.01
NORM_EPS = 1e-06
BUCKET_EDGES = (12, 16, 23, 32, 46, 64, 91)
BETA_ONE = 0.9
BETA_TWO = 0.999
ADAM_EPS = 1e-06
WEIGHT_DECAY = 0.01
LEARN_RATE = 0.5
MASK_FILL = -1000000000.0
MAX_PRECISION = lax.Precision.HIGHEST

@jax.custom_vjp
def low(v):
    return lax.optimization_barrier(v.astype(jnp.bfloat16)).astype(jnp.float32)

@jax.custom_vjp
def low_back(v):
    return v

def low_keep(v):
    return (low(v), None)

def low_pass(kept, grad):
    return (grad,)

def back_keep(v):
    return (v, None)

def back_low(kept, grad):
    return (low(grad),)
low.defvjp(low_keep, low_pass)
low_back.defvjp(back_keep, back_low)

def bucket_table(extent):
    positions = jnp.arange(extent, dtype=jnp.int32)
    relative = positions[None, :] - positions[:, None]
    distance = jnp.abs(relative)
    far_bucket = 8 + sum(((distance >= threshold).astype(jnp.int32) for threshold in BUCKET_EDGES))
    return jnp.where(distance < 8, distance, far_bucket) + jnp.where(relative > 0, 16, 0)

def norm_scale(stream, gain_row):
    return stream * lax.rsqrt(lax.optimization_barrier(jnp.mean(stream * stream, axis=-1, keepdims=True)) + NORM_EPS) * gain_row

def gelu_tanh(pre_act):
    return jax.nn.gelu(pre_act, approximate=True)

def encode_item(inner_params, token_row, item_length, prefix_length):
    low_table, qkv_weight, out_weight, up_weight, down_weight, bias_heads, norm_gains = inner_params
    embedded = low_table[:, token_row].T
    normed_one = low(norm_scale(embedded, norm_gains[0]))
    qkv_rows = low(low_back(jnp.dot(normed_one, qkv_weight.reshape(D, 3 * D), precision=MAX_PRECISION)))
    qkv_rows = qkv_rows.reshape(LENGTH, 3, HEADS, HEAD)
    raw_scores = jnp.einsum('qhd,khd->hqk', qkv_rows[:, 0], qkv_rows[:, 1], precision=MAX_PRECISION) * HEAD ** (-0.5)
    key_valid = jnp.arange(LENGTH) < item_length
    scores = jnp.where(key_valid[None, None, :], low_back(raw_scores) + bias_heads, MASK_FILL)
    soft_probs = jax.nn.softmax(scores, axis=-1)
    mixed_heads = jnp.einsum('hqk,khd->qhd', low(soft_probs), qkv_rows[:, 2], precision=MAX_PRECISION)
    mixed_heads = low(low_back(mixed_heads.reshape(LENGTH, D)))
    after_attn = embedded + low_back(jnp.dot(mixed_heads, out_weight, precision=MAX_PRECISION))
    normed_two = low(norm_scale(after_attn, norm_gains[1]))
    gate_pre = low_back(jnp.dot(normed_two, up_weight, precision=MAX_PRECISION))
    activated = low(gelu_tanh(gate_pre))
    after_ffn = after_attn + low_back(jnp.dot(activated, down_weight.T, precision=MAX_PRECISION))
    normed_three = norm_scale(after_ffn, norm_gains[2])
    positions = jnp.arange(LENGTH)
    pool_mask = ((positions >= prefix_length) & (positions < item_length)).astype(jnp.float32)
    pooled = lax.optimization_barrier(jnp.sum(normed_three * pool_mask[:, None], axis=0)) / jnp.sum(pool_mask)
    return pooled * lax.rsqrt(jnp.sum(pooled * pooled) + NORM_EPS)

def group_loss(sentence_embeddings, mate_slots, live_slots):
    similarity_logits = jnp.dot(sentence_embeddings, sentence_embeddings.T, precision=MAX_PRECISION) / SOFTMAX_WARMTH
    slot_index = jnp.arange(ITEM_GRP)
    allowed = live_slots[None, :] & (slot_index[None, :] != slot_index[:, None])
    masked = jnp.where(allowed, similarity_logits, MASK_FILL)
    row_top = lax.optimization_barrier(jnp.max(masked, axis=1, keepdims=True))
    log_total = row_top[:, 0] + jnp.log(lax.optimization_barrier(jnp.sum(jnp.exp(masked - row_top), axis=1)))
    target = lax.optimization_barrier(jnp.sum(jnp.where(slot_index[None, :] == mate_slots[:, None], similarity_logits, 0.0), axis=1))
    return jnp.sum(jnp.where(live_slots, log_total - target, 0.0))

def lamb_direction(weight, gradient, moment_one, moment_two):
    momentum = BETA_ONE * moment_one + (1.0 - BETA_ONE) * gradient
    variance = BETA_TWO * moment_two + (1.0 - BETA_TWO) * gradient * gradient
    direction = momentum / (1.0 - BETA_ONE ** STEP) / (jnp.sqrt(variance / (1.0 - BETA_TWO ** STEP)) + ADAM_EPS) + WEIGHT_DECAY * weight
    return (momentum, variance, direction)

def reference(token_ids, item_lengths, prefix_lengths, group_live, partner, embedding, qkv_weight, out_weight, up_weight, down_weight, bias_table, norm_gains, embedding_first, embedding_second, qkv_first, qkv_second, out_first, out_second, up_first, up_second, down_first, down_second, bias_first, bias_second, gains_first, gains_second):
    slot_index = jnp.arange(ITEMS) % ITEM_GRP
    group_of = jnp.arange(ITEMS) // ITEM_GRP
    live_rows = slot_index < group_live[group_of]
    live_total = jnp.sum(group_live).astype(jnp.float32)
    onehot = (bucket_table(LENGTH)[:, :, None] == jnp.arange(BUCKETS)).astype(jnp.float32)
    weights = (embedding, qkv_weight, out_weight, up_weight, down_weight, bias_table, norm_gains)

    def objective(params):
        bias_heads = jnp.einsum('qkb,bh->hqk', onehot, params[5], precision=MAX_PRECISION)
        inner_params = (low(params[0]),) + tuple((low(matrix) for matrix in params[1:5])) + (bias_heads, params[6])

        def encode_one(packed):
            return encode_item(inner_params, packed[0], packed[1], packed[2])
        sentence_embeddings = lax.map(jax.checkpoint(encode_one), (token_ids, item_lengths, prefix_lengths))
        loss_sum = jnp.sum(jax.vmap(group_loss)(sentence_embeddings.reshape(N_GRP, ITEM_GRP, D), partner.reshape(N_GRP, ITEM_GRP), live_rows.reshape(N_GRP, ITEM_GRP)))
        return (loss_sum / live_total, loss_sum)
    loss_mean, pull_back, loss_sum = jax.vjp(objective, weights, has_aux=True)
    gradients = pull_back(jnp.ones_like(loss_mean))[0]
    moments = ((embedding_first, embedding_second), (qkv_first, qkv_second), (out_first, out_second), (up_first, up_second), (down_first, down_second), (bias_first, bias_second), (gains_first, gains_second))
    results = [lamb_direction(weight, gradient, states[0], states[1]) for weight, gradient, states in zip(weights, gradients, moments)]
    matrices = list(weights[:6]) + [norm_gains[position] for position in range(3)]
    directions = [entries[2] for entries in results[:6]] + [results[6][2][position] for position in range(3)]
    matrix_norms = jnp.stack([jnp.stack([jnp.sqrt(jnp.sum(matrix * matrix)), jnp.sqrt(jnp.sum(direction * direction))]) for matrix, direction in zip(matrices, directions)])
    trust_ratio = matrix_norms[:, 0] / matrix_norms[:, 1]
    updated = [weights[position] - LEARN_RATE * trust_ratio[position] * results[position][2] for position in range(6)]
    updated.append(norm_gains - LEARN_RATE * trust_ratio[6:, None] * results[6][2])
    outputs = [jnp.stack([loss_sum, live_total]), matrix_norms]
    for position in range(7):
        outputs.extend([results[position][0], results[position][1], updated[position]])
    return tuple(outputs)
```

```python
import functools

import jax
import jax.numpy as jnp
from jax import lax
from jax.experimental import pallas as pl
from jax.experimental.pallas import tpu as pltpu
from jax.sharding import PartitionSpec as P

HEADS = 12
HEAD = 64
BUCKETS = 32
STEP = 10


SOFTMAX_WARMTH = 0.01
NORM_EPS = 1e-06
BUCKET_EDGES = (12, 16, 23, 32, 46, 64, 91)
BETA_ONE = 0.9
BETA_TWO = 0.999
ADAM_EPS = 1e-06
WEIGHT_DECAY = 0.01
LEARN_RATE = 0.5
MASK_FILL = -1000000000.0
MAX_PRECISION = lax.Precision.HIGHEST
LANES = 128
bf = jnp.bfloat16
f32 = jnp.float32


BLOCK=128
NT=(((1,),(1,)),((),()))
TN=(((0,),(0,)),((),()))

def toeplitz(line, rows):
    out = line
    size = 1
    while size < rows:
        out = jnp.concatenate([out, pltpu.roll(out, size, 1)], axis=0)
        size *= 2
    return out

def diagonal_sums(square):
    rows, width = square.shape
    while rows > 8:
        rows //= 2
        square = square[:rows] + pltpu.roll(square[rows:], width - rows, 1)
    for shift in (4, 2, 1):
        square = square + pltpu.roll(pltpu.roll(square, width - shift, 1), 8 - shift, 0)
    return square[:1]

def attend_kernel(pairs, scale, lens_ref, line_ref, qkv_ref, mixed_ref, lse_ref):
    items, length, _ = mixed_ref.shape
    blocks = length // BLOCK
    first = lax.broadcasted_iota(jnp.int32, (1, LANES), 1) < HEAD
    lane = lax.broadcasted_iota(jnp.int32, (BLOCK, LANES), 1)
    column = lax.broadcasted_iota(jnp.int32, (1, length), 1)

    def one_pair(pair, carry):
        at = lambda part: pl.ds(pl.multiple_of((part * pairs + pair) * LANES, LANES), LANES)
        biases = [toeplitz(line_ref[pl.ds(2 * pair + head, 1), :], BLOCK) for head in range(2)]
        for item in range(items):
            keys = qkv_ref[item, :, at(1)]
            values = qkv_ref[item, :, at(2)]
            valid = column < lens_ref[item]
            for block in range(blocks):
                rows = pl.ds(block * BLOCK, BLOCK)
                queries = qkv_ref[item, rows, at(0)] * scale
                low = length - block * BLOCK
                mixed = []
                stats = jnp.zeros((BLOCK, LANES), f32)
                for head in range(2):
                    mine = first if head == 0 else jnp.logical_not(first)
                    scores = lax.dot_general(jnp.where(mine, queries, 0), keys, NT, preferred_element_type=f32)
                    scores = jnp.where(valid, scores + biases[head][:, low : low + length], MASK_FILL)
                    top = jnp.max(scores, axis=1, keepdims=True)
                    powers = jnp.exp(scores - top)
                    whole = jnp.sum(powers, axis=1, keepdims=True)
                    probs = (powers * (1.0 / whole)).astype(bf)
                    mixed.append(jnp.dot(probs, values, preferred_element_type=f32))
                    stats = jnp.where(lane == head, top + jnp.log(whole), stats)
                mixed_ref[item, rows, at(0)] = jnp.where(first, mixed[0], mixed[1]).astype(bf)
                lse_ref[item, rows, at(0)] = stats
        return carry

    lax.fori_loop(0, pairs, one_pair, 0)

def attend(qkv, lines, lengths):
    items, length, width = qkv.shape
    width //= 3
    pairs = width // LANES
    vm = pl.BlockSpec(memory_space=pltpu.VMEM)
    return pl.pallas_call(
        functools.partial(attend_kernel, pairs, HEAD ** -0.5),
        in_specs=[pl.BlockSpec(memory_space=pltpu.SMEM), vm, vm],
        out_specs=[vm, vm],
        out_shape=[jax.ShapeDtypeStruct((items, length, width), bf), jax.ShapeDtypeStruct((items, length, width), f32)],
        compiler_params=pltpu.CompilerParams(vmem_limit_bytes=40 * 2**20),
        cost_estimate=pl.CostEstimate(flops=8 * items * length * length * width, bytes_accessed=items * length * width * 12, transcendentals=items * length * length * width // HEAD),
        name="attend",
    )(lengths, lines, qkv)

def attend_back_kernel(pairs, scale, lens_ref, line_ref, qkv_ref, lse_ref, dmix_ref, dqkv_ref, dline_ref, dkey, dval, diag):
    items, length, _ = dmix_ref.shape
    blocks = length // BLOCK
    first = lax.broadcasted_iota(jnp.int32, (1, LANES), 1) < HEAD
    column = lax.broadcasted_iota(jnp.int32, (1, length), 1)

    def one_pair(pair, carry):
        at = lambda part: pl.ds(pl.multiple_of((part * pairs + pair) * LANES, LANES), LANES)
        biases = [toeplitz(line_ref[pl.ds(2 * pair + head, 1), :], BLOCK) for head in range(2)]
        diag[...] = jnp.zeros_like(diag)
        for item in range(items):
            keys = qkv_ref[item, :, at(1)]
            values = qkv_ref[item, :, at(2)]
            valid = column < lens_ref[item]
            for block in range(blocks):
                rows = pl.ds(block * BLOCK, BLOCK)
                queries = qkv_ref[item, rows, at(0)] * scale
                given = dmix_ref[item, rows, at(0)]
                stats = lse_ref[item, rows, at(0)]
                low = length - block * BLOCK
                dquery, dkeys, dvals = [], [], []
                for head in range(2):
                    mine = first if head == 0 else jnp.logical_not(first)
                    scores = lax.dot_general(jnp.where(mine, queries, 0), keys, NT, preferred_element_type=f32)
                    scores = jnp.where(valid, scores + biases[head][:, low : low + length], MASK_FILL)
                    probs = jnp.exp(scores - stats[:, head : head + 1])
                    dprobs = lax.dot_general(jnp.where(mine, given, 0), values, NT, preferred_element_type=f32)
                    inner = jnp.sum(probs * dprobs, axis=1, keepdims=True)
                    dscores = probs * (dprobs - inner)
                    diag[head, :, low : low + length] += dscores
                    low_scores = dscores.astype(bf)
                    dquery.append(jnp.dot(low_scores, keys, preferred_element_type=f32))
                    dkeys.append(lax.dot_general(low_scores, queries, TN, preferred_element_type=f32))
                    dvals.append(lax.dot_general(probs.astype(bf), given, TN, preferred_element_type=f32))
                dqkv_ref[item, rows, at(0)] = (jnp.where(first, dquery[0], dquery[1]) * scale).astype(bf)
                dk = jnp.where(first, dkeys[0], dkeys[1])
                dv = jnp.where(first, dvals[0], dvals[1])
                if block == 0:
                    dkey[...] = dk
                    dval[...] = dv
                else:
                    dkey[...] += dk
                    dval[...] += dv
            dqkv_ref[item, :, at(1)] = dkey[...].astype(bf)
            dqkv_ref[item, :, at(2)] = dval[...].astype(bf)
        for head in range(2):
            dline_ref[pl.ds(2 * pair + head, 1), :] = diagonal_sums(diag[head])
        return carry

    lax.fori_loop(0, pairs, one_pair, 0)

def attend_back(qkv, lines, lengths, lse, dmixed):
    items, length, width = dmixed.shape
    pairs = width // LANES
    vm = pl.BlockSpec(memory_space=pltpu.VMEM)
    return pl.pallas_call(
        functools.partial(attend_back_kernel, pairs, HEAD ** -0.5),
        in_specs=[pl.BlockSpec(memory_space=pltpu.SMEM), vm, vm, vm, vm],
        out_specs=[vm, vm],
        out_shape=[jax.ShapeDtypeStruct(qkv.shape, bf), jax.ShapeDtypeStruct(lines.shape, f32)],
        scratch_shapes=[pltpu.VMEM((length, LANES), f32), pltpu.VMEM((length, LANES), f32), pltpu.VMEM((2, BLOCK, 2 * length), f32)],
        compiler_params=pltpu.CompilerParams(vmem_limit_bytes=40 * 2**20),
        cost_estimate=pl.CostEstimate(flops=20 * items * length * length * width, bytes_accessed=items * length * width * 20, transcendentals=items * length * length * width // HEAD),
        name="attend_back",
    )(lengths, lines, qkv, lse, dmixed)


def gather_kernel(features, tiles, load_steps, batch, table_ref, ids_ref, out_ref, stash, rows):
    step = pl.program_id(0)
    width = table_ref.shape[1]

    @pl.when(step < load_steps)
    def _():
        base = pl.multiple_of(step * width, width)
        for tile in range(tiles):
            low = tile * LANES
            high = min(features, low + LANES)
            part = table_ref[low:high, :].astype(bf).astype(jnp.float32)
            if high - low < LANES:
                part = jnp.concatenate([part, jnp.zeros((LANES - (high - low), width), jnp.float32)], axis=0)
            stash[tile, pl.ds(base, width), :] = part.T

    @pl.when(step >= load_steps)
    def _():
        count = out_ref.shape[0]
        for half in range(2):
            def take(index, carry):
                start = pl.multiple_of(index * batch, batch)
                for inner in range(batch):
                    token = ids_ref[0, half, start + inner]
                    for tile in range(tiles):
                        rows[half, tile, pl.ds(start + inner, 1), :] = stash[tile, pl.ds(token, 1), :]
                return carry
            lax.fori_loop(0, count // batch, take, 0)
        pieces = []
        for half in range(2):
            for tile in range(tiles):
                low = tile * LANES
                pieces.append(rows[half, tile, :, : min(LANES, features - low)])
        out_ref[...] = jnp.concatenate(pieces, axis=1).astype(bf)

def gather_rows(table, ids, width=2048, chunk=256, batch=32):
    features, vocab = table.shape
    tiles = pl.cdiv(features, LANES)
    load_steps = pl.cdiv(vocab, width)
    steps = ids.shape[0]
    return pl.pallas_call(
        functools.partial(gather_kernel, features, tiles, load_steps, batch),
        grid=(load_steps + steps,),
        in_specs=[
            pl.BlockSpec((features, width), lambda s: (0, jnp.minimum(s, load_steps - 1))),
            pl.BlockSpec((1, 2, chunk), lambda s: (jnp.maximum(s - load_steps, 0), 0, 0), memory_space=pltpu.SMEM),
        ],
        out_specs=pl.BlockSpec((chunk, 2 * features), lambda s: (jnp.maximum(s - load_steps, 0), 0)),
        out_shape=jax.ShapeDtypeStruct((steps * chunk, 2 * features), bf),
        scratch_shapes=[
            pltpu.VMEM((tiles, load_steps * width, LANES), jnp.float32),
            pltpu.VMEM((2, tiles, chunk, LANES), jnp.float32),
        ],
        compiler_params=pltpu.CompilerParams(vmem_limit_bytes=60 * 2**20),
        name="gather_rows",
    )(table, ids)

def scatter_kernel(features, tiles, scatter_steps, batch, ids_ref, ids_row_ref, rows_ref, out_ref, total, summed):
    step = pl.program_id(0)
    width = out_ref.shape[1]
    count = rows_ref.shape[0]

    @pl.when(step == 0)
    def _():
        total[...] = jnp.zeros_like(total)

    @pl.when(step < scatter_steps)
    def _():
        place = lax.broadcasted_iota(jnp.int32, (count, count), 0) // batch
        same_batch = place == lax.broadcasted_iota(jnp.int32, (count, count), 1) // batch
        for half in range(2):
            across = jnp.broadcast_to(ids_row_ref[0, half : half + 1, :], (count, count))
            match = jnp.where((across == across.T) & same_batch, 1.0, 0.0).astype(bf)
            merged = jnp.dot(match, rows_ref[:, half * features : (half + 1) * features], preferred_element_type=jnp.float32)
            for tile in range(tiles):
                low = tile * LANES
                high = min(features, low + LANES)
                part = merged[:, low:high]
                if high - low < LANES:
                    part = jnp.concatenate([part, jnp.zeros((count, LANES - (high - low)), jnp.float32)], axis=1)
                summed[half, tile] = part
        for half in range(2):
            def add(index, carry):
                start = pl.multiple_of(index * batch, batch)
                tokens = [ids_ref[0, half, start + inner] for inner in range(batch)]
                for tile in range(tiles):
                    fresh = [
                        total[tile, pl.ds(tokens[inner], 1), :] + summed[half, tile, pl.ds(start + inner, 1), :]
                        for inner in range(batch)
                    ]
                    for inner in range(batch):
                        total[tile, pl.ds(tokens[inner], 1), :] = fresh[inner]
                return carry
            lax.fori_loop(0, count // batch, add, 0)

    @pl.when(step >= scatter_steps)
    def _():
        base = pl.multiple_of((step - scatter_steps) * width, width)
        for tile in range(tiles):
            low = tile * LANES
            high = min(features, low + LANES)
            out_ref[low:high, :] = total[tile, pl.ds(base, width), :].T[: high - low].astype(bf)

def scatter_rows(rows, ids, vocab, features, width=2048, chunk=256, batch=32):
    tiles = pl.cdiv(features, LANES)
    steps = ids.shape[0]
    flush = pl.cdiv(vocab, width)
    at = lambda s: jnp.minimum(s, steps - 1)
    return pl.pallas_call(
        functools.partial(scatter_kernel, features, tiles, steps, batch),
        grid=(steps + flush,),
        in_specs=[
            pl.BlockSpec((1, 2, chunk), lambda s: (at(s), 0, 0), memory_space=pltpu.SMEM),
            pl.BlockSpec((1, 2, chunk), lambda s: (at(s), 0, 0)),
            pl.BlockSpec((chunk, 2 * features), lambda s: (at(s), 0)),
        ],
        out_specs=pl.BlockSpec((features, width), lambda s: (0, jnp.maximum(s - steps, 0))),
        out_shape=jax.ShapeDtypeStruct((features, vocab), bf),
        scratch_shapes=[
            pltpu.VMEM((tiles, flush * width, LANES), jnp.float32),
            pltpu.VMEM((2, tiles, chunk, LANES), jnp.float32),
        ],
        compiler_params=pltpu.CompilerParams(vmem_limit_bytes=60 * 2**20),
        name="scatter_rows",
    )(ids, ids, rows)


def lamb_direction(weight, gradient, moment_one, moment_two):
    momentum = BETA_ONE * moment_one + (1.0 - BETA_ONE) * gradient
    variance = BETA_TWO * moment_two + (1.0 - BETA_TWO) * gradient * gradient
    direction = (
        momentum / (1.0 - BETA_ONE**STEP) / (jnp.sqrt(variance / (1.0 - BETA_TWO**STEP)) + ADAM_EPS)
        + WEIGHT_DECAY * weight
    )
    return (momentum, variance, direction)


def table_moments_kernel(weight_ref, first_ref, second_ref, mine_ref, other_ref, momentum_ref, variance_ref, direction_ref, squares_ref):
    weight = weight_ref[...]
    gradient = mine_ref[...].astype(f32) + other_ref[...].astype(f32)
    momentum, variance, direction = lamb_direction(weight, gradient, first_ref[...], second_ref[...])
    momentum_ref[...] = momentum
    variance_ref[...] = variance
    direction_ref[...] = direction.astype(bf)

    @pl.when(pl.program_id(0) == 0)
    def _():
        squares_ref[...] = jnp.zeros_like(squares_ref)

    squares_ref[0:1, :] += jnp.full((1, LANES), jnp.sum(weight * weight))
    squares_ref[1:2, :] += jnp.full((1, LANES), jnp.sum(direction * direction))


def table_moments(weight, first, second, mine, other, rows=16):
    features, vocab = weight.shape
    block = pl.BlockSpec((rows, vocab), lambda s: (s, 0))
    full = jax.ShapeDtypeStruct(weight.shape, f32)
    return pl.pallas_call(
        table_moments_kernel,
        grid=(features // rows,),
        in_specs=[block] * 5,
        out_specs=[block, block, block, pl.BlockSpec((8, LANES), lambda s: (0, 0))],
        out_shape=[full, full, jax.ShapeDtypeStruct(weight.shape, bf), jax.ShapeDtypeStruct((8, LANES), f32)],
        compiler_params=pltpu.CompilerParams(vmem_limit_bytes=48 * 2**20),
        name="table_moments",
    )(weight, first, second, mine, other)


def table_update_kernel(rate_ref, weight_ref, direction_ref, updated_ref):
    updated_ref[...] = weight_ref[...] - rate_ref[0] * direction_ref[...].astype(f32)


def table_update(rate, weight, direction, rows=16):
    features, vocab = weight.shape
    block = pl.BlockSpec((rows, vocab), lambda s: (s, 0))
    return pl.pallas_call(
        table_update_kernel,
        grid=(features // rows,),
        in_specs=[pl.BlockSpec(memory_space=pltpu.SMEM), block, block],
        out_specs=block,
        out_shape=jax.ShapeDtypeStruct(weight.shape, f32),
        compiler_params=pltpu.CompilerParams(vmem_limit_bytes=40 * 2**20),
        name="table_update",
    )(rate, weight, direction)


def norm_scale(stream, gain_row):
    return (
        stream * lax.rsqrt(jnp.mean(stream * stream, axis=-1, keepdims=True) + NORM_EPS) * gain_row
    )


def gelu_tanh(pre_act):
    return jax.nn.gelu(pre_act, approximate=True)


def dot(left, right, dims=((1,), (0,))):
    return lax.dot_general(left, right, (dims, ((), ())), preferred_element_type=f32)


def bucket_onehot(length):
    relative = jnp.arange(2 * length, dtype=jnp.int32) - length
    distance = jnp.abs(relative)
    far_bucket = 8 + sum(((distance >= threshold).astype(jnp.int32) for threshold in BUCKET_EDGES))
    bucket = jnp.where(distance < 8, distance, far_bucket) + jnp.where(relative > 0, 16, 0)
    return (bucket[:, None] == jnp.arange(BUCKETS)).astype(f32)


def swap_cores(value):
    size = lax.axis_size("mdl")
    return lax.ppermute(value, "mdl", [(core, (core + 1) % size) for core in range(size)])


def shards(
    token_ids,
    item_lengths,
    prefix_lengths,
    group_live,
    partner,
    embedding,
    qkv_weight,
    out_weight,
    up_weight,
    down_weight,
    bias_table,
    norm_gains,
    embedding_first,
    embedding_second,
    qkv_first,
    qkv_second,
    out_first,
    out_second,
    up_first,
    up_second,
    down_first,
    down_second,
    bias_first,
    bias_second,
    gains_first,
    gains_second,
):
    item_count, length = token_ids.shape
    features, vocab = embedding.shape
    grp_size, dat_size, mdl_size = lax.axis_size("grp"), lax.axis_size("dat"), lax.axis_size("mdl")
    group_index, dat_index, mdl_index = lax.axis_index("grp"), lax.axis_index("dat"), lax.axis_index("mdl")
    mine = item_count // mdl_size
    rows = mine * length
    pair_rows = rows // 2
    chunk = 256
    chunks = pair_rows // chunk
    group_items = item_count * dat_size
    width = features * dat_size
    first_slot = dat_index * item_count + mdl_index * mine

    facts = jnp.concatenate([token_ids, partner[:, None]], axis=1)
    group_facts = lax.all_gather(facts, "dat", axis=0, tiled=True)
    group_partner = group_facts[:, length]
    core_ids = lax.dynamic_index_in_dim(
        group_facts[:, :length].reshape(dat_size, mdl_size, 2, chunks, chunk), mdl_index, 1, keepdims=False
    ).transpose(0, 2, 1, 3)
    my_lengths = lax.dynamic_slice_in_dim(item_lengths, mdl_index * mine, mine)
    my_prefixes = lax.dynamic_slice_in_dim(prefix_lengths, mdl_index * mine, mine)

    def gathered(shard, axis=0):
        own = lax.all_gather(shard.astype(bf), "dat", axis=axis, tiled=True)
        return own, swap_cores(own)

    qkv_halves = gathered(qkv_weight.reshape(features, -1))
    out_halves = gathered(out_weight, 1)
    up_halves = gathered(up_weight)
    down_halves = gathered(down_weight)
    onehot = bucket_onehot(length)
    line_halves = [
        jnp.einsum("rb,bh->hr", onehot, table, precision=MAX_PRECISION)
        for table in (bias_table, swap_cores(bias_table))
    ]

    looked_up = gather_rows(embedding, core_ids.reshape(-1, 2, chunk))
    spread = lax.all_to_all(
        looked_up.reshape(dat_size, pair_rows, 2 * features), "dat", split_axis=0, concat_axis=0, tiled=True
    )
    embedded = (
        spread.reshape(dat_size, pair_rows, 2, features).transpose(2, 1, 0, 3).reshape(rows, width).astype(f32)
    )
    all_ids = lax.all_gather(core_ids, "grp", axis=0)

    normed_one_f, norm_one_back = jax.vjp(norm_scale, embedded, norm_gains[0])
    normed_one = normed_one_f.astype(bf)
    qkv_rows = [dot(normed_one, weight).astype(bf).reshape(mine, length, -1) for weight in qkv_halves]
    mixed, log_totals = zip(*[attend(item_qkv, lines, my_lengths) for item_qkv, lines in zip(qkv_rows, line_halves)])
    mixed_rows = [heads.reshape(rows, -1) for heads in mixed]
    after_attn = embedded + (dot(mixed_rows[0], out_halves[0]) + dot(mixed_rows[1], out_halves[1]))
    normed_two_f, norm_two_back = jax.vjp(norm_scale, after_attn, norm_gains[1])
    normed_two = normed_two_f.astype(bf)
    gate_acts, gelu_backs = zip(*[jax.vjp(gelu_tanh, dot(normed_two, weight)) for weight in up_halves])
    activated = [act.astype(bf) for act in gate_acts]
    after_ffn = after_attn + (
        dot(activated[0], down_halves[0], ((1,), (1,))) + dot(activated[1], down_halves[1], ((1,), (1,)))
    )
    positions = jnp.arange(length)
    pool_mask = (
        (positions[None, :] >= my_prefixes[:, None]) & (positions[None, :] < my_lengths[:, None])
    ).astype(f32)

    def pool_tail(stream, gain_row):
        normed_three = norm_scale(stream, gain_row).reshape(mine, length, -1)
        pooled = jnp.sum(normed_three * pool_mask[:, :, None], axis=1) / jnp.sum(pool_mask, axis=1, keepdims=True)
        return pooled * lax.rsqrt(jnp.sum(pooled * pooled, axis=1, keepdims=True) + NORM_EPS)

    vectors, tail_back = jax.vjp(pool_tail, after_ffn, norm_gains[2])

    group_vectors = lax.all_gather(vectors, ("dat", "mdl"), axis=0, tiled=True)
    live_count = jnp.sum(jnp.where(jnp.arange(grp_size) == group_index, group_live, 0))
    live_total = jnp.sum(group_live).astype(f32)
    slots = jnp.arange(group_items)
    live_rows = slots < live_count
    logits = jnp.dot(group_vectors, group_vectors.T, precision=MAX_PRECISION) / SOFTMAX_WARMTH
    allowed = live_rows[None, :] & (slots[None, :] != slots[:, None])
    masked = jnp.where(allowed, logits, MASK_FILL)
    row_top = jnp.max(masked, axis=1, keepdims=True)
    log_total = row_top[:, 0] + jnp.log(jnp.sum(jnp.exp(masked - row_top), axis=1))
    mate_hits = slots[None, :] == group_partner[:, None]
    target = jnp.sum(jnp.where(mate_hits, logits, 0.0), axis=1)
    loss_part = jnp.sum(jnp.where(live_rows, log_total - target, 0.0))
    row_weight = jnp.where(live_rows, 1.0 / live_total, 0.0)
    grad_logits = (
        row_weight[:, None] * (jnp.exp(masked - log_total[:, None]) - mate_hits.astype(f32)) / SOFTMAX_WARMTH
    )
    my_pulls = lax.dynamic_slice_in_dim(grad_logits + grad_logits.T, first_slot, mine)
    grad_vectors = jnp.dot(my_pulls, group_vectors, precision=MAX_PRECISION)

    def reduced(own, other):
        total = (own + swap_cores(other.astype(bf)).astype(f32)).astype(bf)
        part = lax.psum_scatter(total, "dat", scatter_dimension=0, tiled=True)
        return lax.psum(part, "grp").astype(f32)

    tn = ((0,), (0,))
    nt = ((1,), (1,))
    grad_after_ffn, grad_gain_three = tail_back(grad_vectors)
    grad_ffn = grad_after_ffn.astype(bf)
    grad_down = reduced(*[dot(grad_ffn, act, tn) for act in activated])
    grad_gates = [
        back(dot(grad_ffn, weight))[0].astype(bf) for back, weight in zip(gelu_backs, down_halves)
    ]
    grad_up = reduced(*[dot(normed_two, grad_gate, tn) for grad_gate in grad_gates])
    two_back = dot(grad_gates[0], up_halves[0], nt) + dot(grad_gates[1], up_halves[1], nt)
    grad_after_attn, grad_gain_two = norm_two_back(two_back)
    grad_after_attn = grad_after_attn + grad_after_ffn
    grad_attn = grad_after_attn.astype(bf)
    grad_out = reduced(*[dot(grad_attn, heads, tn) for heads in mixed_rows]).T
    grad_mixed = [dot(grad_attn, weight, nt).astype(bf).reshape(mine, length, -1) for weight in out_halves]
    grad_qkv_items, grad_lines = zip(
        *[
            attend_back(item_qkv, lines, my_lengths, stats, grad)
            for item_qkv, lines, stats, grad in zip(qkv_rows, line_halves, log_totals, grad_mixed)
        ]
    )
    grad_qkv_rows = [grad.reshape(rows, -1) for grad in grad_qkv_items]
    one_back = dot(grad_qkv_rows[0], qkv_halves[0], nt) + dot(grad_qkv_rows[1], qkv_halves[1], nt)
    grad_embedded, grad_gain_one = norm_one_back(one_back)
    grad_embedded = grad_embedded + grad_after_attn
    grad_qkv = reduced(*[dot(normed_one, grad, tn) for grad in grad_qkv_rows]).reshape(qkv_weight.shape)

    outgoing = grad_embedded.astype(bf).reshape(2, pair_rows, dat_size, features).transpose(2, 1, 0, 3)
    own_rows = lax.all_to_all(
        outgoing.reshape(dat_size, pair_rows, 2 * features), "dat", split_axis=0, concat_axis=0, tiled=True
    ).reshape(dat_size * pair_rows, 2 * features)
    upward = [(group, group + 1) for group in range(grp_size - 1)]
    downward = [(group + 1, group) for group in range(grp_size - 1)]
    from_below, from_above = [own_rows], [own_rows]
    for _ in range(grp_size - 1):
        from_below.append(lax.ppermute(from_below[-1], "grp", upward))
        from_above.append(lax.ppermute(from_above[-1], "grp", downward))
    pieces, piece_ids = [own_rows], [core_ids]
    for hop in range(1, grp_size):
        pieces.append(jnp.where(group_index >= hop, from_below[hop], from_above[grp_size - hop]))
        piece_ids.append(lax.dynamic_index_in_dim(all_ids, (group_index - hop) % grp_size, 0, keepdims=False))
    own_table = scatter_rows(
        jnp.concatenate(pieces, axis=0), jnp.stack(piece_ids).reshape(-1, 2, chunk), vocab, features
    )
    other_table = swap_cores(own_table)

    grad_bias_own, grad_bias_other = [
        jnp.einsum("rb,hr->bh", onehot, grad, precision=MAX_PRECISION) for grad in grad_lines
    ]
    grad_bias_all = jnp.where(
        mdl_index == 0,
        jnp.concatenate([grad_bias_own, grad_bias_other], axis=1),
        jnp.concatenate([grad_bias_other, grad_bias_own], axis=1),
    )
    leader = ((dat_index == 0) & (mdl_index == 0)).astype(f32)
    small = jnp.concatenate(
        [
            jnp.stack([grad_gain_one, grad_gain_two, grad_gain_three]).reshape(-1),
            grad_bias_all.reshape(-1),
            (loss_part * leader).reshape(1),
        ]
    )
    small = lax.psum(small, ("grp", "dat", "mdl"))
    grad_gains = small[: 3 * width].reshape(3, width)
    grad_bias = lax.dynamic_slice_in_dim(
        small[3 * width : -1].reshape(BUCKETS, -1), mdl_index * bias_table.shape[1], bias_table.shape[1], axis=1
    )
    loss_total = small[-1]

    weights = (qkv_weight, out_weight, up_weight, down_weight, bias_table, norm_gains)
    gradients = (grad_qkv, grad_out, grad_up, grad_down, grad_bias, grad_gains)
    moments = (
        (qkv_first, qkv_second),
        (out_first, out_second),
        (up_first, up_second),
        (down_first, down_second),
        (bias_first, bias_second),
        (gains_first, gains_second),
    )
    results = [
        lamb_direction(weight, gradient, states[0], states[1])
        for weight, gradient, states in zip(weights, gradients, moments)
    ]
    table_momentum, table_variance, table_direction, table_squares = table_moments(
        embedding, embedding_first, embedding_second, own_table, other_table
    )
    first_mdl = (mdl_index == 0).astype(f32)
    first_dat = (dat_index == 0).astype(f32)
    holder_mask = [1.0, 1.0, 1.0, 1.0, first_dat]
    square_rows = [table_squares[:2, 0] * first_mdl] + [
        jnp.stack(
            [
                jnp.sum(weights[position] * weights[position]),
                jnp.sum(results[position][2] * results[position][2]),
            ]
        )
        * holder_mask[position]
        for position in range(5)
    ]
    gain_rows = jnp.stack(
        [jnp.sum(norm_gains * norm_gains, axis=1), jnp.sum(results[5][2] * results[5][2], axis=1)],
        axis=1,
    ) * (first_mdl * first_dat)
    square_table = jnp.concatenate([jnp.stack(square_rows), gain_rows], axis=0)
    matrix_norms = jnp.sqrt(lax.psum(square_table, ("dat", "mdl")))
    rates = LEARN_RATE * matrix_norms[:, 0] / matrix_norms[:, 1]
    updated = [weights[position] - rates[position + 1] * results[position][2] for position in range(5)]
    updated.append(norm_gains - rates[6:, None] * results[5][2])
    outputs = [
        jnp.stack([loss_total, live_total]),
        matrix_norms,
        table_momentum,
        table_variance,
        table_update(rates[:1], embedding, table_direction),
    ]
    for position in range(6):
        outputs.extend([results[position][0], results[position][1], updated[position]])
    return tuple(outputs)


def solution(mesh):
    state = [
        P("dat", None),
        P("dat", None, "mdl"),
        P("mdl", "dat"),
        P("dat", "mdl"),
        P("dat", "mdl"),
        P(None, "mdl"),
        P(),
    ]
    placed = [P(("grp", "dat"), None), P(("grp", "dat")), P(("grp", "dat")), P(), P(("grp", "dat"))]
    placed += state + [spec for spec in state for _ in range(2)]
    return jax.shard_map(
        shards,
        mesh=mesh,
        in_specs=tuple(placed),
        out_specs=(P(), P(), *[spec for spec in state for _ in range(3)]),
        check_vma=False,
    )
```

```python
import functools

import jax
import jax.numpy as jnp
from jax import lax
from jax.experimental import pallas as pl
from jax.experimental.pallas import tpu as pltpu
from jax.sharding import PartitionSpec as P

HEADS = 12
HEAD = 64
BUCKETS = 32
STEP = 10


SOFTMAX_WARMTH = 0.01
NORM_EPS = 1e-06
BUCKET_EDGES = (12, 16, 23, 32, 46, 64, 91)
BETA_ONE = 0.9
BETA_TWO = 0.999
ADAM_EPS = 1e-06
WEIGHT_DECAY = 0.01
LEARN_RATE = 0.5
MASK_FILL = -1000000000.0
MAX_PRECISION = lax.Precision.HIGHEST
LANES = 128
bf = jnp.bfloat16
f32 = jnp.float32


BLOCK=128
NT=(((1,),(1,)),((),()))
TN=(((0,),(0,)),((),()))

def toeplitz(line, rows):
    out = line
    size = 1
    while size < rows:
        out = jnp.concatenate([out, pltpu.roll(out, size, 1)], axis=0)
        size *= 2
    return out

def diagonal_sums(square):
    rows, width = square.shape
    while rows > 8:
        rows //= 2
        square = square[:rows] + pltpu.roll(square[rows:], width - rows, 1)
    for shift in (4, 2, 1):
        square = square + pltpu.roll(pltpu.roll(square, width - shift, 1), 8 - shift, 0)
    return square[:1]

def attend_kernel(pairs, scale, lens_ref, line_ref, qkv_ref, mixed_ref, lse_ref):
    items, length, _ = mixed_ref.shape
    blocks = length // BLOCK
    first = lax.broadcasted_iota(jnp.int32, (1, LANES), 1) < HEAD
    lane = lax.broadcasted_iota(jnp.int32, (BLOCK, LANES), 1)
    column = lax.broadcasted_iota(jnp.int32, (1, length), 1)

    def one_pair(pair, carry):
        at = lambda part: pl.ds(pl.multiple_of((part * pairs + pair) * LANES, LANES), LANES)
        biases = [toeplitz(line_ref[pl.ds(2 * pair + head, 1), :], BLOCK) for head in range(2)]
        for item in range(items):
            keys = qkv_ref[item, :, at(1)]
            values = qkv_ref[item, :, at(2)]
            valid = column < lens_ref[item]
            for block in range(blocks):
                rows = pl.ds(block * BLOCK, BLOCK)
                queries = qkv_ref[item, rows, at(0)] * scale
                low = length - block * BLOCK
                mixed = []
                stats = jnp.zeros((BLOCK, LANES), f32)
                for head in range(2):
                    mine = first if head == 0 else jnp.logical_not(first)
                    scores = lax.dot_general(jnp.where(mine, queries, 0), keys, NT, preferred_element_type=f32)
                    scores = jnp.where(valid, scores + biases[head][:, low : low + length], MASK_FILL)
                    top = jnp.max(scores, axis=1, keepdims=True)
                    powers = jnp.exp(scores - top)
                    whole = jnp.sum(powers, axis=1, keepdims=True)
                    probs = (powers * (1.0 / whole)).astype(bf)
                    mixed.append(jnp.dot(probs, values, preferred_element_type=f32))
                    stats = jnp.where(lane == head, top + jnp.log(whole), stats)
                mixed_ref[item, rows, at(0)] = jnp.where(first, mixed[0], mixed[1]).astype(bf)
                lse_ref[item, rows, at(0)] = stats
        return carry

    lax.fori_loop(0, pairs, one_pair, 0)

def attend(qkv, lines, lengths):
    items, length, width = qkv.shape
    width //= 3
    pairs = width // LANES
    vm = pl.BlockSpec(memory_space=pltpu.VMEM)
    return pl.pallas_call(
        functools.partial(attend_kernel, pairs, HEAD ** -0.5),
        in_specs=[pl.BlockSpec(memory_space=pltpu.SMEM), vm, vm],
        out_specs=[vm, vm],
        out_shape=[jax.ShapeDtypeStruct((items, length, width), bf), jax.ShapeDtypeStruct((items, length, width), f32)],
        compiler_params=pltpu.CompilerParams(vmem_limit_bytes=40 * 2**20),
        cost_estimate=pl.CostEstimate(flops=8 * items * length * length * width, bytes_accessed=items * length * width * 12, transcendentals=items * length * length * width // HEAD),
        name="attend",
    )(lengths, lines, qkv)

def attend_back_kernel(pairs, scale, lens_ref, line_ref, qkv_ref, lse_ref, dmix_ref, dqkv_ref, dline_ref, dkey, dval, diag):
    items, length, _ = dmix_ref.shape
    blocks = length // BLOCK
    first = lax.broadcasted_iota(jnp.int32, (1, LANES), 1) < HEAD
    column = lax.broadcasted_iota(jnp.int32, (1, length), 1)

    def one_pair(pair, carry):
        at = lambda part: pl.ds(pl.multiple_of((part * pairs + pair) * LANES, LANES), LANES)
        biases = [toeplitz(line_ref[pl.ds(2 * pair + head, 1), :], BLOCK) for head in range(2)]
        diag[...] = jnp.zeros_like(diag)
        for item in range(items):
            keys = qkv_ref[item, :, at(1)]
            values = qkv_ref[item, :, at(2)]
            valid = column < lens_ref[item]
            for block in range(blocks):
                rows = pl.ds(block * BLOCK, BLOCK)
                queries = qkv_ref[item, rows, at(0)] * scale
                given = dmix_ref[item, rows, at(0)]
                stats = lse_ref[item, rows, at(0)]
                low = length - block * BLOCK
                dquery, dkeys, dvals = [], [], []
                for head in range(2):
                    mine = first if head == 0 else jnp.logical_not(first)
                    scores = lax.dot_general(jnp.where(mine, queries, 0), keys, NT, preferred_element_type=f32)
                    scores = jnp.where(valid, scores + biases[head][:, low : low + length], MASK_FILL)
                    probs = jnp.exp(scores - stats[:, head : head + 1])
                    dprobs = lax.dot_general(jnp.where(mine, given, 0), values, NT, preferred_element_type=f32)
                    inner = jnp.sum(probs * dprobs, axis=1, keepdims=True)
                    dscores = probs * (dprobs - inner)
                    diag[head, :, low : low + length] += dscores
                    low_scores = dscores.astype(bf)
                    dquery.append(jnp.dot(low_scores, keys, preferred_element_type=f32))
                    dkeys.append(lax.dot_general(low_scores, queries, TN, preferred_element_type=f32))
                    dvals.append(lax.dot_general(probs.astype(bf), given, TN, preferred_element_type=f32))
                dqkv_ref[item, rows, at(0)] = (jnp.where(first, dquery[0], dquery[1]) * scale).astype(bf)
                dk = jnp.where(first, dkeys[0], dkeys[1])
                dv = jnp.where(first, dvals[0], dvals[1])
                if block == 0:
                    dkey[...] = dk
                    dval[...] = dv
                else:
                    dkey[...] += dk
                    dval[...] += dv
            dqkv_ref[item, :, at(1)] = dkey[...].astype(bf)
            dqkv_ref[item, :, at(2)] = dval[...].astype(bf)
        for head in range(2):
            dline_ref[pl.ds(2 * pair + head, 1), :] = diagonal_sums(diag[head])
        return carry

    lax.fori_loop(0, pairs, one_pair, 0)

def attend_back(qkv, lines, lengths, lse, dmixed):
    items, length, width = dmixed.shape
    pairs = width // LANES
    vm = pl.BlockSpec(memory_space=pltpu.VMEM)
    return pl.pallas_call(
        functools.partial(attend_back_kernel, pairs, HEAD ** -0.5),
        in_specs=[pl.BlockSpec(memory_space=pltpu.SMEM), vm, vm, vm, vm],
        out_specs=[vm, vm],
        out_shape=[jax.ShapeDtypeStruct(qkv.shape, bf), jax.ShapeDtypeStruct(lines.shape, f32)],
        scratch_shapes=[pltpu.VMEM((length, LANES), f32), pltpu.VMEM((length, LANES), f32), pltpu.VMEM((2, BLOCK, 2 * length), f32)],
        compiler_params=pltpu.CompilerParams(vmem_limit_bytes=40 * 2**20),
        cost_estimate=pl.CostEstimate(flops=20 * items * length * length * width, bytes_accessed=items * length * width * 20, transcendentals=items * length * length * width // HEAD),
        name="attend_back",
    )(lengths, lines, qkv, lse, dmixed)


def split_features(features):
    whole = features // LANES * LANES
    return whole, features - whole


def tile_count(features):
    whole, rest = split_features(features)
    return whole // LANES + (rest > 0)


def first_of_pair(packed, features):
    return packed[..., :features]


def second_of_pair(packed, features):
    whole, rest = split_features(features)
    tail = packed[..., features : features + rest]
    return jnp.concatenate([packed[..., features + rest :], tail], axis=-1) if whole else tail


def pack_pair(first, second):
    whole, _ = split_features(first.shape[-1])
    parts = [first, second[..., whole:], second[..., :whole]] if whole else [first, second]
    return jnp.concatenate(parts, axis=-1)


def packed_starts(features, half):
    whole, rest = split_features(features)
    base = 0 if half == 0 else features + rest
    return [base + low for low in range(0, whole, LANES)] + ([whole] if rest else [])


def gather_kernel(features, load_steps, batch, table_ref, ids_ref, out_ref, *scratch):
    step = pl.program_id(0)
    width = table_ref.shape[1]
    tiles = tile_count(features)
    whole, rest = split_features(features)
    stash = scratch[:tiles]
    rows = [scratch[tiles : 2 * tiles], scratch[2 * tiles :]]

    @pl.when(step < load_steps)
    def _():
        base = pl.multiple_of(step * width, width)
        for tile in range(tiles):
            low = tile * LANES
            part = table_ref[low : min(features, low + LANES), :].astype(bf).astype(f32)
            if low == whole:
                blank = [jnp.zeros((LANES - 2 * rest, width), f32)] if 2 * rest < LANES else []
                part = jnp.concatenate([part, part, *blank], axis=0)
            stash[tile][pl.ds(base, width), :] = part.T

    @pl.when(step >= load_steps)
    def _():
        count = out_ref.shape[0]
        for half in range(2):
            def take(index, carry):
                start = pl.multiple_of(index * batch, batch)
                tokens = [ids_ref[0, half, start + inner] for inner in range(batch)]
                for tile in range(tiles):
                    for inner in range(batch):
                        rows[half][tile][pl.ds(start + inner, 1), :] = stash[tile][pl.ds(tokens[inner], 1), :]
                return carry
            lax.fori_loop(0, count // batch, take, 0)
        for half in range(2):
            for tile in range(whole // LANES):
                low = packed_starts(features, half)[tile]
                out_ref[:, low : low + LANES] = rows[half][tile][...].astype(bf)
        if rest:
            lane = lax.broadcasted_iota(jnp.int32, (1, LANES), 1)
            shared = jnp.where(lane < rest, rows[0][-1][...], rows[1][-1][...]).astype(bf)
            out_ref[:, whole : whole + 2 * rest] = shared[:, : 2 * rest]


def gather_rows(table, ids, width=4096, batch=16):
    features, vocab = table.shape
    steps, _, chunk = ids.shape
    tiles = tile_count(features)
    load_steps = pl.cdiv(vocab, width)
    return pl.pallas_call(
        functools.partial(gather_kernel, features, load_steps, batch),
        grid=(load_steps + steps,),
        in_specs=[
            pl.BlockSpec((features, width), lambda s: (0, jnp.minimum(s, load_steps - 1))),
            pl.BlockSpec((1, 2, chunk), lambda s: (jnp.maximum(s - load_steps, 0), 0, 0), memory_space=pltpu.SMEM),
        ],
        out_specs=pl.BlockSpec((chunk, 2 * features), lambda s: (jnp.maximum(s - load_steps, 0), 0)),
        out_shape=jax.ShapeDtypeStruct((steps * chunk, 2 * features), bf),
        scratch_shapes=[pltpu.VMEM((load_steps * width, LANES), f32)] * tiles + [pltpu.VMEM((chunk, LANES), f32)] * (2 * tiles),
        compiler_params=pltpu.CompilerParams(vmem_limit_bytes=60 * 2**20),
        cost_estimate=pl.CostEstimate(flops=0, bytes_accessed=80 * 2**20, transcendentals=0),
        name="gather_rows",
    )(table, ids)


def merge_rows(features, batch, ids_row_ref, rows_ref, summed):
    count = rows_ref.shape[0]
    whole, rest = split_features(features)
    place = lax.broadcasted_iota(jnp.int32, (LANES, LANES), 0) // batch
    same_batch = place == lax.broadcasted_iota(jnp.int32, (LANES, LANES), 1) // batch
    lane = lax.broadcasted_iota(jnp.int32, (1, LANES), 1)
    for low in range(0, count, LANES):
        block = slice(low, low + LANES)
        for half in range(2):
            across = jnp.broadcast_to(ids_row_ref[0, half : half + 1, block], (LANES, LANES))
            match = jnp.where((across == across.T) & same_batch, 1.0, 0.0).astype(bf)
            for tile, start in enumerate(packed_starts(features, half)):
                if start == whole:
                    part = jnp.dot(match, rows_ref[block, start : start + 2 * rest], preferred_element_type=f32)
                    if 2 * rest < LANES:
                        part = jnp.concatenate([part, jnp.zeros((LANES, LANES - 2 * rest), f32)], axis=1)
                    mine = lane < rest if half == 0 else (lane >= rest) & (lane < 2 * rest)
                    part = jnp.where(mine, part, 0.0)
                else:
                    part = jnp.dot(match, rows_ref[block, start : start + LANES], preferred_element_type=f32)
                summed[half][tile][block, :] = part


def add_rows(batch, ids_ref, totals, summed):
    count = summed[0][0].shape[0]
    for half in range(2):
        def add(index, carry):
            start = pl.multiple_of(index * batch, batch)
            tokens = [ids_ref[0, half, start + inner] for inner in range(batch)]
            for total, rows in zip(totals, summed[half]):
                fresh = [
                    total[pl.ds(tokens[inner], 1), :] + rows[pl.ds(start + inner, 1), :] for inner in range(batch)
                ]
                for inner in range(batch):
                    total[pl.ds(tokens[inner], 1), :] = fresh[inner]
            return carry
        lax.fori_loop(0, count // batch, add, 0)


def table_columns(features, totals, base, width):
    whole, rest = split_features(features)
    pieces = [total[pl.ds(base, width), :].T for total in totals]
    if rest:
        pieces[-1] = pieces[-1][:rest] + pieces[-1][rest : 2 * rest]
    return pieces


def scatter_kernel(features, scatter_steps, batch, ids_ref, ids_row_ref, rows_ref, out_ref, *scratch):
    step = pl.program_id(0)
    width = out_ref.shape[1]
    tiles = tile_count(features)
    totals = scratch[:tiles]
    summed = [scratch[tiles : 2 * tiles], scratch[2 * tiles :]]

    @pl.when(step == 0)
    def _():
        for total in totals:
            total[...] = jnp.zeros_like(total)

    @pl.when(step < scatter_steps)
    def _():
        merge_rows(features, batch, ids_row_ref, rows_ref, summed)
        add_rows(batch, ids_ref, totals, summed)

    @pl.when(step >= scatter_steps)
    def _():
        base = pl.multiple_of((step - scatter_steps) * width, width)
        low = 0
        for piece in table_columns(features, totals, base, width):
            out_ref[low : low + piece.shape[0], :] = piece.astype(bf)
            low += piece.shape[0]


def scatter_scratch(features, vocab, chunk):
    tiles = tile_count(features)
    return [pltpu.VMEM((vocab, LANES), f32)] * tiles + [pltpu.VMEM((chunk, LANES), f32)] * (2 * tiles)


def scatter_rows(rows, ids, vocab, features, width=2048, batch=16):
    steps, _, chunk = ids.shape
    flush = pl.cdiv(vocab, width)
    at = lambda s: jnp.minimum(s, steps - 1)
    return pl.pallas_call(
        functools.partial(scatter_kernel, features, steps, batch),
        grid=(steps + flush,),
        in_specs=[
            pl.BlockSpec((1, 2, chunk), lambda s: (at(s), 0, 0), memory_space=pltpu.SMEM),
            pl.BlockSpec((1, 2, chunk), lambda s: (at(s), 0, 0)),
            pl.BlockSpec((chunk, 2 * features), lambda s: (at(s), 0)),
        ],
        out_specs=pl.BlockSpec((features, width), lambda s: (0, jnp.maximum(s - steps, 0))),
        out_shape=jax.ShapeDtypeStruct((features, vocab), bf),
        scratch_shapes=scatter_scratch(features, flush * width, chunk),
        compiler_params=pltpu.CompilerParams(vmem_limit_bytes=60 * 2**20),
        cost_estimate=pl.CostEstimate(flops=0, bytes_accessed=100 * 2**20, transcendentals=0),
        name="scatter_rows",
    )(ids, ids, rows)


def assemble_kernel(features, spread_ref, gain_ref, embedded_ref, normed_ref):
    for half, take in enumerate((first_of_pair, second_of_pair)):
        row = jnp.concatenate([take(spread_ref[part], features) for part in range(spread_ref.shape[0])], axis=1)
        embedded_ref[half] = row
        stream = row.astype(f32)
        scale = lax.rsqrt(jnp.mean(stream * stream, axis=1, keepdims=True) + NORM_EPS)
        normed_ref[half] = (stream * scale * gain_ref[...]).astype(bf)


def assemble(spread, gain, block=128):
    parts, count, features = spread.shape
    features //= 2
    width = parts * features
    block = min(block, count)
    out = jax.ShapeDtypeStruct((2, count, width), bf)
    whole_block = pl.BlockSpec((2, block, width), lambda s: (0, s, 0))
    embedded, normed = pl.pallas_call(
        functools.partial(assemble_kernel, features),
        grid=(count // block,),
        in_specs=[
            pl.BlockSpec((parts, block, 2 * features), lambda s: (0, s, 0)),
            pl.BlockSpec((1, width), lambda s: (0, 0)),
        ],
        out_specs=[whole_block, whole_block],
        out_shape=[out, out],
        compiler_params=pltpu.CompilerParams(vmem_limit_bytes=30 * 2**20),
        name="assemble",
    )(spread, gain.reshape(1, width))
    return embedded.reshape(2 * count, width), normed.reshape(2 * count, width)


def pack_back_kernel(features, back_ref, embedded_ref, passed_ref, gain_ref, packed_ref, grad_gain_ref):
    gain = gain_ref[...]
    halves = []
    grad_gain = jnp.zeros_like(gain)
    for half in range(2):
        stream = embedded_ref[half].astype(f32)
        back = back_ref[half]
        scale = lax.rsqrt(jnp.mean(stream * stream, axis=1, keepdims=True) + NORM_EPS)
        unit = stream * scale
        grad_gain += jnp.sum(back * unit, axis=0, keepdims=True)
        pulled = back * gain
        along = jnp.mean(pulled * unit, axis=1, keepdims=True)
        halves.append((passed_ref[half] + scale * (pulled - unit * along)).astype(bf))
    for part in range(packed_ref.shape[0]):
        cut = slice(part * features, (part + 1) * features)
        packed_ref[part] = pack_pair(halves[0][:, cut], halves[1][:, cut])

    @pl.when(pl.program_id(0) == 0)
    def _():
        grad_gain_ref[...] = jnp.zeros_like(grad_gain_ref)

    grad_gain_ref[...] += grad_gain


def pack_back(back, embedded, passed, gain, features, block=128):
    rows, width = back.shape
    count, parts = rows // 2, width // features
    block = min(block, count)
    pair = pl.BlockSpec((2, block, width), lambda s: (0, s, 0))
    line = pl.BlockSpec((1, width), lambda s: (0, 0))
    packed, grad_gain = pl.pallas_call(
        functools.partial(pack_back_kernel, features),
        grid=(count // block,),
        in_specs=[pair, pair, pair, line],
        out_specs=[pl.BlockSpec((parts, block, 2 * features), lambda s: (0, s, 0)), line],
        out_shape=[jax.ShapeDtypeStruct((parts, count, 2 * features), bf), jax.ShapeDtypeStruct((1, width), f32)],
        compiler_params=pltpu.CompilerParams(vmem_limit_bytes=30 * 2**20),
        name="pack_back",
    )(back.reshape(2, count, width), embedded.reshape(2, count, width), passed.reshape(2, count, width), gain.reshape(1, width))
    return packed, grad_gain[0]


def finish_kernel(features, vocab, scatter_steps, batch, ids_ref, ids_row_ref, rows_ref, weight_ref, first_ref, second_ref, *rest):
    dense_refs, rest = rest[:3], rest[3:]
    momentum_ref, variance_ref, direction_ref, squares_ref = rest[:4]
    scratch = rest[4:]
    step = pl.program_id(0)
    tiles = tile_count(features)
    totals = scratch[:tiles]
    summed = [scratch[tiles : 2 * tiles], scratch[2 * tiles :]]

    @pl.when(step == 0)
    def _():
        for total in totals:
            total[...] = jnp.zeros_like(total)
        squares_ref[...] = jnp.zeros_like(squares_ref)

    @pl.when(step < scatter_steps)
    def _():
        merge_rows(features, batch, ids_row_ref, rows_ref, summed)
        add_rows(batch, ids_ref, totals, summed)

    @pl.when(step >= scatter_steps)
    def _():
        width = weight_ref.shape[1]
        base = pl.multiple_of((step - scatter_steps) * width, width)
        inside = base + lax.broadcasted_iota(jnp.int32, (1, width), 1) < vocab
        low = 0
        for piece in table_columns(features, totals, base, width):
            cut = slice(low, low + piece.shape[0])
            low += piece.shape[0]
            weight = weight_ref[cut, :]
            gradient = piece
            for dense_ref in dense_refs:
                gradient = gradient + dense_ref[cut, :].astype(f32)
            momentum, variance, direction = lamb_direction(weight, gradient, first_ref[cut, :], second_ref[cut, :])
            momentum_ref[cut, :] = momentum
            variance_ref[cut, :] = variance
            direction_ref[cut, :] = direction.astype(bf)
            for line, value in enumerate((weight, direction)):
                value = jnp.where(inside, value, 0.0)
                squares_ref[line : line + 1, :] += jnp.sum(value * value, axis=0, keepdims=True)


def finish(rows, ids, weight, first, second, dense, width=1024, batch=16):
    features, vocab = weight.shape
    steps, _, chunk = ids.shape
    columns = pl.cdiv(vocab, width)
    at = lambda s: jnp.minimum(s, steps - 1)
    block = pl.BlockSpec((features, width), lambda s: (0, jnp.maximum(s - steps, 0)))
    full = jax.ShapeDtypeStruct(weight.shape, f32)
    return pl.pallas_call(
        functools.partial(finish_kernel, features, vocab, steps, batch),
        grid=(steps + columns,),
        in_specs=[
            pl.BlockSpec((1, 2, chunk), lambda s: (at(s), 0, 0), memory_space=pltpu.SMEM),
            pl.BlockSpec((1, 2, chunk), lambda s: (at(s), 0, 0)),
            pl.BlockSpec((chunk, 2 * features), lambda s: (at(s), 0)),
        ]
        + [block] * 6,
        out_specs=[block, block, block, pl.BlockSpec((8, width), lambda s: (0, 0))],
        out_shape=[full, full, jax.ShapeDtypeStruct(weight.shape, bf), jax.ShapeDtypeStruct((8, width), f32)],
        scratch_shapes=scatter_scratch(features, columns * width, chunk),
        compiler_params=pltpu.CompilerParams(vmem_limit_bytes=62 * 2**20),
        cost_estimate=pl.CostEstimate(flops=0, bytes_accessed=300 * 2**20, transcendentals=0),
        name="finish",
    )(ids, ids, rows, weight, first, second, *dense)


MESH = pl.DeviceIdType.MESH


def share_kernel(axes, facts_ref, out_ref, send, received):
    places = [lax.axis_index(axis) for axis in axes]
    sizes = [lax.axis_size(axis) for axis in axes]
    barrier = pltpu.get_barrier_semaphore()
    for axis, place, size in zip(axes, places, sizes):
        for step in range(1, size):
            pl.semaphore_signal(barrier, inc=1, device_id={axis: lax.rem(place + step, size)}, device_id_type=MESH)
    pl.semaphore_wait(barrier, sum(sizes) - len(sizes))
    out_ref[places[0], places[1]] = facts_ref[...]
    slot = 0
    for axis, place, size in reversed(list(zip(axes, places, sizes))):
        block = out_ref.at[places[0]] if axis == axes[0] else out_ref.at[places[0], places[1]]
        copies = []
        for step in range(1, size):
            copy = pltpu.make_async_remote_copy(
                src_ref=block,
                dst_ref=block,
                send_sem=send.at[slot],
                recv_sem=received.at[slot],
                device_id={axis: lax.rem(place + step, size)},
                device_id_type=MESH,
            )
            copy.start()
            copies.append(copy)
            slot += 1
        for copy in copies:
            copy.wait()


def share_facts(facts, axes, sizes):
    slots = sum(sizes) - 2
    return pl.pallas_call(
        functools.partial(share_kernel, axes),
        in_specs=[pl.BlockSpec(memory_space=pltpu.VMEM)],
        out_specs=pl.BlockSpec(memory_space=pltpu.VMEM),
        out_shape=jax.ShapeDtypeStruct((*sizes, *facts.shape), facts.dtype),
        scratch_shapes=[pltpu.SemaphoreType.DMA((slots,)), pltpu.SemaphoreType.DMA((slots,))],
        compiler_params=pltpu.CompilerParams(collective_id=0, has_side_effects=True),
        name="share_facts",
    )(facts)


def sum_squares_kernel(axes, rows_ref, table_ref, out_ref, slots, send, received):
    places = [lax.axis_index(axis) for axis in axes]
    sizes = [lax.axis_size(axis) for axis in axes]
    count = sizes[0] * sizes[1]
    mine = places[0] * sizes[1] + places[1]
    barrier = pltpu.get_barrier_semaphore()
    peers = []
    for step in range(1, count):
        peer = lax.rem(mine + step, count)
        peers.append({axes[0]: peer // sizes[1], axes[1]: lax.rem(peer, sizes[1])})
    for peer in peers:
        pl.semaphore_signal(barrier, inc=1, device_id=peer, device_id_type=MESH)
    pl.semaphore_wait(barrier, count - 1)
    lane = lax.broadcasted_iota(jnp.int32, (1, LANES), 1)
    sums = jnp.sum(rows_ref[...], axis=1, keepdims=True)
    slots[mine] = table_ref[...]
    slots[mine, 0:1, :] = jnp.where(lane == 0, sums[0:1], jnp.where(lane == 1, sums[1:2], 0.0)) * table_ref[0:1, :]
    copies = []
    for step, peer in enumerate(peers):
        copy = pltpu.make_async_remote_copy(
            src_ref=slots.at[mine],
            dst_ref=slots.at[mine],
            send_sem=send.at[step],
            recv_sem=received.at[step],
            device_id=peer,
            device_id_type=MESH,
        )
        copy.start()
        copies.append(copy)
    for copy in copies:
        copy.wait()
    total = slots[0]
    for other in range(1, count):
        total = total + slots[other]
    out_ref[...] = total


def sum_over(rows, table, axes, sizes):
    count = sizes[0] * sizes[1]
    return pl.pallas_call(
        functools.partial(sum_squares_kernel, axes),
        in_specs=[pl.BlockSpec(memory_space=pltpu.VMEM)] * 2,
        out_specs=pl.BlockSpec(memory_space=pltpu.VMEM),
        out_shape=jax.ShapeDtypeStruct(table.shape, f32),
        scratch_shapes=[
            pltpu.VMEM((count, *table.shape), f32),
            pltpu.SemaphoreType.DMA((count - 1,)),
            pltpu.SemaphoreType.DMA((count - 1,)),
        ],
        compiler_params=pltpu.CompilerParams(collective_id=1, has_side_effects=True),
        name="sum_over",
    )(rows, table)


def sum_all_kernel(near, far, value_ref, out_ref, near_slots, far_slots, send, received):
    places = [lax.axis_index(axis) for axis in (*near, far)]
    sizes = [lax.axis_size(axis) for axis in (*near, far)]
    count = sizes[0] * sizes[1]
    mine = places[0] * sizes[1] + places[1]
    barrier = pltpu.get_barrier_semaphore()
    plane, line = [], []
    for step in range(1, count):
        peer = lax.rem(mine + step, count)
        plane.append({near[0]: peer // sizes[1], near[1]: lax.rem(peer, sizes[1])})
    for step in range(1, sizes[2]):
        line.append({far: lax.rem(places[2] + step, sizes[2])})
    for peer in plane + line:
        pl.semaphore_signal(barrier, inc=1, device_id=peer, device_id_type=MESH)
    pl.semaphore_wait(barrier, len(plane) + len(line))
    slot = 0
    value = value_ref[...]
    for peers, slots, at in ((plane, near_slots, mine), (line, far_slots, places[2])):
        slots[at] = value
        copies = []
        for peer in peers:
            copy = pltpu.make_async_remote_copy(
                src_ref=slots.at[at],
                dst_ref=slots.at[at],
                send_sem=send.at[slot],
                recv_sem=received.at[slot],
                device_id=peer,
                device_id_type=MESH,
            )
            copy.start()
            copies.append(copy)
            slot += 1
        for copy in copies:
            copy.wait()
        value = slots[0]
        for other in range(1, slots.shape[0]):
            value = value + slots[other]
    out_ref[...] = value


def sum_all(value, near, far, sizes):
    count = sizes[0] * sizes[1]
    slots = count - 1 + sizes[2] - 1
    return pl.pallas_call(
        functools.partial(sum_all_kernel, near, far),
        in_specs=[pl.BlockSpec(memory_space=pltpu.VMEM)],
        out_specs=pl.BlockSpec(memory_space=pltpu.VMEM),
        out_shape=jax.ShapeDtypeStruct(value.shape, f32),
        scratch_shapes=[
            pltpu.VMEM((count, *value.shape), f32),
            pltpu.VMEM((sizes[2], *value.shape), f32),
            pltpu.SemaphoreType.DMA((slots,)),
            pltpu.SemaphoreType.DMA((slots,)),
        ],
        compiler_params=pltpu.CompilerParams(collective_id=2, has_side_effects=True),
        name="sum_all",
    )(value)


def lamb_direction(weight, gradient, moment_one, moment_two):
    momentum = BETA_ONE * moment_one + (1.0 - BETA_ONE) * gradient
    variance = BETA_TWO * moment_two + (1.0 - BETA_TWO) * gradient * gradient
    direction = (
        momentum / (1.0 - BETA_ONE**STEP) / (jnp.sqrt(variance / (1.0 - BETA_TWO**STEP)) + ADAM_EPS)
        + WEIGHT_DECAY * weight
    )
    return (momentum, variance, direction)


def table_update_kernel(squares_ref, weight_ref, direction_ref, updated_ref):
    norms = jnp.sqrt(squares_ref[0:1, :])
    rate = LEARN_RATE * norms[:, 0:1] / norms[:, 1:2]
    updated_ref[...] = weight_ref[...] - rate * direction_ref[...].astype(f32)


def table_update(squares, weight, direction, rows=16):
    features, vocab = weight.shape
    block = pl.BlockSpec((rows, vocab), lambda s: (s, 0))
    return pl.pallas_call(
        table_update_kernel,
        grid=(features // rows,),
        in_specs=[pl.BlockSpec(squares.shape, lambda s: (0, 0)), block, block],
        out_specs=block,
        out_shape=jax.ShapeDtypeStruct(weight.shape, f32),
        compiler_params=pltpu.CompilerParams(vmem_limit_bytes=40 * 2**20),
        name="table_update",
    )(squares, weight, direction)


def norm_scale(stream, gain_row):
    return (
        stream * lax.rsqrt(jnp.mean(stream * stream, axis=-1, keepdims=True) + NORM_EPS) * gain_row
    )


def gelu_tanh(pre_act):
    return jax.nn.gelu(pre_act, approximate=True)


def dot(left, right, dims=((1,), (0,))):
    return lax.dot_general(left, right, (dims, ((), ())), preferred_element_type=f32)


def bucket_onehot(length):
    relative = jnp.arange(2 * length, dtype=jnp.int32) - length
    distance = jnp.abs(relative)
    far_bucket = 8 + sum(((distance >= threshold).astype(jnp.int32) for threshold in BUCKET_EDGES))
    bucket = jnp.where(distance < 8, distance, far_bucket) + jnp.where(relative > 0, 16, 0)
    return (bucket[:, None] == jnp.arange(BUCKETS)).astype(f32)


def after(value, *others):
    return lax.optimization_barrier((value, *others))[0]


def arrivals(groups):
    found = []
    for group in range(groups):
        found.append([])
        for hop in range(1, groups):
            for source, way in ((group - hop, 0), (group + hop, 1)):
                if 0 <= source < groups:
                    found[-1].append((source, way, hop))
    return found


def swap_cores(value):
    size = lax.axis_size("mdl")
    return lax.ppermute(value, "mdl", [(core, (core + 1) % size) for core in range(size)])


def shards(
    token_ids,
    item_lengths,
    prefix_lengths,
    group_live,
    partner,
    embedding,
    qkv_weight,
    out_weight,
    up_weight,
    down_weight,
    bias_table,
    norm_gains,
    embedding_first,
    embedding_second,
    qkv_first,
    qkv_second,
    out_first,
    out_second,
    up_first,
    up_second,
    down_first,
    down_second,
    bias_first,
    bias_second,
    gains_first,
    gains_second,
):
    item_count, length = token_ids.shape
    features, vocab = embedding.shape
    grp_size, dat_size, mdl_size = lax.axis_size("grp"), lax.axis_size("dat"), lax.axis_size("mdl")
    group_index, dat_index, mdl_index = lax.axis_index("grp"), lax.axis_index("dat"), lax.axis_index("mdl")
    mine = item_count // mdl_size
    rows = mine * length
    pair_rows = rows // 2
    chunk = min(512, pair_rows)
    chunks = pair_rows // chunk
    group_items = item_count * dat_size
    width = features * dat_size
    first_slot = dat_index * item_count + mdl_index * mine

    tn = ((0,), (0,))
    nt = ((1,), (1,))

    facts = jnp.concatenate([token_ids, partner[:, None]], axis=1)
    facts = jnp.pad(facts, ((0, 0), (0, -facts.shape[1] % LANES)))
    shared = share_facts(facts, ("grp", "dat"), (grp_size, dat_size))
    all_ids = shared[..., :length].reshape(grp_size, dat_size, mdl_size, 2, chunks, chunk).transpose(2, 0, 1, 4, 3, 5)
    all_ids = all_ids.reshape(mdl_size, grp_size, dat_size * chunks, 2, chunk)
    core_ids = lax.dynamic_index_in_dim(all_ids, mdl_index, 0, keepdims=False)
    other_ids = lax.dynamic_index_in_dim(all_ids, (mdl_index + 1) % mdl_size, 0, keepdims=False)
    group_partner = lax.dynamic_index_in_dim(shared[..., length], group_index, 0, keepdims=False).reshape(-1)
    my_lengths = lax.dynamic_slice_in_dim(item_lengths, mdl_index * mine, mine)
    my_prefixes = lax.dynamic_slice_in_dim(prefix_lengths, mdl_index * mine, mine)

    def gathered(*shards):
        return lax.all_gather(
            jnp.concatenate([shard.astype(bf) for shard in shards], axis=1), "dat", axis=0, tiled=True
        )

    def halves(own):
        return (own, swap_cores(own))

    first_own = gathered(qkv_weight.reshape(features, -1), out_weight.T)
    split = qkv_weight.shape[1] * qkv_weight.shape[2]
    first_halves = halves(first_own)
    qkv_halves = [part[:, :split] for part in first_halves]
    out_halves = [part[:, split:] for part in first_halves]
    up_own = gathered(after(up_weight, first_own))
    onehot = bucket_onehot(length)
    line_halves = [
        jnp.einsum("rb,bh->hr", onehot, table, precision=MAX_PRECISION)
        for table in (bias_table, swap_cores(bias_table))
    ]

    looked_up = gather_rows(embedding, lax.dynamic_index_in_dim(core_ids, group_index, 0, keepdims=False))
    spread = lax.all_to_all(
        looked_up.reshape(dat_size, pair_rows, 2 * features), "dat", split_axis=0, concat_axis=0, tiled=True
    )
    embedded_low, normed_one = assemble(spread, norm_gains[0])
    down_own = gathered(after(down_weight, embedded_low))
    embedded = embedded_low.astype(f32)
    qkv_rows = [dot(normed_one, weight).astype(bf).reshape(mine, length, -1) for weight in qkv_halves]
    mixed, log_totals = zip(*[attend(item_qkv, lines, my_lengths) for item_qkv, lines in zip(qkv_rows, line_halves)])
    mixed_rows = [heads.reshape(rows, -1) for heads in mixed]
    up_halves = halves(after(up_own, mixed[0]))
    down_halves = halves(after(down_own, mixed[1]))
    after_attn = embedded + (dot(mixed_rows[0], out_halves[0], nt) + dot(mixed_rows[1], out_halves[1], nt))
    normed_two_f, norm_two_back = jax.vjp(norm_scale, after_attn, norm_gains[1])
    normed_two = normed_two_f.astype(bf)
    gate_acts, gelu_backs = zip(*[jax.vjp(gelu_tanh, dot(normed_two, weight)) for weight in up_halves])
    activated = [act.astype(bf) for act in gate_acts]
    after_ffn = after_attn + (
        dot(activated[0], down_halves[0], nt) + dot(activated[1], down_halves[1], nt)
    )
    positions = jnp.arange(length)
    pool_mask = (
        (positions[None, :] >= my_prefixes[:, None]) & (positions[None, :] < my_lengths[:, None])
    ).astype(f32)

    def pool_tail(stream, gain_row):
        normed_three = norm_scale(stream, gain_row).reshape(mine, length, -1)
        pooled = jnp.sum(normed_three * pool_mask[:, :, None], axis=1) / jnp.sum(pool_mask, axis=1, keepdims=True)
        return pooled * lax.rsqrt(jnp.sum(pooled * pooled, axis=1, keepdims=True) + NORM_EPS)

    vectors, tail_back = jax.vjp(pool_tail, after_ffn, norm_gains[2])

    group_vectors = lax.all_gather(vectors, ("dat", "mdl"), axis=0, tiled=True)
    live_count = jnp.sum(jnp.where(jnp.arange(grp_size) == group_index, group_live, 0))
    live_total = jnp.sum(group_live).astype(f32)
    slots = jnp.arange(group_items)
    live_rows = slots < live_count
    logits = jnp.dot(group_vectors, group_vectors.T, precision=MAX_PRECISION) / SOFTMAX_WARMTH
    allowed = live_rows[None, :] & (slots[None, :] != slots[:, None])
    masked = jnp.where(allowed, logits, MASK_FILL)
    row_top = jnp.max(masked, axis=1, keepdims=True)
    log_total = row_top[:, 0] + jnp.log(jnp.sum(jnp.exp(masked - row_top), axis=1))
    mate_hits = slots[None, :] == group_partner[:, None]
    target = jnp.sum(jnp.where(mate_hits, logits, 0.0), axis=1)
    loss_part = jnp.sum(jnp.where(live_rows, log_total - target, 0.0))
    row_weight = jnp.where(live_rows, 1.0 / live_total, 0.0)
    grad_logits = (
        row_weight[:, None] * (jnp.exp(masked - log_total[:, None]) - mate_hits.astype(f32)) / SOFTMAX_WARMTH
    )
    my_pulls = lax.dynamic_slice_in_dim(grad_logits + grad_logits.T, first_slot, mine)
    grad_vectors = jnp.dot(my_pulls, group_vectors, precision=MAX_PRECISION)

    def both_cores(own, other):
        return (own + swap_cores(other.astype(bf)).astype(f32)).astype(bf)

    def scattered(total):
        return lax.psum_scatter(total, "dat", scatter_dimension=0, tiled=True)

    grad_after_ffn, grad_gain_three = tail_back(grad_vectors)
    grad_ffn = grad_after_ffn.astype(bf)
    total_down = both_cores(*[dot(grad_ffn, act, tn) for act in activated])
    grad_gates = [
        back(dot(grad_ffn, weight))[0].astype(bf) for back, weight in zip(gelu_backs, down_halves)
    ]
    total_up = both_cores(*[dot(normed_two, grad_gate, tn) for grad_gate in grad_gates])
    part_ffn = scattered(jnp.concatenate([total_down, total_up], axis=1))
    two_back = dot(grad_gates[0], up_halves[0], nt) + dot(grad_gates[1], up_halves[1], nt)
    grad_after_attn, grad_gain_two = norm_two_back(two_back)
    grad_after_attn = grad_after_attn + grad_after_ffn
    grad_attn = grad_after_attn.astype(bf)
    total_out = both_cores(*[dot(grad_attn, heads, tn) for heads in mixed_rows])
    grad_mixed = [dot(grad_attn, weight).astype(bf).reshape(mine, length, -1) for weight in out_halves]
    grad_qkv_items, grad_lines = zip(
        *[
            attend_back(item_qkv, lines, my_lengths, stats, grad)
            for item_qkv, lines, stats, grad in zip(qkv_rows, line_halves, log_totals, grad_mixed)
        ]
    )
    grad_qkv_rows = [grad.reshape(rows, -1) for grad in grad_qkv_items]
    one_back = dot(grad_qkv_rows[0], qkv_halves[0], nt) + dot(grad_qkv_rows[1], qkv_halves[1], nt)
    outgoing, grad_gain_one = pack_back(one_back, embedded_low, grad_after_attn, norm_gains[0], features)
    total_qkv = both_cores(*[dot(normed_one, grad, tn) for grad in grad_qkv_rows])
    total_rest = jnp.concatenate([total_qkv, total_out], axis=1)
    part_rest = scattered(total_rest)

    grad_bias_own, grad_bias_other = [
        jnp.einsum("rb,hr->bh", onehot, grad, precision=MAX_PRECISION) for grad in grad_lines
    ]
    grad_bias_all = jnp.where(
        mdl_index == 0,
        jnp.concatenate([grad_bias_own, grad_bias_other], axis=1),
        jnp.concatenate([grad_bias_other, grad_bias_own], axis=1),
    )
    leader = ((dat_index == 0) & (mdl_index == 0)).astype(f32)
    small = jnp.concatenate(
        [
            jnp.stack([grad_gain_one, grad_gain_two, grad_gain_three]).reshape(-1),
            grad_bias_all.reshape(-1),
            (loss_part * leader).reshape(1),
        ]
    )
    used = small.shape[0]
    small = after(jnp.pad(small, (0, -used % (8 * LANES))).reshape(-1, LANES), total_rest)
    small = sum_all(small, ("dat", "mdl"), "grp", (dat_size, mdl_size, grp_size)).reshape(-1)
    grad_gains = small[: 3 * width].reshape(3, width)
    grad_bias = lax.dynamic_slice_in_dim(
        small[3 * width : used - 1].reshape(BUCKETS, -1), mdl_index * bias_table.shape[1], bias_table.shape[1], axis=1
    )
    loss_total = small[used - 1]

    outgoing = after(outgoing, part_ffn)
    own_rows = lax.all_to_all(outgoing, "dat", split_axis=0, concat_axis=0, tiled=True)
    own_rows = own_rows.reshape(dat_size * pair_rows, 2 * features)
    by_group = arrivals(grp_size)
    moving = [[own_rows], [own_rows]]

    def move(hop, *waits):
        senders = range(hop - 1, grp_size - 1)
        upward = [(group, group + 1) for group in senders]
        downward = [(grp_size - 1 - group, grp_size - 2 - group) for group in senders]
        if {group for group, _ in upward} & {group for group, _ in downward}:
            for way, pairs in enumerate((upward, downward)):
                moving[way].append(lax.ppermute(after(moving[way][-1], *waits), "grp", pairs))
        else:
            rising = group_index >= hop - 1
            moved = lax.ppermute(after(jnp.where(rising, moving[0][-1], moving[1][-1]), *waits), "grp", upward + downward)
            moving[0].append(moved)
            moving[1].append(moved)

    def arrived(place):
        chosen = None
        for way, hop in sorted({found[place][1:] for found in by_group}):
            hit = jnp.any(jnp.array([found[place][1:] == (way, hop) for found in by_group])[group_index])
            chosen = moving[way][hop] if chosen is None else jnp.where(hit, moving[way][hop], chosen)
        return chosen, jnp.array([found[place][0] for found in by_group], jnp.int32)[group_index]

    def ids_of(table, group):
        return lax.dynamic_index_in_dim(table, group, 0, keepdims=False)

    def both_rows(part, group):
        return (
            jnp.concatenate([part, swap_cores(part)], axis=0),
            jnp.concatenate([ids_of(core_ids, group), ids_of(other_ids, group)], axis=0),
        )

    early = [(own_rows, group_index)]
    move(1)
    for hop in range(2, grp_size - 1):
        early.append(arrived(hop - 2))
        move(hop, small, early[-1][0])
    own_table = scatter_rows(
        after(jnp.concatenate([part for part, _ in early], axis=0), part_rest, small),
        jnp.concatenate([ids_of(core_ids, group) for _, group in early], axis=0),
        vocab,
        features,
    )
    other_table = swap_cores(after(own_table, *[ways[-1] for ways in moving]))
    late_part, late_group = arrived(grp_size - 3)
    move(grp_size - 1, own_table, late_part)
    late_rows, late_ids = both_rows(late_part, late_group)
    late_table = scatter_rows(late_rows, late_ids, vocab, features)
    last_part, last_group = arrived(grp_size - 2)
    last_rows, last_ids = both_rows(after(last_part, late_table), last_group)
    full_ffn, full_rest = lax.psum((after(part_ffn, moving[0][-1], moving[1][-1]), part_rest), "grp")

    table_momentum, table_variance, table_direction, table_squares = finish(
        last_rows,
        last_ids,
        embedding,
        embedding_first,
        embedding_second,
        (own_table, other_table, late_table),
    )
    full_ffn, full_rest = after(full_ffn, table_squares), after(full_rest, table_squares)
    half = total_down.shape[1]
    grad_down, grad_up = full_ffn[:, :half].astype(f32), full_ffn[:, half:].astype(f32)
    half = total_qkv.shape[1]
    grad_qkv = full_rest[:, :half].astype(f32).reshape(qkv_weight.shape)
    grad_out = full_rest[:, half:].astype(f32).T

    weights = (qkv_weight, out_weight, up_weight, down_weight, bias_table, norm_gains)
    gradients = (grad_qkv, grad_out, grad_up, grad_down, grad_bias, grad_gains)
    moments = (
        (qkv_first, qkv_second),
        (out_first, out_second),
        (up_first, up_second),
        (down_first, down_second),
        (bias_first, bias_second),
        (gains_first, gains_second),
    )
    results = [
        lamb_direction(weight, gradient, states[0], states[1])
        for weight, gradient, states in zip(weights, gradients, moments)
    ]
    first_mdl = (mdl_index == 0).astype(f32)
    first_dat = (dat_index == 0).astype(f32)
    holder_mask = [1.0, 1.0, 1.0, 1.0, first_dat]
    square_rows = [jnp.stack([first_mdl, first_mdl])] + [
        jnp.stack(
            [
                jnp.sum(weights[position] * weights[position]),
                jnp.sum(results[position][2] * results[position][2]),
            ]
        )
        * holder_mask[position]
        for position in range(5)
    ]
    gain_rows = jnp.stack(
        [jnp.sum(norm_gains * norm_gains, axis=1), jnp.sum(results[5][2] * results[5][2], axis=1)],
        axis=1,
    ) * (first_mdl * first_dat)
    square_table = jnp.concatenate([jnp.stack(square_rows), gain_rows], axis=0)
    square_table = jnp.pad(square_table, ((0, 16 - square_table.shape[0]), (0, LANES - 2)))
    squares = sum_over(table_squares, square_table, ("dat", "mdl"), (dat_size, mdl_size))
    matrix_norms = jnp.sqrt(squares[:9, :2])
    rates = LEARN_RATE * matrix_norms[:, 0] / matrix_norms[:, 1]
    updated = [weights[position] - rates[position + 1] * results[position][2] for position in range(5)]
    updated.append(norm_gains - rates[6:, None] * results[5][2])
    outputs = [
        jnp.stack([loss_total, live_total]),
        matrix_norms,
        table_momentum,
        table_variance,
        table_update(squares, embedding, table_direction),
    ]
    for position in range(6):
        outputs.extend([results[position][0], results[position][1], updated[position]])
    return tuple(outputs)


def solution(mesh):
    state = [
        P("dat", None),
        P("dat", None, "mdl"),
        P("mdl", "dat"),
        P("dat", "mdl"),
        P("dat", "mdl"),
        P(None, "mdl"),
        P(),
    ]
    placed = [P(("grp", "dat"), None), P(("grp", "dat")), P(("grp", "dat")), P(), P(("grp", "dat"))]
    placed += state + [spec for spec in state for _ in range(2)]
    return jax.shard_map(
        shards,
        mesh=mesh,
        in_specs=tuple(placed),
        out_specs=(P(), P(), *[spec for spec in state for _ in range(3)]),
        check_vma=False,
    )
```

```python
import functools

import jax
import jax.numpy as jnp
from jax import lax
from jax.experimental import pallas as pl
from jax.experimental.pallas import tpu as pltpu
from jax.sharding import PartitionSpec as P

HEADS = 12
HEAD = 64
BUCKETS = 32
STEP = 10


SOFTMAX_WARMTH = 0.01
NORM_EPS = 1e-06
BUCKET_EDGES = (12, 16, 23, 32, 46, 64, 91)
BETA_ONE = 0.9
BETA_TWO = 0.999
ADAM_EPS = 1e-06
WEIGHT_DECAY = 0.01
LEARN_RATE = 0.5
MASK_FILL = -1000000000.0
MAX_PRECISION = lax.Precision.HIGHEST
LANES = 128
bf = jnp.bfloat16
f32 = jnp.float32


BLOCK = 128
NT = (((1,), (1,)), ((), ()))
TN = (((0,), (0,)), ((), ()))


def toeplitz(line, rows):
    out = line
    size = 1
    while size < rows:
        out = jnp.concatenate([out, pltpu.roll(out, size, 1)], axis=0)
        size *= 2
    return out


def diagonal_sums(square):
    rows, width = square.shape
    while rows > 8:
        rows //= 2
        square = square[:rows] + pltpu.roll(square[rows:], width - rows, 1)
    for shift in (4, 2, 1):
        square = square + pltpu.roll(pltpu.roll(square, width - shift, 1), 8 - shift, 0)
    return square[:1]


def head_halves(pair):
    first = lax.broadcasted_iota(jnp.int32, (1, LANES), 1) < HEAD
    return jnp.where(first, pair, 0), jnp.where(first, 0, pair)


def attend_kernel(pairs, scale, lens_ref, line_ref, qkv_ref, mixed_ref, lse_ref, scores, probs):
    items, length, _ = mixed_ref.shape
    blocks = length // BLOCK
    first = lax.broadcasted_iota(jnp.int32, (1, LANES), 1) < HEAD
    key = lax.broadcasted_iota(jnp.int32, (BLOCK, 1), 0)

    def one_pair(pair, carry):
        at = lambda part: pl.ds(pl.multiple_of((part * pairs + pair) * LANES, LANES), LANES)
        biases = [toeplitz(line_ref[pl.ds(2 * pair + head, 1), :], BLOCK) for head in range(2)]
        for item in range(items):
            keys = qkv_ref[item, :, at(1)]
            values = qkv_ref[item, :, at(2)]
            mixed = []
            for head, queries in enumerate(head_halves(qkv_ref[item, :, at(0)] * scale)):
                top = jnp.full((1, length), MASK_FILL, f32)
                for block in range(blocks):
                    rows = slice(block * BLOCK, (block + 1) * BLOCK)
                    low = length - block * BLOCK
                    part = lax.dot_general(keys[rows], queries, NT, preferred_element_type=f32)
                    part = part + biases[head][:, low : low + length]
                    part = jnp.where(key < lens_ref[item] - block * BLOCK, part, MASK_FILL)
                    scores[head, rows, :] = part
                    top = jnp.maximum(top, jnp.max(part, axis=0, keepdims=True))
                whole = jnp.zeros((1, length), f32)
                for block in range(blocks):
                    rows = slice(block * BLOCK, (block + 1) * BLOCK)
                    part = jnp.exp(scores[head, rows, :] - top)
                    scores[head, rows, :] = part
                    whole += jnp.sum(part, axis=0, keepdims=True)
                share = 1.0 / whole
                for block in range(blocks):
                    rows = slice(block * BLOCK, (block + 1) * BLOCK)
                    probs[head, rows, :] = (scores[head, rows, :] * share).astype(bf)
                lse_ref[pl.ds(2 * pair + head, 1), item * length : (item + 1) * length] = top + jnp.log(whole)
                mixed.append(lax.dot_general(probs[head], values, TN, preferred_element_type=f32))
            mixed_ref[item, :, at(0)] = jnp.where(first, mixed[0], mixed[1]).astype(bf)
        return carry

    lax.fori_loop(0, pairs, one_pair, 0)


def attend(qkv, lines, lengths):
    items, length, width = qkv.shape
    width //= 3
    pairs = width // LANES
    vm = pl.BlockSpec(memory_space=pltpu.VMEM)
    return pl.pallas_call(
        functools.partial(attend_kernel, pairs, HEAD**-0.5),
        in_specs=[pl.BlockSpec(memory_space=pltpu.SMEM), vm, vm],
        out_specs=[vm, vm],
        out_shape=[
            jax.ShapeDtypeStruct((items, length, width), bf),
            jax.ShapeDtypeStruct((2 * pairs, items * length), f32),
        ],
        scratch_shapes=[pltpu.VMEM((2, length, length), f32), pltpu.VMEM((2, length, length), bf)],
        compiler_params=pltpu.CompilerParams(vmem_limit_bytes=40 * 2**20),
        cost_estimate=pl.CostEstimate(
            flops=8 * items * length * length * width,
            bytes_accessed=items * length * width * 12,
            transcendentals=items * length * length * width // HEAD,
        ),
        name="attend",
    )(lengths, lines, qkv)


def attend_back_kernel(
    pairs, scale, lens_ref, line_ref, qkv_ref, lse_ref, dmix_ref, dqkv_ref, dline_ref, probs, dprobs, low, diag
):
    items, length, _ = dmix_ref.shape
    blocks = length // BLOCK
    first = lax.broadcasted_iota(jnp.int32, (1, LANES), 1) < HEAD
    key = lax.broadcasted_iota(jnp.int32, (BLOCK, 1), 0)

    def one_pair(pair, carry):
        at = lambda part: pl.ds(pl.multiple_of((part * pairs + pair) * LANES, LANES), LANES)
        biases = [toeplitz(line_ref[pl.ds(2 * pair + head, 1), :], BLOCK) for head in range(2)]
        diag[...] = jnp.zeros_like(diag)
        for item in range(items):
            keys = qkv_ref[item, :, at(1)]
            values = qkv_ref[item, :, at(2)]
            queries = qkv_ref[item, :, at(0)] * scale
            given = dmix_ref[item, :, at(0)]
            dquery, dkeys, dvals = [], [], []
            for head, (mine, pulled) in enumerate(zip(head_halves(queries), head_halves(given))):
                stats = lse_ref[pl.ds(2 * pair + head, 1), item * length : (item + 1) * length]
                inner = jnp.zeros((1, length), f32)
                for block in range(blocks):
                    rows = slice(block * BLOCK, (block + 1) * BLOCK)
                    start = length - block * BLOCK
                    part = lax.dot_general(keys[rows], mine, NT, preferred_element_type=f32)
                    part = jnp.exp(part + biases[head][:, start : start + length] - stats)
                    part = jnp.where(key < lens_ref[item] - block * BLOCK, part, 0.0)
                    back = lax.dot_general(values[rows], pulled, NT, preferred_element_type=f32)
                    probs[head, rows, :] = part
                    dprobs[head, rows, :] = back
                    low[head, rows, :] = part.astype(bf)
                    inner += jnp.sum(part * back, axis=0, keepdims=True)
                dvals.append(jnp.dot(low[head], given, preferred_element_type=f32))
                for block in range(blocks):
                    rows = slice(block * BLOCK, (block + 1) * BLOCK)
                    start = length - block * BLOCK
                    part = probs[head, rows, :] * (dprobs[head, rows, :] - inner)
                    diag[head, :, start : start + length] += part
                    low[head, rows, :] = part.astype(bf)
                dkeys.append(jnp.dot(low[head], queries, preferred_element_type=f32))
                dquery.append(lax.dot_general(low[head], keys, TN, preferred_element_type=f32))
            dqkv_ref[item, :, at(0)] = (jnp.where(first, dquery[0], dquery[1]) * scale).astype(bf)
            dqkv_ref[item, :, at(1)] = jnp.where(first, dkeys[0], dkeys[1]).astype(bf)
            dqkv_ref[item, :, at(2)] = jnp.where(first, dvals[0], dvals[1]).astype(bf)
        for head in range(2):
            dline_ref[pl.ds(2 * pair + head, 1), :] = diagonal_sums(diag[head])
        return carry

    lax.fori_loop(0, pairs, one_pair, 0)


def attend_back(qkv, lines, lengths, lse, dmixed):
    items, length, width = dmixed.shape
    pairs = width // LANES
    vm = pl.BlockSpec(memory_space=pltpu.VMEM)
    square = (2, length, length)
    return pl.pallas_call(
        functools.partial(attend_back_kernel, pairs, HEAD**-0.5),
        in_specs=[pl.BlockSpec(memory_space=pltpu.SMEM), vm, vm, vm, vm],
        out_specs=[vm, vm],
        out_shape=[jax.ShapeDtypeStruct(qkv.shape, bf), jax.ShapeDtypeStruct(lines.shape, f32)],
        scratch_shapes=[
            pltpu.VMEM(square, f32),
            pltpu.VMEM(square, f32),
            pltpu.VMEM(square, bf),
            pltpu.VMEM((2, BLOCK, 2 * length), f32),
        ],
        compiler_params=pltpu.CompilerParams(vmem_limit_bytes=40 * 2**20),
        cost_estimate=pl.CostEstimate(
            flops=20 * items * length * length * width,
            bytes_accessed=items * length * width * 20,
            transcendentals=items * length * length * width // HEAD,
        ),
        name="attend_back",
    )(lengths, lines, qkv, lse, dmixed)


def split_features(features):
    whole = features // LANES * LANES
    return whole, features - whole


def tile_count(features):
    whole, rest = split_features(features)
    return whole // LANES + (rest > 0)


def first_of_pair(packed, features):
    return packed[..., :features]


def second_of_pair(packed, features):
    whole, rest = split_features(features)
    tail = packed[..., features : features + rest]
    return jnp.concatenate([packed[..., features + rest :], tail], axis=-1) if whole else tail


def pack_pair(first, second):
    whole, _ = split_features(first.shape[-1])
    parts = [first, second[..., whole:], second[..., :whole]] if whole else [first, second]
    return jnp.concatenate(parts, axis=-1)


def packed_starts(features, half):
    whole, rest = split_features(features)
    base = 0 if half == 0 else features + rest
    return [base + low for low in range(0, whole, LANES)] + ([whole] if rest else [])


def gather_kernel(features, load_steps, batch, table_ref, ids_ref, out_ref, *scratch):
    step = pl.program_id(0)
    width = table_ref.shape[1]
    tiles = tile_count(features)
    whole, rest = split_features(features)
    stash = scratch[:tiles]
    rows = [scratch[tiles : 2 * tiles], scratch[2 * tiles :]]

    @pl.when(step < load_steps)
    def _():
        base = pl.multiple_of(step * width, width)
        for tile in range(tiles):
            low = tile * LANES
            part = table_ref[low : min(features, low + LANES), :].astype(bf).astype(f32)
            if low == whole:
                blank = [jnp.zeros((LANES - 2 * rest, width), f32)] if 2 * rest < LANES else []
                part = jnp.concatenate([part, part, *blank], axis=0)
            stash[tile][pl.ds(base, width), :] = part.T

    @pl.when(step >= load_steps)
    def _():
        count = out_ref.shape[0]
        for half in range(2):
            def take(index, carry):
                start = pl.multiple_of(index * batch, batch)
                tokens = [ids_ref[0, half, start + inner] for inner in range(batch)]
                for tile in range(tiles):
                    for inner in range(batch):
                        rows[half][tile][pl.ds(start + inner, 1), :] = stash[tile][pl.ds(tokens[inner], 1), :]
                return carry
            lax.fori_loop(0, count // batch, take, 0)
        for half in range(2):
            for tile in range(whole // LANES):
                low = packed_starts(features, half)[tile]
                out_ref[:, low : low + LANES] = rows[half][tile][...].astype(bf)
        if rest:
            lane = lax.broadcasted_iota(jnp.int32, (1, LANES), 1)
            shared = jnp.where(lane < rest, rows[0][-1][...], rows[1][-1][...]).astype(bf)
            out_ref[:, whole : whole + 2 * rest] = shared[:, : 2 * rest]


def gather_rows(table, ids, width=4096, batch=16):
    features, vocab = table.shape
    steps, _, chunk = ids.shape
    tiles = tile_count(features)
    load_steps = pl.cdiv(vocab, width)
    return pl.pallas_call(
        functools.partial(gather_kernel, features, load_steps, batch),
        grid=(load_steps + steps,),
        in_specs=[
            pl.BlockSpec((features, width), lambda s: (0, jnp.minimum(s, load_steps - 1))),
            pl.BlockSpec((1, 2, chunk), lambda s: (jnp.maximum(s - load_steps, 0), 0, 0), memory_space=pltpu.SMEM),
        ],
        out_specs=pl.BlockSpec((chunk, 2 * features), lambda s: (jnp.maximum(s - load_steps, 0), 0)),
        out_shape=jax.ShapeDtypeStruct((steps * chunk, 2 * features), bf),
        scratch_shapes=[pltpu.VMEM((load_steps * width, LANES), f32)] * tiles + [pltpu.VMEM((chunk, LANES), f32)] * (2 * tiles),
        compiler_params=pltpu.CompilerParams(vmem_limit_bytes=60 * 2**20),
        cost_estimate=pl.CostEstimate(flops=0, bytes_accessed=80 * 2**20, transcendentals=0),
        name="gather_rows",
    )(table, ids)


def stage_ids_kernel(batch, order, place_ref, ids_ref, out_ref, flags_ref, flat):
    lane = lax.broadcasted_iota(jnp.int32, (1, LANES), 1)
    count, _, chunk = ids_ref.shape[2:]
    flat[...] = jnp.zeros_like(flat)
    for at, (slot, other) in enumerate(order):
        core = lax.rem(place_ref[0] + other, ids_ref.shape[0])
        for step in range(count):
            index = at * count + step
            ids = ids_ref[core, place_ref[1 + slot], step]
            out_ref[index] = ids
            flat[2 * index : 2 * index + 2, :] = ids
    flags = jnp.zeros((flat.shape[0], LANES), jnp.int32)
    for block in range(chunk // LANES):
        part = flat[:, block * LANES : (block + 1) * LANES]
        found = jnp.zeros(part.shape, jnp.int32)
        for shift in range(1, batch):
            again = (part == pltpu.roll(part, shift, 1)) & (lane % batch >= shift)
            found = jnp.where(again, 1, found)
        flags = jnp.where(lane == block, jnp.max(found, axis=1, keepdims=True), flags)
    for index in range(out_ref.shape[0]):
        flags_ref[index] = flags[2 * index : 2 * index + 2]


def stage_ids(place, ids, order, batch=8):
    *_, count, _, chunk = ids.shape
    vm = pl.BlockSpec(memory_space=pltpu.VMEM)
    total = len(order) * count
    return pl.pallas_call(
        functools.partial(stage_ids_kernel, batch, order),
        in_specs=[pl.BlockSpec(memory_space=pltpu.SMEM), vm],
        out_specs=[vm, vm],
        out_shape=[
            jax.ShapeDtypeStruct((total, 2, chunk), jnp.int32),
            jax.ShapeDtypeStruct((total, 2, LANES), jnp.int32),
        ],
        scratch_shapes=[pltpu.VMEM((2 * total + -2 * total % 8, chunk), jnp.int32)],
        name="stage_ids",
    )(place, ids)


def spread_rows(features, rows_ref, summed):
    whole, rest = split_features(features)
    lane = lax.broadcasted_iota(jnp.int32, (1, LANES), 1)
    for half in range(2):
        for tile, start in enumerate(packed_starts(features, half)):
            if start == whole:
                part = rows_ref[:, start : start + 2 * rest].astype(f32)
                if 2 * rest < LANES:
                    part = jnp.concatenate([part, jnp.zeros((part.shape[0], LANES - 2 * rest), f32)], axis=1)
                mine = lane < rest if half == 0 else (lane >= rest) & (lane < 2 * rest)
                part = jnp.where(mine, part, 0.0)
            else:
                part = rows_ref[:, start : start + LANES].astype(f32)
            summed[half][tile][...] = part


def merge_rows(batch, ids_row_ref, flags_ref, summed):
    count = summed[0][0].shape[0]
    for half in range(2):
        for at in range(count // LANES):
            block = slice(at * LANES, (at + 1) * LANES)

            @pl.when(flags_ref[0, half, at] > 0)
            def _():
                place = lax.broadcasted_iota(jnp.int32, (LANES, LANES), 0) // batch
                same_batch = place == lax.broadcasted_iota(jnp.int32, (LANES, LANES), 1) // batch
                across = jnp.broadcast_to(ids_row_ref[0, half : half + 1, block], (LANES, LANES))
                match = jnp.where((across == across.T) & same_batch, 1.0, 0.0).astype(bf)
                for rows in summed[half]:
                    rows[block, :] = jnp.dot(match, rows[block, :].astype(bf), preferred_element_type=f32)


def add_rows(batch, ids_ref, totals, summed):
    count = summed[0][0].shape[0]

    def add(index, carry):
        start = pl.multiple_of(index * batch, batch)
        for half in range(2):
            tokens = [ids_ref[0, half, start + inner] for inner in range(batch)]
            fresh = [
                [total[pl.ds(tokens[inner], 1), :] + rows[pl.ds(start + inner, 1), :] for inner in range(batch)]
                for total, rows in zip(totals, summed[half])
            ]
            for total, new in zip(totals, fresh):
                for inner in range(batch):
                    total[pl.ds(tokens[inner], 1), :] = new[inner]
        return carry

    lax.fori_loop(0, count // batch, add, 0)


def table_columns(features, totals, base, width):
    whole, rest = split_features(features)
    pieces = [total[pl.ds(base, width), :].T for total in totals]
    if rest:
        pieces[-1] = pieces[-1][:rest] + pieces[-1][rest : 2 * rest]
    return pieces


class Stage:
    def __init__(self, segments, choices, ids, flags, first, features):
        self.arrays = [array for candidates in segments for array in candidates]
        self.segments = [len(candidates) for candidates in segments]
        self.chunk = ids.shape[2]
        self.each = segments[0][0].shape[0] // self.chunk
        self.steps = self.each * len(segments)
        self.operands = [choices, ids, ids, flags, *self.arrays]
        at = lambda s: first + jnp.minimum(s, self.steps - 1)
        self.in_specs = [
            pl.BlockSpec(memory_space=pltpu.SMEM),
            pl.BlockSpec((1, 2, self.chunk), lambda s: (at(s), 0, 0), memory_space=pltpu.SMEM),
            pl.BlockSpec((1, 2, self.chunk), lambda s: (at(s), 0, 0)),
            pl.BlockSpec((1, 2, LANES), lambda s: (at(s), 0, 0), memory_space=pltpu.SMEM),
        ]
        for segment, candidates in enumerate(segments):
            for _ in candidates:
                low = segment * self.each
                self.in_specs.append(
                    pl.BlockSpec(
                        (self.chunk, 2 * features), lambda s, low=low: (jnp.clip(s - low, 0, self.each - 1), 0)
                    )
                )
        self.features = features

    def scratch(self, vocab):
        tiles = tile_count(self.features)
        return [pltpu.VMEM((vocab, LANES), f32)] * tiles + [pltpu.VMEM((self.chunk, LANES), f32)] * (2 * tiles)

    def add(self, batch, refs, scratch):
        choice_ref, ids_ref, ids_row_ref, flags_ref, *rows_refs = refs
        step = pl.program_id(0)
        tiles = tile_count(self.features)
        totals = scratch[:tiles]
        summed = [scratch[tiles : 2 * tiles], scratch[2 * tiles :]]

        @pl.when(step == 0)
        def _():
            for total in totals:
                total[...] = jnp.zeros_like(total)

        for segment, candidates in enumerate(self.segments):
            now = (step >= segment * self.each) & (step < (segment + 1) * self.each)
            for candidate in range(candidates):
                rows_ref, rows_refs = rows_refs[0], rows_refs[1:]

                @pl.when(now & (choice_ref[segment] == candidate))
                def _():
                    spread_rows(self.features, rows_ref, summed)

        @pl.when(step < self.steps)
        def _():
            merge_rows(batch, ids_row_ref, flags_ref, summed)
            add_rows(batch, ids_ref, totals, summed)

        return totals


def scatter_kernel(stage, batch, *refs):
    count = len(stage.operands)
    out_ref = refs[count]
    totals = stage.add(batch, refs[:count], refs[count + 1 :])
    step = pl.program_id(0)
    width = out_ref.shape[1]

    @pl.when(step >= stage.steps)
    def _():
        base = pl.multiple_of((step - stage.steps) * width, width)
        low = 0
        for piece in table_columns(stage.features, totals, base, width):
            out_ref[low : low + piece.shape[0], :] = piece.astype(bf)
            low += piece.shape[0]


def scatter_rows(stage, vocab, width=2048, batch=8):
    flush = pl.cdiv(vocab, width)
    return pl.pallas_call(
        functools.partial(scatter_kernel, stage, batch),
        grid=(stage.steps + flush,),
        in_specs=stage.in_specs,
        out_specs=pl.BlockSpec((stage.features, width), lambda s: (0, jnp.maximum(s - stage.steps, 0))),
        out_shape=jax.ShapeDtypeStruct((stage.features, vocab), bf),
        scratch_shapes=stage.scratch(flush * width),
        compiler_params=pltpu.CompilerParams(vmem_limit_bytes=127 * 2**19),
        cost_estimate=pl.CostEstimate(flops=0, bytes_accessed=100 * 2**20, transcendentals=0),
        name="scatter_rows",
    )(*stage.operands)


def assemble_kernel(features, spread_ref, gain_ref, embedded_ref, normed_ref):
    for half, take in enumerate((first_of_pair, second_of_pair)):
        row = jnp.concatenate([take(spread_ref[part], features) for part in range(spread_ref.shape[0])], axis=1)
        embedded_ref[half] = row
        stream = row.astype(f32)
        scale = lax.rsqrt(jnp.mean(stream * stream, axis=1, keepdims=True) + NORM_EPS)
        normed_ref[half] = (stream * scale * gain_ref[...]).astype(bf)


def assemble(spread, gain, block=128):
    parts, count, features = spread.shape
    features //= 2
    width = parts * features
    block = min(block, count)
    out = jax.ShapeDtypeStruct((2, count, width), bf)
    whole_block = pl.BlockSpec((2, block, width), lambda s: (0, s, 0))
    embedded, normed = pl.pallas_call(
        functools.partial(assemble_kernel, features),
        grid=(count // block,),
        in_specs=[
            pl.BlockSpec((parts, block, 2 * features), lambda s: (0, s, 0)),
            pl.BlockSpec((1, width), lambda s: (0, 0)),
        ],
        out_specs=[whole_block, whole_block],
        out_shape=[out, out],
        compiler_params=pltpu.CompilerParams(vmem_limit_bytes=30 * 2**20),
        name="assemble",
    )(spread, gain.reshape(1, width))
    return embedded.reshape(2 * count, width), normed.reshape(2 * count, width)


def pack_back_kernel(features, back_ref, embedded_ref, passed_ref, gain_ref, packed_ref, grad_gain_ref):
    gain = gain_ref[...]
    halves = []
    grad_gain = jnp.zeros_like(gain)
    for half in range(2):
        stream = embedded_ref[half].astype(f32)
        back = back_ref[half]
        scale = lax.rsqrt(jnp.mean(stream * stream, axis=1, keepdims=True) + NORM_EPS)
        unit = stream * scale
        grad_gain += jnp.sum(back * unit, axis=0, keepdims=True)
        pulled = back * gain
        along = jnp.mean(pulled * unit, axis=1, keepdims=True)
        halves.append((passed_ref[half] + scale * (pulled - unit * along)).astype(bf))
    for part in range(packed_ref.shape[0]):
        cut = slice(part * features, (part + 1) * features)
        packed_ref[part] = pack_pair(halves[0][:, cut], halves[1][:, cut])

    @pl.when(pl.program_id(0) == 0)
    def _():
        grad_gain_ref[...] = jnp.zeros_like(grad_gain_ref)

    grad_gain_ref[...] += grad_gain


def pack_back(back, embedded, passed, gain, features, block=128):
    rows, width = back.shape
    count, parts = rows // 2, width // features
    block = min(block, count)
    pair = pl.BlockSpec((2, block, width), lambda s: (0, s, 0))
    line = pl.BlockSpec((1, width), lambda s: (0, 0))
    packed, grad_gain = pl.pallas_call(
        functools.partial(pack_back_kernel, features),
        grid=(count // block,),
        in_specs=[pair, pair, pair, line],
        out_specs=[pl.BlockSpec((parts, block, 2 * features), lambda s: (0, s, 0)), line],
        out_shape=[jax.ShapeDtypeStruct((parts, count, 2 * features), bf), jax.ShapeDtypeStruct((1, width), f32)],
        compiler_params=pltpu.CompilerParams(vmem_limit_bytes=30 * 2**20),
        name="pack_back",
    )(back.reshape(2, count, width), embedded.reshape(2, count, width), passed.reshape(2, count, width), gain.reshape(1, width))
    return packed, grad_gain[0]


def finish_kernel(stage, vocab, batch, *refs):
    count = len(stage.operands)
    weight_ref, first_ref, second_ref, *dense_refs = refs[count : count + 6]
    momentum_ref, variance_ref, direction_ref, squares_ref = refs[count + 6 : count + 10]
    totals = stage.add(batch, refs[:count], refs[count + 10 :])
    step = pl.program_id(0)

    @pl.when(step == 0)
    def _():
        squares_ref[...] = jnp.zeros_like(squares_ref)

    @pl.when(step >= stage.steps)
    def _():
        width = weight_ref.shape[1]
        base = pl.multiple_of((step - stage.steps) * width, width)
        inside = base + lax.broadcasted_iota(jnp.int32, (1, width), 1) < vocab
        low = 0
        for piece in table_columns(stage.features, totals, base, width):
            cut = slice(low, low + piece.shape[0])
            low += piece.shape[0]
            weight = weight_ref[cut, :]
            gradient = piece
            for dense_ref in dense_refs:
                gradient = gradient + dense_ref[cut, :].astype(f32)
            momentum, variance, direction = lamb_direction(weight, gradient, first_ref[cut, :], second_ref[cut, :])
            momentum_ref[cut, :] = momentum
            variance_ref[cut, :] = variance
            direction_ref[cut, :] = direction.astype(bf)
            for line, value in enumerate((weight, direction)):
                value = jnp.where(inside, value, 0.0)
                squares_ref[line : line + 1, :] += jnp.sum(value * value, axis=0, keepdims=True)


def finish(stage, weight, first, second, dense, width=1024, batch=8):
    features, vocab = weight.shape
    columns = pl.cdiv(vocab, width)
    block = pl.BlockSpec((features, width), lambda s: (0, jnp.maximum(s - stage.steps, 0)))
    full = jax.ShapeDtypeStruct(weight.shape, f32)
    return pl.pallas_call(
        functools.partial(finish_kernel, stage, vocab, batch),
        grid=(stage.steps + columns,),
        in_specs=stage.in_specs + [block] * 6,
        out_specs=[block, block, block, pl.BlockSpec((8, width), lambda s: (0, 0))],
        out_shape=[full, full, jax.ShapeDtypeStruct(weight.shape, bf), jax.ShapeDtypeStruct((8, width), f32)],
        scratch_shapes=stage.scratch(columns * width),
        compiler_params=pltpu.CompilerParams(vmem_limit_bytes=127 * 2**19),
        cost_estimate=pl.CostEstimate(flops=0, bytes_accessed=300 * 2**20, transcendentals=0),
        name="finish",
    )(*stage.operands, weight, first, second, *dense)


MESH = pl.DeviceIdType.MESH


def exchange(value_ref, out_ref, mine, peers, send, received, slot):
    copies = []
    for peer in peers:
        copy = pltpu.make_async_remote_copy(
            src_ref=value_ref,
            dst_ref=out_ref.at[mine],
            send_sem=send.at[slot],
            recv_sem=received.at[slot],
            device_id=peer,
            device_id_type=MESH,
        )
        copy.start()
        copies.append(copy)
        slot += 1
    return copies


def line_peers(axis):
    place, size = lax.axis_index(axis), lax.axis_size(axis)
    return place, [{axis: lax.rem(place + step, size)} for step in range(1, size)]


def plane_peers(axes):
    places = [lax.axis_index(axis) for axis in axes]
    sizes = [lax.axis_size(axis) for axis in axes]
    count = sizes[0] * sizes[1]
    mine = places[0] * sizes[1] + places[1]
    peers = []
    for step in range(1, count):
        peer = lax.rem(mine + step, count)
        peers.append({axes[0]: peer // sizes[1], axes[1]: lax.rem(peer, sizes[1])})
    return mine, peers


def greet(peers):
    barrier = pltpu.get_barrier_semaphore()
    for peer in peers:
        pl.semaphore_signal(barrier, inc=1, device_id=peer, device_id_type=MESH)
    pl.semaphore_wait(barrier, len(peers))


def share_kernel(axis, value_ref, out_ref, send, received):
    mine, peers = line_peers(axis)
    greet(peers)
    out_ref[mine] = value_ref[...]
    for copy in exchange(value_ref, out_ref, mine, peers, send, received, 0):
        copy.wait()


def share(value, axis, size):
    return pl.pallas_call(
        functools.partial(share_kernel, axis),
        in_specs=[pl.BlockSpec(memory_space=pltpu.VMEM)],
        out_specs=pl.BlockSpec(memory_space=pltpu.VMEM),
        out_shape=jax.ShapeDtypeStruct((size, *value.shape), value.dtype),
        scratch_shapes=[pltpu.SemaphoreType.DMA((size - 1,)), pltpu.SemaphoreType.DMA((size - 1,))],
        compiler_params=pltpu.CompilerParams(collective_id=0, has_side_effects=True),
        name="share",
    )(value)


def sum_squares_kernel(axes, rows_ref, table_ref, out_ref, slots, send, received):
    places = [lax.axis_index(axis) for axis in axes]
    sizes = [lax.axis_size(axis) for axis in axes]
    count = sizes[0] * sizes[1]
    mine = places[0] * sizes[1] + places[1]
    barrier = pltpu.get_barrier_semaphore()
    peers = []
    for step in range(1, count):
        peer = lax.rem(mine + step, count)
        peers.append({axes[0]: peer // sizes[1], axes[1]: lax.rem(peer, sizes[1])})
    for peer in peers:
        pl.semaphore_signal(barrier, inc=1, device_id=peer, device_id_type=MESH)
    pl.semaphore_wait(barrier, count - 1)
    lane = lax.broadcasted_iota(jnp.int32, (1, LANES), 1)
    sums = jnp.sum(rows_ref[...], axis=1, keepdims=True)
    slots[mine] = table_ref[...]
    slots[mine, 0:1, :] = jnp.where(lane == 0, sums[0:1], jnp.where(lane == 1, sums[1:2], 0.0)) * table_ref[0:1, :]
    copies = []
    for step, peer in enumerate(peers):
        copy = pltpu.make_async_remote_copy(
            src_ref=slots.at[mine],
            dst_ref=slots.at[mine],
            send_sem=send.at[step],
            recv_sem=received.at[step],
            device_id=peer,
            device_id_type=MESH,
        )
        copy.start()
        copies.append(copy)
    for copy in copies:
        copy.wait()
    total = slots[0]
    for other in range(1, count):
        total = total + slots[other]
    out_ref[...] = total


def sum_over(rows, table, axes, sizes):
    count = sizes[0] * sizes[1]
    return pl.pallas_call(
        functools.partial(sum_squares_kernel, axes),
        in_specs=[pl.BlockSpec(memory_space=pltpu.VMEM)] * 2,
        out_specs=pl.BlockSpec(memory_space=pltpu.VMEM),
        out_shape=jax.ShapeDtypeStruct(table.shape, f32),
        scratch_shapes=[
            pltpu.VMEM((count, *table.shape), f32),
            pltpu.SemaphoreType.DMA((count - 1,)),
            pltpu.SemaphoreType.DMA((count - 1,)),
        ],
        compiler_params=pltpu.CompilerParams(collective_id=1, has_side_effects=True),
        name="sum_over",
    )(rows, table)


def sum_all_kernel(near, far, value_ref, out_ref, near_slots, far_slots, send, received):
    places = [lax.axis_index(axis) for axis in (*near, far)]
    sizes = [lax.axis_size(axis) for axis in (*near, far)]
    count = sizes[0] * sizes[1]
    mine = places[0] * sizes[1] + places[1]
    barrier = pltpu.get_barrier_semaphore()
    plane, line = [], []
    for step in range(1, count):
        peer = lax.rem(mine + step, count)
        plane.append({near[0]: peer // sizes[1], near[1]: lax.rem(peer, sizes[1])})
    for step in range(1, sizes[2]):
        line.append({far: lax.rem(places[2] + step, sizes[2])})
    for peer in plane + line:
        pl.semaphore_signal(barrier, inc=1, device_id=peer, device_id_type=MESH)
    pl.semaphore_wait(barrier, len(plane) + len(line))
    slot = 0
    value = value_ref[...]
    for peers, slots, at in ((plane, near_slots, mine), (line, far_slots, places[2])):
        slots[at] = value
        copies = []
        for peer in peers:
            copy = pltpu.make_async_remote_copy(
                src_ref=slots.at[at],
                dst_ref=slots.at[at],
                send_sem=send.at[slot],
                recv_sem=received.at[slot],
                device_id=peer,
                device_id_type=MESH,
            )
            copy.start()
            copies.append(copy)
            slot += 1
        for copy in copies:
            copy.wait()
        value = slots[0]
        for other in range(1, slots.shape[0]):
            value = value + slots[other]
    out_ref[...] = value


def sum_all(value, near, far, sizes):
    count = sizes[0] * sizes[1]
    slots = count - 1 + sizes[2] - 1
    return pl.pallas_call(
        functools.partial(sum_all_kernel, near, far),
        in_specs=[pl.BlockSpec(memory_space=pltpu.VMEM)],
        out_specs=pl.BlockSpec(memory_space=pltpu.VMEM),
        out_shape=jax.ShapeDtypeStruct(value.shape, f32),
        scratch_shapes=[
            pltpu.VMEM((count, *value.shape), f32),
            pltpu.VMEM((sizes[2], *value.shape), f32),
            pltpu.SemaphoreType.DMA((slots,)),
            pltpu.SemaphoreType.DMA((slots,)),
        ],
        compiler_params=pltpu.CompilerParams(collective_id=2, has_side_effects=True),
        name="sum_all",
    )(value)


def share_both_kernel(plane, line, vectors_ref, ids_ref, all_vectors_ref, all_ids_ref, send, received):
    mine, near = plane_peers(plane)
    place, far = line_peers(line)
    greet(near + far)
    all_vectors_ref[mine] = vectors_ref[...]
    all_ids_ref[place] = ids_ref[...]
    copies = exchange(vectors_ref, all_vectors_ref, mine, near, send, received, 0)
    copies += exchange(ids_ref, all_ids_ref, place, far, send, received, len(near))
    for copy in copies:
        copy.wait()


def share_both(vectors, ids, plane, line, sizes):
    count = sizes[0] * sizes[1]
    slots = count - 1 + sizes[2] - 1
    vm = pl.BlockSpec(memory_space=pltpu.VMEM)
    return pl.pallas_call(
        functools.partial(share_both_kernel, plane, line),
        in_specs=[vm, vm],
        out_specs=[vm, vm],
        out_shape=[
            jax.ShapeDtypeStruct((count, *vectors.shape), vectors.dtype),
            jax.ShapeDtypeStruct((sizes[2], *ids.shape), ids.dtype),
        ],
        scratch_shapes=[pltpu.SemaphoreType.DMA((slots,)), pltpu.SemaphoreType.DMA((slots,))],
        compiler_params=pltpu.CompilerParams(collective_id=3, has_side_effects=True),
        name="share_both",
    )(vectors, ids)


def lamb_direction(weight, gradient, moment_one, moment_two):
    momentum = BETA_ONE * moment_one + (1.0 - BETA_ONE) * gradient
    variance = BETA_TWO * moment_two + (1.0 - BETA_TWO) * gradient * gradient
    direction = (
        momentum / (1.0 - BETA_ONE**STEP) / (jnp.sqrt(variance / (1.0 - BETA_TWO**STEP)) + ADAM_EPS)
        + WEIGHT_DECAY * weight
    )
    return (momentum, variance, direction)


def total_of(value):
    while value.ndim > 2:
        value = jnp.sum(value, axis=1)
    return jnp.sum(jnp.sum(value, axis=1, keepdims=True), axis=0, keepdims=True)


def small_moments_kernel(mask_ref, ffn_ref, rest_ref, *refs):
    grad_refs, inputs, outputs, squares_ref = refs[:2], refs[2:20], refs[20:-1], refs[-1]
    parts, _, width = inputs[0].shape
    half = ffn_ref.shape[1] // 2
    gradient_of = (
        lambda: jnp.stack([rest_ref[:, part * width : (part + 1) * width] for part in range(parts)]),
        lambda: rest_ref[:, parts * width :],
        lambda: ffn_ref[:, half:],
        lambda: ffn_ref[:, :half],
        lambda: grad_refs[0][...],
        lambda: grad_refs[1][...],
    )
    lane = lax.broadcasted_iota(jnp.int32, (1, LANES), 1)

    @pl.when(pl.program_id(0) == 0)
    def _():
        squares_ref[...] = jnp.zeros_like(squares_ref)
        squares_ref[0:1, :] = mask_ref[0:1, :]

    def update(place):
        weight_ref, first_ref, second_ref = inputs[3 * place : 3 * place + 3]
        weight = weight_ref[...]
        results = lamb_direction(weight, gradient_of[place]().astype(f32), first_ref[...], second_ref[...])
        for ref, value in zip(outputs[3 * place : 3 * place + 3], results):
            ref[...] = value
        return weight * weight, results[2] * results[2]

    def add(line, weight_square, direction_square):
        both = jnp.where(lane == 0, weight_square, jnp.where(lane == 1, direction_square, 0.0))
        squares_ref[line : line + 1, :] += both * mask_ref[line : line + 1, :]

    for place in range(4):
        weight_square, direction_square = update(place)
        add(place + 1, total_of(weight_square), total_of(direction_square))

    @pl.when(pl.program_id(0) == 0)
    def _():
        weight_square, direction_square = update(4)
        add(5, total_of(weight_square), total_of(direction_square))
        weight_square, direction_square = update(5)
        for row in range(weight_square.shape[0]):
            add(6 + row, total_of(weight_square[row : row + 1]), total_of(direction_square[row : row + 1]))


def row_block(value, steps):
    if value.ndim == 3:
        return pl.BlockSpec((value.shape[0], value.shape[1] // steps, value.shape[2]), lambda s: (0, s, 0))
    return pl.BlockSpec((value.shape[0] // steps, value.shape[1]), lambda s: (s, 0))


def whole_block(value):
    return pl.BlockSpec(value.shape, lambda s: (0,) * value.ndim)


def small_moments(mask, weights, gradients, moments, steps):
    operands = [mask, *gradients]
    in_specs = [whole_block(mask)] + [row_block(value, steps) for value in operands[1:3]]
    in_specs += [whole_block(value) for value in operands[3:]]
    out_specs, out_shape = [], []
    for place, (weight, states) in enumerate(zip(weights, moments)):
        spec = row_block(weight, steps) if place < 4 else whole_block(weight)
        operands += [weight, *states]
        in_specs += [spec] * 3
        out_specs += [spec] * 3
        out_shape += [jax.ShapeDtypeStruct(weight.shape, f32)] * 3
    return pl.pallas_call(
        small_moments_kernel,
        grid=(steps,),
        in_specs=in_specs,
        out_specs=out_specs + [whole_block(mask)],
        out_shape=out_shape + [jax.ShapeDtypeStruct(mask.shape, f32)],
        compiler_params=pltpu.CompilerParams(vmem_limit_bytes=127 * 2**19),
        name="small_moments",
    )(*operands)


def update_all_kernel(squares_ref, *refs):
    norms = jnp.sqrt(squares_ref[...])
    rates = LEARN_RATE * norms[:, 0:1] / norms[:, 1:2]
    count = len(refs) // 3
    for place in range(count):
        weight_ref, direction_ref, updated_ref = refs[2 * place], refs[2 * place + 1], refs[2 * count + place]
        rate = rates[6:9] if place == 6 else rates[place : place + 1]
        weight = weight_ref[...]
        if weight.ndim == 3:
            rate = rate[:, :, None]
        updated_ref[...] = weight - rate * direction_ref[...].astype(f32)


def update_all(squares, weights, directions, steps):
    operands, in_specs, out_specs, out_shape = [squares], [whole_block(squares)], [], []
    for place, (weight, direction) in enumerate(zip(weights, directions)):
        spec = row_block(weight, steps) if place < 5 else whole_block(weight)
        operands += [weight, direction]
        in_specs += [spec] * 2
        out_specs += [spec]
        out_shape += [jax.ShapeDtypeStruct(weight.shape, f32)]
    return pl.pallas_call(
        update_all_kernel,
        grid=(steps,),
        in_specs=in_specs,
        out_specs=out_specs,
        out_shape=out_shape,
        compiler_params=pltpu.CompilerParams(vmem_limit_bytes=127 * 2**19),
        name="update_all",
    )(*operands)


def norm_scale(stream, gain_row):
    return (
        stream * lax.rsqrt(jnp.mean(stream * stream, axis=-1, keepdims=True) + NORM_EPS) * gain_row
    )


def gelu_tanh(pre_act):
    return jax.nn.gelu(pre_act, approximate=True)


def dot(left, right, dims=((1,), (0,))):
    return lax.dot_general(left, right, (dims, ((), ())), preferred_element_type=f32)


def bucket_onehot(length):
    relative = length - jnp.arange(2 * length, dtype=jnp.int32)
    distance = jnp.abs(relative)
    far_bucket = 8 + sum(((distance >= threshold).astype(jnp.int32) for threshold in BUCKET_EDGES))
    bucket = jnp.where(distance < 8, distance, far_bucket) + jnp.where(relative > 0, 16, 0)
    return (bucket[:, None] == jnp.arange(BUCKETS)).astype(f32)


def after(value, *others):
    return lax.optimization_barrier((value, *others))[0]


def arrivals(groups):
    found = []
    for group in range(groups):
        found.append([])
        for hop in range(1, groups):
            for source, way in ((group - hop, 0), (group + hop, 1)):
                if 0 <= source < groups:
                    found[-1].append((source, way, hop))
    return found


def swap_cores(value):
    size = lax.axis_size("mdl")
    return lax.ppermute(value, "mdl", [(core, (core + 1) % size) for core in range(size)])


def shards(
    token_ids,
    item_lengths,
    prefix_lengths,
    group_live,
    partner,
    embedding,
    qkv_weight,
    out_weight,
    up_weight,
    down_weight,
    bias_table,
    norm_gains,
    embedding_first,
    embedding_second,
    qkv_first,
    qkv_second,
    out_first,
    out_second,
    up_first,
    up_second,
    down_first,
    down_second,
    bias_first,
    bias_second,
    gains_first,
    gains_second,
):
    item_count, length = token_ids.shape
    features, vocab = embedding.shape
    grp_size, dat_size, mdl_size = lax.axis_size("grp"), lax.axis_size("dat"), lax.axis_size("mdl")
    group_index, dat_index, mdl_index = lax.axis_index("grp"), lax.axis_index("dat"), lax.axis_index("mdl")
    mine = item_count // mdl_size
    rows = mine * length
    pair_rows = rows // 2
    chunk = min(512, pair_rows)
    chunks = pair_rows // chunk
    group_items = item_count * dat_size
    width = features * dat_size
    first_slot = dat_index * item_count + mdl_index * mine

    tn = ((0,), (0,))
    nt = ((1,), (1,))

    group_ids = share(token_ids, "dat", dat_size)

    def of_core(table, core):
        return lax.dynamic_index_in_dim(table, core % mdl_size, 0, keepdims=False)

    def by_core(ids):
        lead = ids.shape[:-3]
        ids = ids.reshape(-1, dat_size, mdl_size, 2, chunks, chunk).transpose(2, 0, 1, 4, 3, 5)
        return ids.reshape(mdl_size, *lead, dat_size * chunks, 2, chunk)

    def gathered(*shards):
        return lax.all_gather(
            jnp.concatenate([shard.astype(bf) for shard in shards], axis=1), "dat", axis=0, tiled=True
        )

    def halves(own, *widths):
        both = (own, swap_cores(own))
        edges = [0]
        for part in widths:
            edges.append(edges[-1] + part)
        return [[part[:, low:high] for part in both] for low, high in zip(edges, edges[1:])]

    flat_qkv = qkv_weight.reshape(features, -1)
    first_own = gathered(flat_qkv, out_weight.T)
    onehot = bucket_onehot(length)
    line_halves = [
        jnp.einsum("rb,bh->hr", onehot, table, precision=MAX_PRECISION)
        for table in (bias_table, swap_cores(bias_table))
    ]

    looked_up = gather_rows(embedding, of_core(by_core(group_ids), mdl_index))
    spread = lax.all_to_all(
        looked_up.reshape(dat_size, pair_rows, 2 * features), "dat", split_axis=0, concat_axis=0, tiled=True
    )
    second_own = gathered(after(up_weight, looked_up), after(down_weight, looked_up))
    item_lengths, prefix_lengths, partner = after((item_lengths, prefix_lengths, partner), looked_up)
    my_lengths, my_prefixes, my_partner = [
        lax.dynamic_slice_in_dim(value, mdl_index * mine, mine) for value in (item_lengths, prefix_lengths, partner)
    ]
    embedded_low, normed_one = assemble(spread, norm_gains[0])
    embedded = embedded_low.astype(f32)
    qkv_halves, out_halves = halves(after(first_own, spread), flat_qkv.shape[1], out_weight.shape[0])
    qkv_rows = [dot(normed_one, weight).astype(bf).reshape(mine, length, -1) for weight in qkv_halves]
    mixed, log_totals = zip(*[attend(item_qkv, lines, my_lengths) for item_qkv, lines in zip(qkv_rows, line_halves)])
    mixed_rows = [heads.reshape(rows, -1) for heads in mixed]
    up_halves, down_halves = halves(after(second_own, *mixed), up_weight.shape[1], down_weight.shape[1])
    after_attn = embedded + (dot(mixed_rows[0], out_halves[0], nt) + dot(mixed_rows[1], out_halves[1], nt))
    normed_two_f, norm_two_back = jax.vjp(norm_scale, after_attn, norm_gains[1])
    normed_two = normed_two_f.astype(bf)
    gate_acts, gelu_backs = zip(*[jax.vjp(gelu_tanh, dot(normed_two, weight)) for weight in up_halves])
    activated = [act.astype(bf) for act in gate_acts]
    after_ffn = after_attn + (
        dot(activated[0], down_halves[0], nt) + dot(activated[1], down_halves[1], nt)
    )
    positions = jnp.arange(length)
    pool_mask = (
        (positions[None, :] >= my_prefixes[:, None]) & (positions[None, :] < my_lengths[:, None])
    ).astype(f32)

    def pool_tail(stream, gain_row):
        normed_three = norm_scale(stream, gain_row).reshape(mine, length, -1)
        pooled = jnp.sum(normed_three * pool_mask[:, :, None], axis=1) / jnp.sum(pool_mask, axis=1, keepdims=True)
        return pooled * lax.rsqrt(jnp.sum(pooled * pooled, axis=1, keepdims=True) + NORM_EPS)

    vectors, tail_back = jax.vjp(pool_tail, after_ffn, norm_gains[2])

    partner_row = jnp.pad(my_partner.astype(f32), (0, width - mine))[None]
    plane_facts = jnp.concatenate([vectors, partner_row, jnp.zeros((-(mine + 1) % 8, width), f32)], axis=0)
    plane_facts, all_ids = share_both(
        plane_facts, group_ids.reshape(-1, length), ("dat", "mdl"), "grp", (dat_size, mdl_size, grp_size)
    )
    group_vectors = plane_facts[:, :mine].reshape(group_items, width)
    group_partner = plane_facts[:, mine, :mine].reshape(group_items).astype(jnp.int32)
    all_ids = by_core(all_ids.reshape(grp_size, dat_size, item_count, length))
    live_count = jnp.sum(jnp.where(jnp.arange(grp_size) == group_index, group_live, 0))
    live_total = jnp.sum(group_live).astype(f32)
    slots = jnp.arange(group_items)
    live_rows = slots < live_count
    logits = jnp.dot(group_vectors, group_vectors.T, precision=MAX_PRECISION) / SOFTMAX_WARMTH
    allowed = live_rows[None, :] & (slots[None, :] != slots[:, None])
    masked = jnp.where(allowed, logits, MASK_FILL)
    row_top = jnp.max(masked, axis=1, keepdims=True)
    log_total = row_top[:, 0] + jnp.log(jnp.sum(jnp.exp(masked - row_top), axis=1))
    mate_hits = slots[None, :] == group_partner[:, None]
    target = jnp.sum(jnp.where(mate_hits, logits, 0.0), axis=1)
    loss_part = jnp.sum(jnp.where(live_rows, log_total - target, 0.0))
    row_weight = jnp.where(live_rows, 1.0 / live_total, 0.0)
    grad_logits = (
        row_weight[:, None] * (jnp.exp(masked - log_total[:, None]) - mate_hits.astype(f32)) / SOFTMAX_WARMTH
    )
    my_pulls = lax.dynamic_slice_in_dim(grad_logits + grad_logits.T, first_slot, mine)
    grad_vectors = jnp.dot(my_pulls, group_vectors, precision=MAX_PRECISION)

    def both_cores(own, other):
        return (own + swap_cores(other.astype(bf)).astype(f32)).astype(bf)

    def scattered(total):
        return lax.psum_scatter(total, "dat", scatter_dimension=0, tiled=True)

    grad_after_ffn, grad_gain_three = tail_back(grad_vectors)
    grad_ffn = grad_after_ffn.astype(bf)
    total_down = both_cores(*[dot(grad_ffn, act, tn) for act in activated])
    grad_gates = [
        back(dot(grad_ffn, weight))[0].astype(bf) for back, weight in zip(gelu_backs, down_halves)
    ]
    total_up = both_cores(*[dot(normed_two, grad_gate, tn) for grad_gate in grad_gates])
    part_ffn = scattered(jnp.concatenate([total_down, total_up], axis=1))
    two_back = dot(grad_gates[0], up_halves[0], nt) + dot(grad_gates[1], up_halves[1], nt)
    grad_after_attn, grad_gain_two = norm_two_back(two_back)
    grad_after_attn = grad_after_attn + grad_after_ffn
    grad_attn = grad_after_attn.astype(bf)
    total_out = both_cores(*[dot(grad_attn, heads, tn) for heads in mixed_rows])
    grad_mixed = [dot(grad_attn, weight).astype(bf).reshape(mine, length, -1) for weight in out_halves]
    grad_qkv_items, grad_lines = zip(
        *[
            attend_back(item_qkv, lines, my_lengths, stats, grad)
            for item_qkv, lines, stats, grad in zip(qkv_rows, line_halves, log_totals, grad_mixed)
        ]
    )
    grad_qkv_rows = [grad.reshape(rows, -1) for grad in grad_qkv_items]
    one_back = dot(grad_qkv_rows[0], qkv_halves[0], nt) + dot(grad_qkv_rows[1], qkv_halves[1], nt)
    outgoing, grad_gain_one = pack_back(one_back, embedded_low, grad_after_attn, norm_gains[0], features)
    total_qkv = both_cores(*[dot(normed_one, grad, tn) for grad in grad_qkv_rows])
    total_rest = jnp.concatenate([total_qkv, total_out], axis=1)
    part_rest = scattered(total_rest)

    grad_bias_own, grad_bias_other = [
        jnp.einsum("rb,hr->bh", onehot, grad, precision=MAX_PRECISION) for grad in grad_lines
    ]
    grad_bias_all = jnp.where(
        mdl_index == 0,
        jnp.concatenate([grad_bias_own, grad_bias_other], axis=1),
        jnp.concatenate([grad_bias_other, grad_bias_own], axis=1),
    )
    leader = ((dat_index == 0) & (mdl_index == 0)).astype(f32)
    small = jnp.concatenate(
        [
            jnp.stack([grad_gain_one, grad_gain_two, grad_gain_three]).reshape(-1),
            grad_bias_all.reshape(-1),
            (loss_part * leader).reshape(1),
        ]
    )
    used = small.shape[0]
    small = after(jnp.pad(small, (0, -used % (8 * LANES))).reshape(-1, LANES), total_rest)
    small = sum_all(small, ("dat", "mdl"), "grp", (dat_size, mdl_size, grp_size)).reshape(-1)
    grad_gains = small[: 3 * width].reshape(3, width)
    grad_bias = lax.dynamic_slice_in_dim(
        small[3 * width : used - 1].reshape(BUCKETS, -1), mdl_index * bias_table.shape[1], bias_table.shape[1], axis=1
    )
    loss_total = small[used - 1]

    by_group = arrivals(grp_size)
    sources = jnp.array([[group] + [found[0] for found in by_group[group]] for group in range(grp_size)], jnp.int32)
    sources = lax.dynamic_index_in_dim(sources, group_index, 0, keepdims=False)
    place = jnp.concatenate([mdl_index[None].astype(jnp.int32), sources])
    order = [(slot, 0) for slot in range(grp_size)]
    order[-1:] = [(grp_size - 2, 1), (grp_size - 1, 0), (grp_size - 1, 1)]
    staged_ids, staged_flags = stage_ids(place, after(all_ids, outgoing), order)

    outgoing = after(outgoing, part_ffn)
    own_rows = lax.all_to_all(outgoing, "dat", split_axis=0, concat_axis=0, tiled=True)
    own_rows = own_rows.reshape(dat_size * pair_rows, 2 * features)
    moving = [[own_rows], [own_rows]]
    swapped = [[None], [None]]

    def swap(hop, *waits):
        for way in range(2):
            both = way == 1 and moving[0][hop] is moving[1][hop]
            swapped[way].append(swapped[0][hop] if both else swap_cores(after(moving[way][hop], *waits)))

    def move(hop, *waits):
        senders = range(hop - 1, grp_size - 1)
        upward = [(group, group + 1) for group in senders]
        downward = [(grp_size - 1 - group, grp_size - 2 - group) for group in senders]
        if {group for group, _ in upward} & {group for group, _ in downward}:
            for way, pairs in enumerate((upward, downward)):
                moving[way].append(lax.ppermute(after(moving[way][-1], *waits), "grp", pairs))
        else:
            rising = group_index >= hop - 1
            moved = lax.ppermute(after(jnp.where(rising, moving[0][-1], moving[1][-1]), *waits), "grp", upward + downward)
            moving[0].append(moved)
            moving[1].append(moved)

    def candidates(slot):
        found = [by_group[group][slot - 1][1:] for group in range(grp_size)]
        kinds = sorted(set(found))
        return kinds, [kinds.index(kind) for kind in found]

    def stage(slots, first, both):
        segments, picks = [], []
        for slot in slots:
            if slot == 0:
                segments.append([own_rows])
                picks.append([0] * grp_size)
                continue
            kinds, pick = candidates(slot)
            for buffers in (moving, swapped)[: 1 + both]:
                segments.append([buffers[way][hop] for way, hop in kinds])
                picks.append(pick)
        choices = lax.dynamic_index_in_dim(jnp.array(picks, jnp.int32).T, group_index, 0, keepdims=False)
        return Stage(segments, choices, staged_ids, staged_flags, first * dat_size * chunks, features)

    move(1, staged_flags)
    for hop in range(2, grp_size - 1):
        move(hop, small)
    early = stage(range(grp_size - 2), 0, False)
    early.operands[0] = after(early.operands[0], part_rest, small)
    own_table = scatter_rows(early, vocab)
    for hop in range(1, grp_size - 1):
        swap(hop, *((own_table,) if hop == grp_size - 2 else ()))
    move(grp_size - 1, own_table)
    late_table = scatter_rows(stage([grp_size - 2], grp_size - 2, True), vocab)
    other_table = swap_cores(after(own_table, *[ways[-1] for ways in swapped]))
    swap(grp_size - 1, late_table)
    last = stage([grp_size - 1], grp_size, True)
    full_ffn, full_rest = lax.psum((after(part_ffn, late_table), part_rest), "grp")

    table_momentum, table_variance, table_direction, table_squares = finish(
        last,
        embedding,
        embedding_first,
        embedding_second,
        (own_table, other_table, late_table),
    )
    full_ffn, full_rest = after(full_ffn, table_squares), after(full_rest, table_squares)
    by_part = lambda value: value.transpose(1, 0, 2)
    weights = (by_part(qkv_weight), out_weight.T, up_weight, down_weight, bias_table.T, norm_gains)
    gradients = (full_ffn, full_rest, grad_bias.T, grad_gains)
    moments = (
        (by_part(qkv_first), by_part(qkv_second)),
        (out_first.T, out_second.T),
        (up_first, up_second),
        (down_first, down_second),
        (bias_first.T, bias_second.T),
        (gains_first, gains_second),
    )
    first_mdl = (mdl_index == 0).astype(f32)
    first_dat = (dat_index == 0).astype(f32)
    mask = jnp.stack([first_mdl, *[jnp.ones((), f32)] * 4, first_dat, *[first_mdl * first_dat] * 3])
    mask = jnp.broadcast_to(jnp.pad(mask, (0, 16 - mask.shape[0]))[:, None], (16, LANES))
    *results, square_table = small_moments(mask, weights, gradients, moments, max(1, features // 48))
    squares = sum_over(table_squares, square_table, ("dat", "mdl"), (dat_size, mdl_size))
    updated = update_all(squares, (embedding, *weights), (table_direction, *results[2::3]), features // 16)
    outputs = [
        jnp.stack([loss_total, live_total]),
        jnp.sqrt(squares[:9, :2]),
        table_momentum,
        table_variance,
        updated[0],
    ]
    outputs.extend(by_part(value) for value in (results[0], results[1], updated[1]))
    outputs.extend(value.T for value in (results[3], results[4], updated[2]))
    for position in range(2, 6):
        three = (results[3 * position], results[3 * position + 1], updated[position + 1])
        outputs.extend(value.T if position == 4 else value for value in three)
    return tuple(outputs)


def solution(mesh):
    state = [
        P("dat", None),
        P("dat", None, "mdl"),
        P("mdl", "dat"),
        P("dat", "mdl"),
        P("dat", "mdl"),
        P(None, "mdl"),
        P(),
    ]
    placed = [P(("grp", "dat"), None), P(("grp", "dat")), P(("grp", "dat")), P(), P(("grp", "dat"))]
    placed += state + [spec for spec in state for _ in range(2)]
    return jax.shard_map(
        shards,
        mesh=mesh,
        in_specs=tuple(placed),
        out_specs=(P(), P(), *[spec for spec in state for _ in range(3)]),
        check_vma=False,
    )
```

```python
import functools

import jax
import jax.numpy as jnp
from jax import lax
from jax.experimental import pallas as pl
from jax.experimental.pallas import tpu as pltpu
from jax.sharding import PartitionSpec as P

HEADS = 12
HEAD = 64
BUCKETS = 32
STEP = 10


SOFTMAX_WARMTH = 0.01
NORM_EPS = 1e-06
BUCKET_EDGES = (12, 16, 23, 32, 46, 64, 91)
BETA_ONE = 0.9
BETA_TWO = 0.999
ADAM_EPS = 1e-06
WEIGHT_DECAY = 0.01
LEARN_RATE = 0.5
MASK_FILL = -1000000000.0
MAX_PRECISION = lax.Precision.HIGHEST
LANES = 128
bf = jnp.bfloat16
f32 = jnp.float32


BLOCK = 128
NT = (((1,), (1,)), ((), ()))
TN = (((0,), (0,)), ((), ()))


def toeplitz(line, rows):
    out = line
    size = 1
    while size < rows:
        out = jnp.concatenate([out, pltpu.roll(out, size, 1)], axis=0)
        size *= 2
    return out


def diagonal_sums(square):
    rows, width = square.shape
    while rows > 8:
        rows //= 2
        square = square[:rows] + pltpu.roll(square[rows:], width - rows, 1)
    for shift in (4, 2, 1):
        square = square + pltpu.roll(pltpu.roll(square, width - shift, 1), 8 - shift, 0)
    return square[:1]


def head_halves(pair):
    first = lax.broadcasted_iota(jnp.int32, (1, LANES), 1) < HEAD
    return jnp.where(first, pair, 0), jnp.where(first, 0, pair)


def attend_kernel(pairs, scale, lens_ref, line_ref, qkv_ref, mixed_ref, lse_ref, scores, probs):
    items, length, _ = mixed_ref.shape
    blocks = length // BLOCK
    first = lax.broadcasted_iota(jnp.int32, (1, LANES), 1) < HEAD
    key = lax.broadcasted_iota(jnp.int32, (BLOCK, 1), 0)

    def one_pair(pair, carry):
        at = lambda part: pl.ds(pl.multiple_of((part * pairs + pair) * LANES, LANES), LANES)
        biases = [toeplitz(line_ref[pl.ds(2 * pair + head, 1), :], BLOCK) for head in range(2)]
        for item in range(items):
            keys = qkv_ref[item, :, at(1)]
            values = qkv_ref[item, :, at(2)]
            mixed = []
            for head, queries in enumerate(head_halves(qkv_ref[item, :, at(0)] * scale)):
                top = jnp.full((1, length), MASK_FILL, f32)
                for block in range(blocks):
                    rows = slice(block * BLOCK, (block + 1) * BLOCK)
                    low = length - block * BLOCK
                    part = lax.dot_general(keys[rows], queries, NT, preferred_element_type=f32)
                    part = part + biases[head][:, low : low + length]
                    part = jnp.where(key < lens_ref[item] - block * BLOCK, part, MASK_FILL)
                    scores[head, rows, :] = part
                    top = jnp.maximum(top, jnp.max(part, axis=0, keepdims=True))
                whole = jnp.zeros((1, length), f32)
                for block in range(blocks):
                    rows = slice(block * BLOCK, (block + 1) * BLOCK)
                    part = jnp.exp(scores[head, rows, :] - top)
                    scores[head, rows, :] = part
                    whole += jnp.sum(part, axis=0, keepdims=True)
                share = 1.0 / whole
                for block in range(blocks):
                    rows = slice(block * BLOCK, (block + 1) * BLOCK)
                    probs[head, rows, :] = (scores[head, rows, :] * share).astype(bf)
                lse_ref[pl.ds(2 * pair + head, 1), item * length : (item + 1) * length] = top + jnp.log(whole)
                mixed.append(lax.dot_general(probs[head], values, TN, preferred_element_type=f32))
            mixed_ref[item, :, at(0)] = jnp.where(first, mixed[0], mixed[1]).astype(bf)
        return carry

    lax.fori_loop(0, pairs, one_pair, 0)


def attend(qkv, lines, lengths):
    items, length, width = qkv.shape
    width //= 3
    pairs = width // LANES
    vm = pl.BlockSpec(memory_space=pltpu.VMEM)
    return pl.pallas_call(
        functools.partial(attend_kernel, pairs, HEAD**-0.5),
        in_specs=[pl.BlockSpec(memory_space=pltpu.SMEM), vm, vm],
        out_specs=[vm, vm],
        out_shape=[
            jax.ShapeDtypeStruct((items, length, width), bf),
            jax.ShapeDtypeStruct((2 * pairs, items * length), f32),
        ],
        scratch_shapes=[pltpu.VMEM((2, length, length), f32), pltpu.VMEM((2, length, length), bf)],
        compiler_params=pltpu.CompilerParams(vmem_limit_bytes=40 * 2**20),
        cost_estimate=pl.CostEstimate(
            flops=8 * items * length * length * width,
            bytes_accessed=items * length * width * 12,
            transcendentals=items * length * length * width // HEAD,
        ),
        name="attend",
    )(lengths, lines, qkv)


def attend_back_kernel(
    pairs, scale, lens_ref, line_ref, qkv_ref, lse_ref, dmix_ref, dqkv_ref, dline_ref, probs, dprobs, low, diag
):
    items, length, _ = dmix_ref.shape
    blocks = length // BLOCK
    first = lax.broadcasted_iota(jnp.int32, (1, LANES), 1) < HEAD
    key = lax.broadcasted_iota(jnp.int32, (BLOCK, 1), 0)

    def one_pair(pair, carry):
        at = lambda part: pl.ds(pl.multiple_of((part * pairs + pair) * LANES, LANES), LANES)
        biases = [toeplitz(line_ref[pl.ds(2 * pair + head, 1), :], BLOCK) for head in range(2)]
        diag[...] = jnp.zeros_like(diag)
        for item in range(items):
            keys = qkv_ref[item, :, at(1)]
            values = qkv_ref[item, :, at(2)]
            queries = qkv_ref[item, :, at(0)] * scale
            given = dmix_ref[item, :, at(0)]
            dquery, dkeys, dvals = [], [], []
            for head, (mine, pulled) in enumerate(zip(head_halves(queries), head_halves(given))):
                stats = lse_ref[pl.ds(2 * pair + head, 1), item * length : (item + 1) * length]
                inner = jnp.zeros((1, length), f32)
                for block in range(blocks):
                    rows = slice(block * BLOCK, (block + 1) * BLOCK)
                    start = length - block * BLOCK
                    part = lax.dot_general(keys[rows], mine, NT, preferred_element_type=f32)
                    part = jnp.exp(part + biases[head][:, start : start + length] - stats)
                    part = jnp.where(key < lens_ref[item] - block * BLOCK, part, 0.0)
                    back = lax.dot_general(values[rows], pulled, NT, preferred_element_type=f32)
                    probs[head, rows, :] = part
                    dprobs[head, rows, :] = back
                    low[head, rows, :] = part.astype(bf)
                    inner += jnp.sum(part * back, axis=0, keepdims=True)
                dvals.append(jnp.dot(low[head], given, preferred_element_type=f32))
                for block in range(blocks):
                    rows = slice(block * BLOCK, (block + 1) * BLOCK)
                    start = length - block * BLOCK
                    part = probs[head, rows, :] * (dprobs[head, rows, :] - inner)
                    diag[head, :, start : start + length] += part
                    low[head, rows, :] = part.astype(bf)
                dkeys.append(jnp.dot(low[head], queries, preferred_element_type=f32))
                dquery.append(lax.dot_general(low[head], keys, TN, preferred_element_type=f32))
            dqkv_ref[item, :, at(0)] = (jnp.where(first, dquery[0], dquery[1]) * scale).astype(bf)
            dqkv_ref[item, :, at(1)] = jnp.where(first, dkeys[0], dkeys[1]).astype(bf)
            dqkv_ref[item, :, at(2)] = jnp.where(first, dvals[0], dvals[1]).astype(bf)
        for head in range(2):
            dline_ref[pl.ds(2 * pair + head, 1), :] = diagonal_sums(diag[head])
        return carry

    lax.fori_loop(0, pairs, one_pair, 0)


def attend_back(qkv, lines, lengths, lse, dmixed):
    items, length, width = dmixed.shape
    pairs = width // LANES
    vm = pl.BlockSpec(memory_space=pltpu.VMEM)
    square = (2, length, length)
    return pl.pallas_call(
        functools.partial(attend_back_kernel, pairs, HEAD**-0.5),
        in_specs=[pl.BlockSpec(memory_space=pltpu.SMEM), vm, vm, vm, vm],
        out_specs=[vm, vm],
        out_shape=[jax.ShapeDtypeStruct(qkv.shape, bf), jax.ShapeDtypeStruct(lines.shape, f32)],
        scratch_shapes=[
            pltpu.VMEM(square, f32),
            pltpu.VMEM(square, f32),
            pltpu.VMEM(square, bf),
            pltpu.VMEM((2, BLOCK, 2 * length), f32),
        ],
        compiler_params=pltpu.CompilerParams(vmem_limit_bytes=40 * 2**20),
        cost_estimate=pl.CostEstimate(
            flops=20 * items * length * length * width,
            bytes_accessed=items * length * width * 20,
            transcendentals=items * length * length * width // HEAD,
        ),
        name="attend_back",
    )(lengths, lines, qkv, lse, dmixed)


def split_features(features):
    whole = features // LANES * LANES
    return whole, features - whole


def tile_count(features):
    whole, rest = split_features(features)
    return whole // LANES + (rest > 0)


def first_of_pair(packed, features):
    return packed[..., :features]


def second_of_pair(packed, features):
    whole, rest = split_features(features)
    tail = packed[..., features : features + rest]
    return jnp.concatenate([packed[..., features + rest :], tail], axis=-1) if whole else tail


def pack_pair(first, second):
    whole, _ = split_features(first.shape[-1])
    parts = [first, second[..., whole:], second[..., :whole]] if whole else [first, second]
    return jnp.concatenate(parts, axis=-1)


def packed_starts(features, half):
    whole, rest = split_features(features)
    base = 0 if half == 0 else features + rest
    return [base + low for low in range(0, whole, LANES)] + ([whole] if rest else [])


def gather_kernel(features, load_steps, batch, table_ref, ids_ref, out_ref, *scratch):
    step = pl.program_id(0)
    width = table_ref.shape[1]
    tiles = tile_count(features)
    whole, rest = split_features(features)
    stash = scratch[:tiles]
    rows = [scratch[tiles : 2 * tiles], scratch[2 * tiles :]]

    @pl.when(step < load_steps)
    def _():
        base = pl.multiple_of(step * width, width)
        for tile in range(tiles):
            low = tile * LANES
            part = table_ref[low : min(features, low + LANES), :].astype(bf).astype(f32)
            if low == whole:
                blank = [jnp.zeros((LANES - 2 * rest, width), f32)] if 2 * rest < LANES else []
                part = jnp.concatenate([part, part, *blank], axis=0)
            stash[tile][pl.ds(base, width), :] = part.T

    @pl.when(step >= load_steps)
    def _():
        count = out_ref.shape[0]
        for half in range(2):
            def take(index, carry):
                start = pl.multiple_of(index * batch, batch)
                tokens = [ids_ref[0, half, start + inner] for inner in range(batch)]
                for tile in range(tiles):
                    for inner in range(batch):
                        rows[half][tile][pl.ds(start + inner, 1), :] = stash[tile][pl.ds(tokens[inner], 1), :]
                return carry
            lax.fori_loop(0, count // batch, take, 0, unroll=2)
        for half in range(2):
            for tile in range(whole // LANES):
                low = packed_starts(features, half)[tile]
                out_ref[:, low : low + LANES] = rows[half][tile][...].astype(bf)
        if rest:
            lane = lax.broadcasted_iota(jnp.int32, (1, LANES), 1)
            shared = jnp.where(lane < rest, rows[0][-1][...], rows[1][-1][...]).astype(bf)
            out_ref[:, whole : whole + 2 * rest] = shared[:, : 2 * rest]


def gather_rows(table, ids, width=4096, batch=16):
    features, vocab = table.shape
    steps, _, chunk = ids.shape
    tiles = tile_count(features)
    load_steps = pl.cdiv(vocab, width)
    return pl.pallas_call(
        functools.partial(gather_kernel, features, load_steps, batch),
        grid=(load_steps + steps,),
        in_specs=[
            pl.BlockSpec((features, width), lambda s: (0, jnp.minimum(s, load_steps - 1))),
            pl.BlockSpec((1, 2, chunk), lambda s: (jnp.maximum(s - load_steps, 0), 0, 0), memory_space=pltpu.SMEM),
        ],
        out_specs=pl.BlockSpec((chunk, 2 * features), lambda s: (jnp.maximum(s - load_steps, 0), 0)),
        out_shape=jax.ShapeDtypeStruct((steps * chunk, 2 * features), bf),
        scratch_shapes=[pltpu.VMEM((load_steps * width, LANES), f32)] * tiles + [pltpu.VMEM((chunk, LANES), f32)] * (2 * tiles),
        compiler_params=pltpu.CompilerParams(vmem_limit_bytes=60 * 2**20),
        cost_estimate=pl.CostEstimate(flops=0, bytes_accessed=80 * 2**20, transcendentals=0),
        name="gather_rows",
    )(table, ids)


def stage_ids_kernel(batch, order, place_ref, ids_ref, out_ref, flags_ref, flat):
    lane = lax.broadcasted_iota(jnp.int32, (1, LANES), 1)
    count, _, chunk = ids_ref.shape[2:]
    flat[...] = jnp.zeros_like(flat)
    for at, (slot, other) in enumerate(order):
        core = lax.rem(place_ref[0] + other, ids_ref.shape[0])
        for step in range(count):
            index = at * count + step
            ids = ids_ref[core, place_ref[1 + slot], step]
            out_ref[index] = ids
            flat[2 * index : 2 * index + 2, :] = ids
    flags = jnp.zeros((flat.shape[0], LANES), jnp.int32)
    for block in range(chunk // LANES):
        part = flat[:, block * LANES : (block + 1) * LANES]
        found = jnp.zeros(part.shape, jnp.int32)
        for shift in range(1, batch):
            again = (part == pltpu.roll(part, shift, 1)) & (lane % batch >= shift)
            found = jnp.where(again, 1, found)
        flags = jnp.where(lane == block, jnp.max(found, axis=1, keepdims=True), flags)
    for index in range(out_ref.shape[0]):
        flags_ref[index] = flags[2 * index : 2 * index + 2]


def stage_ids(place, ids, order, batch=4):
    *_, count, _, chunk = ids.shape
    vm = pl.BlockSpec(memory_space=pltpu.VMEM)
    total = len(order) * count
    return pl.pallas_call(
        functools.partial(stage_ids_kernel, batch, order),
        in_specs=[pl.BlockSpec(memory_space=pltpu.SMEM), vm],
        out_specs=[vm, vm],
        out_shape=[
            jax.ShapeDtypeStruct((total, 2, chunk), jnp.int32),
            jax.ShapeDtypeStruct((total, 2, LANES), jnp.int32),
        ],
        scratch_shapes=[pltpu.VMEM((2 * total + -2 * total % 8, chunk), jnp.int32)],
        name="stage_ids",
    )(place, ids)


def spread_rows(features, rows_ref, summed):
    whole, rest = split_features(features)
    lane = lax.broadcasted_iota(jnp.int32, (1, LANES), 1)
    for half in range(2):
        for tile, start in enumerate(packed_starts(features, half)):
            if start == whole:
                part = rows_ref[:, start : start + 2 * rest].astype(f32)
                if 2 * rest < LANES:
                    part = jnp.concatenate([part, jnp.zeros((part.shape[0], LANES - 2 * rest), f32)], axis=1)
                mine = lane < rest if half == 0 else (lane >= rest) & (lane < 2 * rest)
                part = jnp.where(mine, part, 0.0)
            else:
                part = rows_ref[:, start : start + LANES].astype(f32)
            summed[half][tile][...] = part


def merge_rows(batch, ids_row_ref, flags_ref, summed):
    count = summed[0][0].shape[0]
    for half in range(2):
        for at in range(count // LANES):
            block = slice(at * LANES, (at + 1) * LANES)

            @pl.when(flags_ref[0, half, at] > 0)
            def _():
                place = lax.broadcasted_iota(jnp.int32, (LANES, LANES), 0) // batch
                same_batch = place == lax.broadcasted_iota(jnp.int32, (LANES, LANES), 1) // batch
                across = jnp.broadcast_to(ids_row_ref[0, half : half + 1, block], (LANES, LANES))
                match = jnp.where((across == across.T) & same_batch, 1.0, 0.0).astype(bf)
                for rows in summed[half]:
                    rows[block, :] = jnp.dot(match, rows[block, :].astype(bf), preferred_element_type=f32)


def add_rows(batch, ids_ref, totals, summed):
    count = summed[0][0].shape[0]

    def add(index, carry):
        start = pl.multiple_of(index * batch, batch)
        for half in range(2):
            tokens = [ids_ref[0, half, start + inner] for inner in range(batch)]
            fresh = [
                [total[pl.ds(tokens[inner], 1), :] + rows[pl.ds(start + inner, 1), :] for inner in range(batch)]
                for total, rows in zip(totals, summed[half])
            ]
            for total, new in zip(totals, fresh):
                for inner in range(batch):
                    total[pl.ds(tokens[inner], 1), :] = new[inner]
        return carry

    lax.fori_loop(0, count // batch, add, 0, unroll=4)


def table_columns(features, totals, base, width):
    whole, rest = split_features(features)
    pieces = [total[pl.ds(base, width), :].T for total in totals]
    if rest:
        pieces[-1] = pieces[-1][:rest] + pieces[-1][rest : 2 * rest]
    return pieces


class Stage:
    def __init__(self, segments, choices, ids, flags, first, features):
        self.arrays = [array for candidates in segments for array in candidates]
        self.segments = [len(candidates) for candidates in segments]
        self.chunk = ids.shape[2]
        self.each = segments[0][0].shape[0] // self.chunk
        self.steps = self.each * len(segments)
        self.operands = [choices, ids, ids, flags, *self.arrays]
        at = lambda s: first + jnp.minimum(s, self.steps - 1)
        self.in_specs = [
            pl.BlockSpec(memory_space=pltpu.SMEM),
            pl.BlockSpec((1, 2, self.chunk), lambda s: (at(s), 0, 0), memory_space=pltpu.SMEM),
            pl.BlockSpec((1, 2, self.chunk), lambda s: (at(s), 0, 0)),
            pl.BlockSpec((1, 2, LANES), lambda s: (at(s), 0, 0), memory_space=pltpu.SMEM),
        ]
        for segment, candidates in enumerate(segments):
            for _ in candidates:
                low = segment * self.each
                self.in_specs.append(
                    pl.BlockSpec(
                        (self.chunk, 2 * features), lambda s, low=low: (jnp.clip(s - low, 0, self.each - 1), 0)
                    )
                )
        self.features = features

    def scratch(self, vocab):
        tiles = tile_count(self.features)
        return [pltpu.VMEM((vocab, LANES), f32)] * tiles + [pltpu.VMEM((self.chunk, LANES), f32)] * (2 * tiles)

    def add(self, batch, refs, scratch):
        choice_ref, ids_ref, ids_row_ref, flags_ref, *rows_refs = refs
        step = pl.program_id(0)
        tiles = tile_count(self.features)
        totals = scratch[:tiles]
        summed = [scratch[tiles : 2 * tiles], scratch[2 * tiles :]]

        @pl.when(step == 0)
        def _():
            for total in totals:
                total[...] = jnp.zeros_like(total)

        for segment, candidates in enumerate(self.segments):
            now = (step >= segment * self.each) & (step < (segment + 1) * self.each)
            for candidate in range(candidates):
                rows_ref, rows_refs = rows_refs[0], rows_refs[1:]

                @pl.when(now & (choice_ref[segment] == candidate))
                def _():
                    spread_rows(self.features, rows_ref, summed)

        @pl.when(step < self.steps)
        def _():
            merge_rows(batch, ids_row_ref, flags_ref, summed)
            add_rows(batch, ids_ref, totals, summed)

        return totals


def scatter_kernel(stage, batch, dense, *refs):
    count = len(stage.operands)
    dense_refs = refs[count : count + dense]
    out_ref = refs[count + dense]
    totals = stage.add(batch, refs[:count], refs[count + dense + 1 :])
    step = pl.program_id(0)
    width = out_ref.shape[1]

    @pl.when(step >= stage.steps)
    def _():
        base = pl.multiple_of((step - stage.steps) * width, width)
        low = 0
        for piece in table_columns(stage.features, totals, base, width):
            cut = slice(low, low + piece.shape[0])
            low += piece.shape[0]
            for dense_ref in dense_refs:
                piece = piece + dense_ref[cut, :].astype(f32)
            out_ref[cut, :] = piece.astype(bf)


def scatter_rows(stage, vocab, dense=(), width=2048, batch=4):
    flush = pl.cdiv(vocab, width)
    block = pl.BlockSpec((stage.features, width), lambda s: (0, jnp.maximum(s - stage.steps, 0)))
    return pl.pallas_call(
        functools.partial(scatter_kernel, stage, batch, len(dense)),
        grid=(stage.steps + flush,),
        in_specs=stage.in_specs + [block] * len(dense),
        out_specs=block,
        out_shape=jax.ShapeDtypeStruct((stage.features, vocab), bf),
        scratch_shapes=stage.scratch(flush * width),
        compiler_params=pltpu.CompilerParams(vmem_limit_bytes=127 * 2**19),
        cost_estimate=pl.CostEstimate(flops=0, bytes_accessed=100 * 2**20, transcendentals=0),
        name="scatter_rows",
    )(*stage.operands, *dense)


def assemble_kernel(features, spread_ref, gain_ref, embedded_ref, normed_ref):
    for half, take in enumerate((first_of_pair, second_of_pair)):
        row = jnp.concatenate([take(spread_ref[part], features) for part in range(spread_ref.shape[0])], axis=1)
        embedded_ref[half] = row
        stream = row.astype(f32)
        scale = lax.rsqrt(jnp.mean(stream * stream, axis=1, keepdims=True) + NORM_EPS)
        normed_ref[half] = (stream * scale * gain_ref[...]).astype(bf)


def assemble(spread, gain, block=128):
    parts, count, features = spread.shape
    features //= 2
    width = parts * features
    block = min(block, count)
    out = jax.ShapeDtypeStruct((2, count, width), bf)
    whole_block = pl.BlockSpec((2, block, width), lambda s: (0, s, 0))
    embedded, normed = pl.pallas_call(
        functools.partial(assemble_kernel, features),
        grid=(count // block,),
        in_specs=[
            pl.BlockSpec((parts, block, 2 * features), lambda s: (0, s, 0)),
            pl.BlockSpec((1, width), lambda s: (0, 0)),
        ],
        out_specs=[whole_block, whole_block],
        out_shape=[out, out],
        compiler_params=pltpu.CompilerParams(vmem_limit_bytes=30 * 2**20),
        name="assemble",
    )(spread, gain.reshape(1, width))
    return embedded.reshape(2 * count, width), normed.reshape(2 * count, width)


def pack_back_kernel(features, back_ref, embedded_ref, passed_ref, gain_ref, packed_ref, grad_gain_ref):
    gain = gain_ref[...]
    halves = []
    grad_gain = jnp.zeros_like(gain)
    for half in range(2):
        stream = embedded_ref[half].astype(f32)
        back = back_ref[half]
        scale = lax.rsqrt(jnp.mean(stream * stream, axis=1, keepdims=True) + NORM_EPS)
        unit = stream * scale
        grad_gain += jnp.sum(back * unit, axis=0, keepdims=True)
        pulled = back * gain
        along = jnp.mean(pulled * unit, axis=1, keepdims=True)
        halves.append((passed_ref[half] + scale * (pulled - unit * along)).astype(bf))
    for part in range(packed_ref.shape[0]):
        cut = slice(part * features, (part + 1) * features)
        packed_ref[part] = pack_pair(halves[0][:, cut], halves[1][:, cut])

    @pl.when(pl.program_id(0) == 0)
    def _():
        grad_gain_ref[...] = jnp.zeros_like(grad_gain_ref)

    grad_gain_ref[...] += grad_gain


def pack_back(back, embedded, passed, gain, features, block=128):
    rows, width = back.shape
    count, parts = rows // 2, width // features
    block = min(block, count)
    pair = pl.BlockSpec((2, block, width), lambda s: (0, s, 0))
    line = pl.BlockSpec((1, width), lambda s: (0, 0))
    packed, grad_gain = pl.pallas_call(
        functools.partial(pack_back_kernel, features),
        grid=(count // block,),
        in_specs=[pair, pair, pair, line],
        out_specs=[pl.BlockSpec((parts, block, 2 * features), lambda s: (0, s, 0)), line],
        out_shape=[jax.ShapeDtypeStruct((parts, count, 2 * features), bf), jax.ShapeDtypeStruct((1, width), f32)],
        compiler_params=pltpu.CompilerParams(vmem_limit_bytes=30 * 2**20),
        name="pack_back",
    )(back.reshape(2, count, width), embedded.reshape(2, count, width), passed.reshape(2, count, width), gain.reshape(1, width))
    return packed, grad_gain[0]


def finish_kernel(stage, vocab, batch, dense, *refs):
    count = len(stage.operands)
    weight_ref, first_ref, second_ref, *dense_refs = refs[count : count + 3 + dense]
    refs, scratch = refs[: count + 7 + dense], refs[count + 7 + dense :]
    momentum_ref, variance_ref, direction_ref, squares_ref = refs[-4:]
    totals = stage.add(batch, refs[:count], scratch)
    step = pl.program_id(0)

    @pl.when(step == 0)
    def _():
        squares_ref[...] = jnp.zeros_like(squares_ref)

    @pl.when(step >= stage.steps)
    def _():
        width = weight_ref.shape[1]
        base = pl.multiple_of((step - stage.steps) * width, width)
        inside = base + lax.broadcasted_iota(jnp.int32, (1, width), 1) < vocab
        low = 0
        for piece in table_columns(stage.features, totals, base, width):
            cut = slice(low, low + piece.shape[0])
            low += piece.shape[0]
            weight = weight_ref[cut, :]
            gradient = piece
            for dense_ref in dense_refs:
                gradient = gradient + dense_ref[cut, :].astype(f32)
            momentum, variance, direction = lamb_direction(weight, gradient, first_ref[cut, :], second_ref[cut, :])
            momentum_ref[cut, :] = momentum
            variance_ref[cut, :] = variance
            direction_ref[cut, :] = direction.astype(bf)
            for line, value in enumerate((weight, direction)):
                value = jnp.where(inside, value, 0.0)
                squares_ref[line : line + 1, :] += jnp.sum(value * value, axis=0, keepdims=True)


def finish(stage, weight, first, second, dense, width=1024, batch=4):
    features, vocab = weight.shape
    columns = pl.cdiv(vocab, width)
    block = pl.BlockSpec((features, width), lambda s: (0, jnp.maximum(s - stage.steps, 0)))
    full = jax.ShapeDtypeStruct(weight.shape, f32)
    return pl.pallas_call(
        functools.partial(finish_kernel, stage, vocab, batch, len(dense)),
        grid=(stage.steps + columns,),
        in_specs=stage.in_specs + [block] * (3 + len(dense)),
        out_specs=[block, block, block, pl.BlockSpec((8, width), lambda s: (0, 0))],
        out_shape=[full, full, jax.ShapeDtypeStruct(weight.shape, bf), jax.ShapeDtypeStruct((8, width), f32)],
        scratch_shapes=stage.scratch(columns * width),
        compiler_params=pltpu.CompilerParams(vmem_limit_bytes=127 * 2**19),
        cost_estimate=pl.CostEstimate(flops=0, bytes_accessed=300 * 2**20, transcendentals=0),
        name="finish",
    )(*stage.operands, weight, first, second, *dense)


MESH = pl.DeviceIdType.MESH


def exchange(value_ref, out_ref, mine, peers, send, received, slot):
    copies = []
    for peer in peers:
        copy = pltpu.make_async_remote_copy(
            src_ref=value_ref,
            dst_ref=out_ref.at[mine],
            send_sem=send.at[slot],
            recv_sem=received.at[slot],
            device_id=peer,
            device_id_type=MESH,
        )
        copy.start()
        copies.append(copy)
        slot += 1
    return copies


def line_peers(axis):
    place, size = lax.axis_index(axis), lax.axis_size(axis)
    return place, [{axis: lax.rem(place + step, size)} for step in range(1, size)]


def plane_peers(axes):
    places = [lax.axis_index(axis) for axis in axes]
    sizes = [lax.axis_size(axis) for axis in axes]
    count = sizes[0] * sizes[1]
    mine = places[0] * sizes[1] + places[1]
    peers = []
    for step in range(1, count):
        peer = lax.rem(mine + step, count)
        peers.append({axes[0]: peer // sizes[1], axes[1]: lax.rem(peer, sizes[1])})
    return mine, peers


def greet(peers):
    barrier = pltpu.get_barrier_semaphore()
    for peer in peers:
        pl.semaphore_signal(barrier, inc=1, device_id=peer, device_id_type=MESH)
    pl.semaphore_wait(barrier, len(peers))


def share_kernel(axis, value_ref, out_ref, send, received):
    mine, peers = line_peers(axis)
    greet(peers)
    out_ref[mine] = value_ref[...]
    for copy in exchange(value_ref, out_ref, mine, peers, send, received, 0):
        copy.wait()


def share(value, axis, size):
    return pl.pallas_call(
        functools.partial(share_kernel, axis),
        in_specs=[pl.BlockSpec(memory_space=pltpu.VMEM)],
        out_specs=pl.BlockSpec(memory_space=pltpu.VMEM),
        out_shape=jax.ShapeDtypeStruct((size, *value.shape), value.dtype),
        scratch_shapes=[pltpu.SemaphoreType.DMA((size - 1,)), pltpu.SemaphoreType.DMA((size - 1,))],
        compiler_params=pltpu.CompilerParams(collective_id=0, has_side_effects=True),
        name="share",
    )(value)


def sum_squares_kernel(axes, rows_ref, table_ref, out_ref, slots, send, received):
    places = [lax.axis_index(axis) for axis in axes]
    sizes = [lax.axis_size(axis) for axis in axes]
    count = sizes[0] * sizes[1]
    mine = places[0] * sizes[1] + places[1]
    barrier = pltpu.get_barrier_semaphore()
    peers = []
    for step in range(1, count):
        peer = lax.rem(mine + step, count)
        peers.append({axes[0]: peer // sizes[1], axes[1]: lax.rem(peer, sizes[1])})
    for peer in peers:
        pl.semaphore_signal(barrier, inc=1, device_id=peer, device_id_type=MESH)
    pl.semaphore_wait(barrier, count - 1)
    lane = lax.broadcasted_iota(jnp.int32, (1, LANES), 1)
    sums = jnp.sum(rows_ref[...], axis=1, keepdims=True)
    slots[mine] = table_ref[...]
    slots[mine, 0:1, :] = jnp.where(lane == 0, sums[0:1], jnp.where(lane == 1, sums[1:2], 0.0)) * table_ref[0:1, :]
    copies = []
    for step, peer in enumerate(peers):
        copy = pltpu.make_async_remote_copy(
            src_ref=slots.at[mine],
            dst_ref=slots.at[mine],
            send_sem=send.at[step],
            recv_sem=received.at[step],
            device_id=peer,
            device_id_type=MESH,
        )
        copy.start()
        copies.append(copy)
    for copy in copies:
        copy.wait()
    total = slots[0]
    for other in range(1, count):
        total = total + slots[other]
    out_ref[...] = total


def sum_over(rows, table, axes, sizes):
    count = sizes[0] * sizes[1]
    return pl.pallas_call(
        functools.partial(sum_squares_kernel, axes),
        in_specs=[pl.BlockSpec(memory_space=pltpu.VMEM)] * 2,
        out_specs=pl.BlockSpec(memory_space=pltpu.VMEM),
        out_shape=jax.ShapeDtypeStruct(table.shape, f32),
        scratch_shapes=[
            pltpu.VMEM((count, *table.shape), f32),
            pltpu.SemaphoreType.DMA((count - 1,)),
            pltpu.SemaphoreType.DMA((count - 1,)),
        ],
        compiler_params=pltpu.CompilerParams(collective_id=1, has_side_effects=True),
        name="sum_over",
    )(rows, table)


def sum_all_kernel(near, far, value_ref, out_ref, near_slots, far_slots, send, received):
    places = [lax.axis_index(axis) for axis in (*near, far)]
    sizes = [lax.axis_size(axis) for axis in (*near, far)]
    count = sizes[0] * sizes[1]
    mine = places[0] * sizes[1] + places[1]
    barrier = pltpu.get_barrier_semaphore()
    plane, line = [], []
    for step in range(1, count):
        peer = lax.rem(mine + step, count)
        plane.append({near[0]: peer // sizes[1], near[1]: lax.rem(peer, sizes[1])})
    for step in range(1, sizes[2]):
        line.append({far: lax.rem(places[2] + step, sizes[2])})
    for peer in plane + line:
        pl.semaphore_signal(barrier, inc=1, device_id=peer, device_id_type=MESH)
    pl.semaphore_wait(barrier, len(plane) + len(line))
    slot = 0
    value = value_ref[...]
    for peers, slots, at in ((plane, near_slots, mine), (line, far_slots, places[2])):
        slots[at] = value
        copies = []
        for peer in peers:
            copy = pltpu.make_async_remote_copy(
                src_ref=slots.at[at],
                dst_ref=slots.at[at],
                send_sem=send.at[slot],
                recv_sem=received.at[slot],
                device_id=peer,
                device_id_type=MESH,
            )
            copy.start()
            copies.append(copy)
            slot += 1
        for copy in copies:
            copy.wait()
        value = slots[0]
        for other in range(1, slots.shape[0]):
            value = value + slots[other]
    out_ref[...] = value


def sum_all(value, near, far, sizes):
    count = sizes[0] * sizes[1]
    slots = count - 1 + sizes[2] - 1
    return pl.pallas_call(
        functools.partial(sum_all_kernel, near, far),
        in_specs=[pl.BlockSpec(memory_space=pltpu.VMEM)],
        out_specs=pl.BlockSpec(memory_space=pltpu.VMEM),
        out_shape=jax.ShapeDtypeStruct(value.shape, f32),
        scratch_shapes=[
            pltpu.VMEM((count, *value.shape), f32),
            pltpu.VMEM((sizes[2], *value.shape), f32),
            pltpu.SemaphoreType.DMA((slots,)),
            pltpu.SemaphoreType.DMA((slots,)),
        ],
        compiler_params=pltpu.CompilerParams(collective_id=2, has_side_effects=True),
        name="sum_all",
    )(value)


def share_both_kernel(plane, line, vectors_ref, ids_ref, all_vectors_ref, all_ids_ref, send, received):
    mine, near = plane_peers(plane)
    place, far = line_peers(line)
    greet(near + far)
    all_vectors_ref[mine] = vectors_ref[...]
    all_ids_ref[place] = ids_ref[...]
    copies = exchange(vectors_ref, all_vectors_ref, mine, near, send, received, 0)
    copies += exchange(ids_ref, all_ids_ref, place, far, send, received, len(near))
    for copy in copies:
        copy.wait()


def share_both(vectors, ids, plane, line, sizes):
    count = sizes[0] * sizes[1]
    slots = count - 1 + sizes[2] - 1
    vm = pl.BlockSpec(memory_space=pltpu.VMEM)
    return pl.pallas_call(
        functools.partial(share_both_kernel, plane, line),
        in_specs=[vm, vm],
        out_specs=[vm, vm],
        out_shape=[
            jax.ShapeDtypeStruct((count, *vectors.shape), vectors.dtype),
            jax.ShapeDtypeStruct((sizes[2], *ids.shape), ids.dtype),
        ],
        scratch_shapes=[pltpu.SemaphoreType.DMA((slots,)), pltpu.SemaphoreType.DMA((slots,))],
        compiler_params=pltpu.CompilerParams(collective_id=3, has_side_effects=True),
        name="share_both",
    )(vectors, ids)


def lamb_direction(weight, gradient, moment_one, moment_two):
    momentum = BETA_ONE * moment_one + (1.0 - BETA_ONE) * gradient
    variance = BETA_TWO * moment_two + (1.0 - BETA_TWO) * gradient * gradient
    direction = (
        momentum / (1.0 - BETA_ONE**STEP) / (jnp.sqrt(variance / (1.0 - BETA_TWO**STEP)) + ADAM_EPS)
        + WEIGHT_DECAY * weight
    )
    return (momentum, variance, direction)


def total_of(value):
    while value.ndim > 2:
        value = jnp.sum(value, axis=1)
    return jnp.sum(jnp.sum(value, axis=1, keepdims=True), axis=0, keepdims=True)


def small_moments_kernel(ffn_ref, rest_ref, small_ref, *refs):
    inputs, outputs, squares_ref = refs[:18], refs[18:-1], refs[-1]
    parts, _, width = inputs[0].shape
    half = ffn_ref.shape[1] // 2
    heads, buckets = inputs[12].shape
    gains, model = inputs[15].shape
    lines = model // LANES
    first_mdl, first_dat = lax.axis_index("mdl") == 0, lax.axis_index("dat") == 0

    def bias_gradient():
        start = gains * lines
        own = [small_ref[start + core * heads : start + (core + 1) * heads, :buckets] for core in range(HEADS // heads)]
        return functools.reduce(
            lambda kept, at: jnp.where(lax.axis_index("mdl") == at, own[at], kept), range(1, len(own)), own[0]
        )

    def gain_gradient():
        rows = [[small_ref[gain * lines + at : gain * lines + at + 1, :] for at in range(lines)] for gain in range(gains)]
        return jnp.concatenate([jnp.concatenate(row, axis=1) for row in rows], axis=0)

    gradient_of = (
        lambda: jnp.stack([rest_ref[:, part * width : (part + 1) * width] for part in range(parts)]),
        lambda: rest_ref[:, parts * width :],
        lambda: ffn_ref[:, half:],
        lambda: ffn_ref[:, :half],
        bias_gradient,
        gain_gradient,
    )
    lane = lax.broadcasted_iota(jnp.int32, (1, LANES), 1)
    counted = [first_mdl, True, True, True, True, first_dat] + [first_mdl & first_dat] * 3

    @pl.when(pl.program_id(0) == 0)
    def _():
        squares_ref[...] = jnp.zeros_like(squares_ref)
        squares_ref[0:1, :] = jnp.where(counted[0], jnp.ones((1, LANES), f32), 0.0)

    def update(place):
        weight_ref, first_ref, second_ref = inputs[3 * place : 3 * place + 3]
        weight = weight_ref[...]
        results = lamb_direction(weight, gradient_of[place]().astype(f32), first_ref[...], second_ref[...])
        for ref, value in zip(outputs[3 * place : 3 * place + 3], results):
            ref[...] = value
        return weight * weight, results[2] * results[2]

    def add(line, weight_square, direction_square):
        both = jnp.where(lane == 0, weight_square, jnp.where(lane == 1, direction_square, 0.0))
        squares_ref[line : line + 1, :] += jnp.where(counted[line], both, 0.0)

    for place in range(4):
        weight_square, direction_square = update(place)
        add(place + 1, total_of(weight_square), total_of(direction_square))

    @pl.when(pl.program_id(0) == 0)
    def _():
        weight_square, direction_square = update(4)
        add(5, total_of(weight_square), total_of(direction_square))
        weight_square, direction_square = update(5)
        for row in range(weight_square.shape[0]):
            add(6 + row, total_of(weight_square[row : row + 1]), total_of(direction_square[row : row + 1]))


def row_block(value, steps):
    if value.ndim == 3:
        return pl.BlockSpec((value.shape[0], value.shape[1] // steps, value.shape[2]), lambda s: (0, s, 0))
    return pl.BlockSpec((value.shape[0] // steps, value.shape[1]), lambda s: (s, 0))


def whole_block(value):
    return pl.BlockSpec(value.shape, lambda s: (0,) * value.ndim)


def small_moments(weights, gradients, moments, steps):
    operands = [*gradients]
    in_specs = [row_block(value, steps) for value in operands[:2]] + [whole_block(operands[2])]
    out_specs, out_shape = [], []
    for place, (weight, states) in enumerate(zip(weights, moments)):
        spec = row_block(weight, steps) if place < 4 else whole_block(weight)
        operands += [weight, *states]
        in_specs += [spec] * 3
        out_specs += [spec] * 3
        out_shape += [jax.ShapeDtypeStruct(weight.shape, f32)] * 3
    return pl.pallas_call(
        small_moments_kernel,
        grid=(steps,),
        in_specs=in_specs,
        out_specs=out_specs + [pl.BlockSpec((16, LANES), lambda s: (0, 0))],
        out_shape=out_shape + [jax.ShapeDtypeStruct((16, LANES), f32)],
        compiler_params=pltpu.CompilerParams(vmem_limit_bytes=127 * 2**19),
        name="small_moments",
    )(*operands)


def update_all_kernel(squares_ref, *refs):
    norms = jnp.sqrt(squares_ref[...])
    rates = LEARN_RATE * norms[:, 0:1] / norms[:, 1:2]
    count = len(refs) // 3
    for place in range(count):
        weight_ref, direction_ref, updated_ref = refs[2 * place], refs[2 * place + 1], refs[2 * count + place]
        rate = rates[6:9] if place == 6 else rates[place : place + 1]
        weight = weight_ref[...]
        if weight.ndim == 3:
            rate = rate[:, :, None]
        updated_ref[...] = weight - rate * direction_ref[...].astype(f32)


def update_all(squares, weights, directions, steps):
    operands, in_specs, out_specs, out_shape = [squares], [whole_block(squares)], [], []
    for place, (weight, direction) in enumerate(zip(weights, directions)):
        spec = row_block(weight, steps) if place < 5 else whole_block(weight)
        operands += [weight, direction]
        in_specs += [spec] * 2
        out_specs += [spec]
        out_shape += [jax.ShapeDtypeStruct(weight.shape, f32)]
    return pl.pallas_call(
        update_all_kernel,
        grid=(steps,),
        in_specs=in_specs,
        out_specs=out_specs,
        out_shape=out_shape,
        compiler_params=pltpu.CompilerParams(vmem_limit_bytes=127 * 2**19),
        name="update_all",
    )(*operands)


def norm_scale(stream, gain_row):
    return (
        stream * lax.rsqrt(jnp.mean(stream * stream, axis=-1, keepdims=True) + NORM_EPS) * gain_row
    )


def gelu_tanh(pre_act):
    return jax.nn.gelu(pre_act, approximate=True)


def dot(left, right, dims=((1,), (0,))):
    return lax.dot_general(left, right, (dims, ((), ())), preferred_element_type=f32)


def bucket_onehot(length):
    relative = length - jnp.arange(2 * length, dtype=jnp.int32)
    distance = jnp.abs(relative)
    far_bucket = 8 + sum(((distance >= threshold).astype(jnp.int32) for threshold in BUCKET_EDGES))
    bucket = jnp.where(distance < 8, distance, far_bucket) + jnp.where(relative > 0, 16, 0)
    return (bucket[:, None] == jnp.arange(BUCKETS)).astype(f32)


def after(value, *others):
    return lax.optimization_barrier((value, *others))[0]


def arrivals(groups):
    found = []
    for group in range(groups):
        found.append([])
        for hop in range(1, groups):
            for source, way in ((group - hop, 0), (group + hop, 1)):
                if 0 <= source < groups:
                    found[-1].append((source, way, hop))
    return found


def swap_cores(value):
    size = lax.axis_size("mdl")
    return lax.ppermute(value, "mdl", [(core, (core + 1) % size) for core in range(size)])


def shards(
    token_ids,
    item_lengths,
    prefix_lengths,
    group_live,
    partner,
    embedding,
    qkv_weight,
    out_weight,
    up_weight,
    down_weight,
    bias_table,
    norm_gains,
    embedding_first,
    embedding_second,
    qkv_first,
    qkv_second,
    out_first,
    out_second,
    up_first,
    up_second,
    down_first,
    down_second,
    bias_first,
    bias_second,
    gains_first,
    gains_second,
):
    item_count, length = token_ids.shape
    features, vocab = embedding.shape
    grp_size, dat_size, mdl_size = lax.axis_size("grp"), lax.axis_size("dat"), lax.axis_size("mdl")
    group_index, dat_index, mdl_index = lax.axis_index("grp"), lax.axis_index("dat"), lax.axis_index("mdl")
    mine = item_count // mdl_size
    rows = mine * length
    pair_rows = rows // 2
    chunk = min(512, pair_rows)
    chunks = pair_rows // chunk
    group_items = item_count * dat_size
    width = features * dat_size
    first_slot = dat_index * item_count + mdl_index * mine

    tn = ((0,), (0,))
    nt = ((1,), (1,))

    group_ids = share(token_ids, "dat", dat_size)

    def of_core(table, core):
        return lax.dynamic_index_in_dim(table, core % mdl_size, 0, keepdims=False)

    def by_core(ids):
        lead = ids.shape[:-3]
        ids = ids.reshape(-1, dat_size, mdl_size, 2, chunks, chunk).transpose(2, 0, 1, 4, 3, 5)
        return ids.reshape(mdl_size, *lead, dat_size * chunks, 2, chunk)

    def gathered(*shards):
        return lax.all_gather(
            jnp.concatenate([shard.astype(bf) for shard in shards], axis=1), "dat", axis=0, tiled=True
        )

    def halves(own, *widths):
        both = (own, swap_cores(own))
        edges = [0]
        for part in widths:
            edges.append(edges[-1] + part)
        return [[part[:, low:high] for part in both] for low, high in zip(edges, edges[1:])]

    flat_qkv = qkv_weight.reshape(features, -1)
    first_own = gathered(flat_qkv, out_weight.T)
    onehot = bucket_onehot(length)
    line_halves = [
        jnp.einsum("rb,bh->hr", onehot, table, precision=MAX_PRECISION)
        for table in (bias_table, swap_cores(bias_table))
    ]

    looked_up = gather_rows(embedding, of_core(by_core(group_ids), mdl_index))
    spread = lax.all_to_all(
        looked_up.reshape(dat_size, pair_rows, 2 * features), "dat", split_axis=0, concat_axis=0, tiled=True
    )
    second_own = gathered(after(up_weight, looked_up), after(down_weight, looked_up))
    item_lengths, prefix_lengths, partner = after((item_lengths, prefix_lengths, partner), looked_up)
    my_lengths, my_prefixes, my_partner = [
        lax.dynamic_slice_in_dim(value, mdl_index * mine, mine) for value in (item_lengths, prefix_lengths, partner)
    ]
    embedded_low, normed_one = assemble(spread, norm_gains[0])
    embedded = embedded_low.astype(f32)
    qkv_halves, out_halves = halves(after(first_own, spread), flat_qkv.shape[1], out_weight.shape[0])
    qkv_rows = [dot(normed_one, weight).astype(bf).reshape(mine, length, -1) for weight in qkv_halves]
    mixed, log_totals = zip(*[attend(item_qkv, lines, my_lengths) for item_qkv, lines in zip(qkv_rows, line_halves)])
    mixed_rows = [heads.reshape(rows, -1) for heads in mixed]
    up_halves, down_halves = halves(after(second_own, *mixed), up_weight.shape[1], down_weight.shape[1])
    after_attn = embedded + (dot(mixed_rows[0], out_halves[0], nt) + dot(mixed_rows[1], out_halves[1], nt))
    normed_two_f, norm_two_back = jax.vjp(norm_scale, after_attn, norm_gains[1])
    normed_two = normed_two_f.astype(bf)
    gate_acts, gelu_backs = zip(*[jax.vjp(gelu_tanh, dot(normed_two, weight)) for weight in up_halves])
    activated = [act.astype(bf) for act in gate_acts]
    after_ffn = after_attn + (
        dot(activated[0], down_halves[0], nt) + dot(activated[1], down_halves[1], nt)
    )
    positions = jnp.arange(length)
    pool_mask = (
        (positions[None, :] >= my_prefixes[:, None]) & (positions[None, :] < my_lengths[:, None])
    ).astype(f32)

    def pool_tail(stream, gain_row):
        normed_three = norm_scale(stream, gain_row).reshape(mine, length, -1)
        pooled = jnp.sum(normed_three * pool_mask[:, :, None], axis=1) / jnp.sum(pool_mask, axis=1, keepdims=True)
        return pooled * lax.rsqrt(jnp.sum(pooled * pooled, axis=1, keepdims=True) + NORM_EPS)

    vectors, tail_back = jax.vjp(pool_tail, after_ffn, norm_gains[2])

    partner_row = jnp.pad(my_partner.astype(f32), (0, width - mine))[None]
    plane_facts = jnp.concatenate([vectors, partner_row, jnp.zeros((-(mine + 1) % 8, width), f32)], axis=0)
    plane_facts, all_ids = share_both(
        plane_facts, group_ids.reshape(-1, length), ("dat", "mdl"), "grp", (dat_size, mdl_size, grp_size)
    )
    group_vectors = plane_facts[:, :mine].reshape(group_items, width)
    group_partner = plane_facts[:, mine, :mine].reshape(group_items).astype(jnp.int32)
    all_ids = by_core(all_ids.reshape(grp_size, dat_size, item_count, length))
    live_count = jnp.sum(jnp.where(jnp.arange(grp_size) == group_index, group_live, 0))
    live_total = jnp.sum(group_live).astype(f32)
    slots = jnp.arange(group_items)
    live_rows = slots < live_count
    logits = jnp.dot(group_vectors, group_vectors.T, precision=MAX_PRECISION) / SOFTMAX_WARMTH
    allowed = live_rows[None, :] & (slots[None, :] != slots[:, None])
    masked = jnp.where(allowed, logits, MASK_FILL)
    row_top = jnp.max(masked, axis=1, keepdims=True)
    log_total = row_top[:, 0] + jnp.log(jnp.sum(jnp.exp(masked - row_top), axis=1))
    mate_hits = slots[None, :] == group_partner[:, None]
    target = jnp.sum(jnp.where(mate_hits, logits, 0.0), axis=1)
    loss_part = jnp.sum(jnp.where(live_rows, log_total - target, 0.0))
    row_weight = jnp.where(live_rows, 1.0 / live_total, 0.0)
    grad_logits = (
        row_weight[:, None] * (jnp.exp(masked - log_total[:, None]) - mate_hits.astype(f32)) / SOFTMAX_WARMTH
    )
    my_pulls = lax.dynamic_slice_in_dim(grad_logits + grad_logits.T, first_slot, mine)
    grad_vectors = jnp.dot(my_pulls, group_vectors, precision=MAX_PRECISION)

    def both_cores(own, other):
        return (own + swap_cores(other.astype(bf)).astype(f32)).astype(bf)

    def scattered(total):
        return lax.psum_scatter(total, "dat", scatter_dimension=0, tiled=True)

    grad_after_ffn, grad_gain_three = tail_back(grad_vectors)
    grad_ffn = grad_after_ffn.astype(bf)
    total_down = both_cores(*[dot(grad_ffn, act, tn) for act in activated])
    grad_gates = [
        back(dot(grad_ffn, weight))[0].astype(bf) for back, weight in zip(gelu_backs, down_halves)
    ]
    total_up = both_cores(*[dot(normed_two, grad_gate, tn) for grad_gate in grad_gates])
    part_ffn = scattered(jnp.concatenate([total_down, total_up], axis=1))
    two_back = dot(grad_gates[0], up_halves[0], nt) + dot(grad_gates[1], up_halves[1], nt)
    grad_after_attn, grad_gain_two = norm_two_back(two_back)
    grad_after_attn = grad_after_attn + grad_after_ffn
    grad_attn = grad_after_attn.astype(bf)
    total_out = both_cores(*[dot(grad_attn, heads, tn) for heads in mixed_rows])
    grad_mixed = [dot(grad_attn, weight).astype(bf).reshape(mine, length, -1) for weight in out_halves]
    grad_qkv_items, grad_lines = zip(
        *[
            attend_back(item_qkv, lines, my_lengths, stats, grad)
            for item_qkv, lines, stats, grad in zip(qkv_rows, line_halves, log_totals, grad_mixed)
        ]
    )
    grad_qkv_rows = [grad.reshape(rows, -1) for grad in grad_qkv_items]
    one_back = dot(grad_qkv_rows[0], qkv_halves[0], nt) + dot(grad_qkv_rows[1], qkv_halves[1], nt)
    outgoing, grad_gain_one = pack_back(one_back, embedded_low, grad_after_attn, norm_gains[0], features)
    total_qkv = both_cores(*[dot(normed_one, grad, tn) for grad in grad_qkv_rows])
    total_rest = jnp.concatenate([total_qkv, total_out], axis=1)
    part_rest = scattered(total_rest)

    grad_bias_own, grad_bias_other = [
        jnp.einsum("rb,hr->hb", onehot, grad, precision=MAX_PRECISION) for grad in grad_lines
    ]
    grad_bias_all = jnp.where(
        mdl_index == 0,
        jnp.concatenate([grad_bias_own, grad_bias_other], axis=0),
        jnp.concatenate([grad_bias_other, grad_bias_own], axis=0),
    )
    leader = ((dat_index == 0) & (mdl_index == 0)).astype(f32)
    gain_lines = jnp.stack([grad_gain_one, grad_gain_two, grad_gain_three]).reshape(-1, LANES)
    loss_line = jnp.full((1, LANES), loss_part * leader)
    small = jnp.concatenate(
        [gain_lines, jnp.pad(grad_bias_all, ((0, 0), (0, LANES - BUCKETS))), loss_line], axis=0
    )
    small = jnp.pad(small, ((0, -small.shape[0] % 8), (0, 0)))

    by_group = arrivals(grp_size)
    sources = jnp.array([[group] + [found[0] for found in by_group[group]] for group in range(grp_size)], jnp.int32)
    sources = lax.dynamic_index_in_dim(sources, group_index, 0, keepdims=False)
    place = jnp.concatenate([mdl_index[None].astype(jnp.int32), sources])
    order = [(slot, 0) for slot in range(grp_size)]
    order[-1:] = [(grp_size - 2, 1), (grp_size - 1, 0), (grp_size - 1, 1)]
    staged_ids, staged_flags = stage_ids(place, after(all_ids, outgoing), order)

    outgoing = after(outgoing, part_ffn)
    own_rows = lax.all_to_all(outgoing, "dat", split_axis=0, concat_axis=0, tiled=True)
    own_rows = own_rows.reshape(dat_size * pair_rows, 2 * features)
    moving = [[own_rows], [own_rows]]
    swapped = [[None], [None]]

    def swap(hop, *waits):
        for way in range(2):
            both = way == 1 and moving[0][hop] is moving[1][hop]
            swapped[way].append(swapped[0][hop] if both else swap_cores(after(moving[way][hop], *waits)))

    def move(hop, *waits):
        senders = range(hop - 1, grp_size - 1)
        upward = [(group, group + 1) for group in senders]
        downward = [(grp_size - 1 - group, grp_size - 2 - group) for group in senders]
        if {group for group, _ in upward} & {group for group, _ in downward}:
            for way, pairs in enumerate((upward, downward)):
                moving[way].append(lax.ppermute(after(moving[way][-1], *waits), "grp", pairs))
        else:
            rising = group_index >= hop - 1
            moved = lax.ppermute(after(jnp.where(rising, moving[0][-1], moving[1][-1]), *waits), "grp", upward + downward)
            moving[0].append(moved)
            moving[1].append(moved)

    def candidates(slot):
        found = [by_group[group][slot - 1][1:] for group in range(grp_size)]
        kinds = sorted(set(found))
        return kinds, [kinds.index(kind) for kind in found]

    def stage(slots, first, both):
        segments, picks = [], []
        for slot in slots:
            if slot == 0:
                segments.append([own_rows])
                picks.append([0] * grp_size)
                continue
            kinds, pick = candidates(slot)
            for buffers in (moving, swapped)[: 1 + both]:
                segments.append([buffers[way][hop] for way, hop in kinds])
                picks.append(pick)
        choices = lax.dynamic_index_in_dim(jnp.array(picks, jnp.int32).T, group_index, 0, keepdims=False)
        return Stage(segments, choices, staged_ids, staged_flags, first * dat_size * chunks, features)

    move(1, staged_flags)
    first_table = scatter_rows(stage([0], 0, False), vocab)
    small = sum_all(after(small, first_table), ("dat", "mdl"), "grp", (dat_size, mdl_size, grp_size))
    for hop in range(2, grp_size - 1):
        move(hop, small)
        swap(hop - 1)
    early = stage(range(1, grp_size - 2), 1, False)
    early.operands[0] = after(early.operands[0], part_rest)
    own_table = scatter_rows(early, vocab, (first_table,))
    swap(grp_size - 2, own_table)
    move(grp_size - 1, own_table)
    other_table = swap_cores(after(own_table, *[kept for way in swapped for kept in way[1:]]))
    late_table = scatter_rows(stage([grp_size - 2], grp_size - 2, True), vocab)
    swap(grp_size - 1, late_table)
    last = stage([grp_size - 1], grp_size, True)
    full_ffn, full_rest = lax.psum((after(part_ffn, late_table), part_rest), "grp")
    table_momentum, table_variance, table_direction, table_squares = finish(
        last,
        embedding,
        embedding_first,
        embedding_second,
        (own_table, other_table, late_table),
    )
    full_ffn, full_rest = after(full_ffn, table_squares), after(full_rest, table_squares)
    loss_total = small[gain_lines.shape[0] + HEADS, 0]
    by_part = lambda value: value.transpose(1, 0, 2)
    weights = (by_part(qkv_weight), out_weight.T, up_weight, down_weight, bias_table.T, norm_gains)
    gradients = (full_ffn, full_rest, small)
    moments = (
        (by_part(qkv_first), by_part(qkv_second)),
        (out_first.T, out_second.T),
        (up_first, up_second),
        (down_first, down_second),
        (bias_first.T, bias_second.T),
        (gains_first, gains_second),
    )
    *results, square_table = small_moments(weights, gradients, moments, max(1, features // 48))
    squares = sum_over(table_squares, square_table, ("dat", "mdl"), (dat_size, mdl_size))
    updated = update_all(squares, (embedding, *weights), (table_direction, *results[2::3]), features // 16)
    outputs = [
        jnp.stack([loss_total, live_total]),
        jnp.sqrt(squares[:9, :2]),
        table_momentum,
        table_variance,
        updated[0],
    ]
    outputs.extend(by_part(value) for value in (results[0], results[1], updated[1]))
    outputs.extend(value.T for value in (results[3], results[4], updated[2]))
    for position in range(2, 6):
        three = (results[3 * position], results[3 * position + 1], updated[position + 1])
        outputs.extend(value.T if position == 4 else value for value in three)
    return tuple(outputs)


def solution(mesh):
    state = [
        P("dat", None),
        P("dat", None, "mdl"),
        P("mdl", "dat"),
        P("dat", "mdl"),
        P("dat", "mdl"),
        P(None, "mdl"),
        P(),
    ]
    placed = [P(("grp", "dat"), None), P(("grp", "dat")), P(("grp", "dat")), P(), P(("grp", "dat"))]
    placed += state + [spec for spec in state for _ in range(2)]
    return jax.shard_map(
        shards,
        mesh=mesh,
        in_specs=tuple(placed),
        out_specs=(P(), P(), *[spec for spec in state for _ in range(3)]),
        check_vma=False,
    )
```

```python
import functools

import jax
import jax.numpy as jnp
from jax import lax
from jax.experimental import pallas as pl
from jax.experimental.pallas import tpu as pltpu
from jax.sharding import PartitionSpec as P

HEADS = 12
HEAD = 64
BUCKETS = 32
STEP = 10


SOFTMAX_WARMTH = 0.01
NORM_EPS = 1e-06
BUCKET_EDGES = (12, 16, 23, 32, 46, 64, 91)
BETA_ONE = 0.9
BETA_TWO = 0.999
ADAM_EPS = 1e-06
WEIGHT_DECAY = 0.01
LEARN_RATE = 0.5
MASK_FILL = -1000000000.0
MAX_PRECISION = lax.Precision.HIGHEST
LANES = 128
bf = jnp.bfloat16
f32 = jnp.float32


BLOCK = 128
NT = (((1,), (1,)), ((), ()))
TN = (((0,), (0,)), ((), ()))


def toeplitz(line, rows):
    out = line
    size = 1
    while size < rows:
        out = jnp.concatenate([out, pltpu.roll(out, size, 1)], axis=0)
        size *= 2
    return out


def diagonal_sums(square):
    rows, width = square.shape
    while rows > 8:
        rows //= 2
        square = square[:rows] + pltpu.roll(square[rows:], width - rows, 1)
    for shift in (4, 2, 1):
        square = square + pltpu.roll(pltpu.roll(square, width - shift, 1), 8 - shift, 0)
    return square[:1]


def head_halves(pair):
    first = lax.broadcasted_iota(jnp.int32, (1, LANES), 1) < HEAD
    return jnp.where(first, pair, 0), jnp.where(first, 0, pair)


def attend_kernel(pairs, scale, lens_ref, line_ref, qkv_ref, mixed_ref, lse_ref, scores, probs):
    items, length, _ = mixed_ref.shape
    blocks = length // BLOCK
    first = lax.broadcasted_iota(jnp.int32, (1, LANES), 1) < HEAD
    key = lax.broadcasted_iota(jnp.int32, (BLOCK, 1), 0)

    def one_pair(pair, carry):
        at = lambda part: pl.ds(pl.multiple_of((part * pairs + pair) * LANES, LANES), LANES)
        biases = [toeplitz(line_ref[pl.ds(2 * pair + head, 1), :], BLOCK) for head in range(2)]
        for item in range(items):
            keys = qkv_ref[item, :, at(1)]
            values = qkv_ref[item, :, at(2)]
            mixed = []
            for head, queries in enumerate(head_halves(qkv_ref[item, :, at(0)] * scale)):
                top = jnp.full((1, length), MASK_FILL, f32)
                for block in range(blocks):
                    rows = slice(block * BLOCK, (block + 1) * BLOCK)
                    low = length - block * BLOCK
                    part = lax.dot_general(keys[rows], queries, NT, preferred_element_type=f32)
                    part = part + biases[head][:, low : low + length]
                    part = jnp.where(key < lens_ref[item] - block * BLOCK, part, MASK_FILL)
                    scores[head, rows, :] = part
                    top = jnp.maximum(top, jnp.max(part, axis=0, keepdims=True))
                whole = jnp.zeros((1, length), f32)
                for block in range(blocks):
                    rows = slice(block * BLOCK, (block + 1) * BLOCK)
                    part = jnp.exp(scores[head, rows, :] - top)
                    scores[head, rows, :] = part
                    whole += jnp.sum(part, axis=0, keepdims=True)
                share = 1.0 / whole
                for block in range(blocks):
                    rows = slice(block * BLOCK, (block + 1) * BLOCK)
                    probs[head, rows, :] = (scores[head, rows, :] * share).astype(bf)
                lse_ref[pl.ds(2 * pair + head, 1), item * length : (item + 1) * length] = top + jnp.log(whole)
                mixed.append(lax.dot_general(probs[head], values, TN, preferred_element_type=f32))
            mixed_ref[item, :, at(0)] = jnp.where(first, mixed[0], mixed[1]).astype(bf)
        return carry

    lax.fori_loop(0, pairs, one_pair, 0)


def attend(qkv, lines, lengths):
    items, length, width = qkv.shape
    width //= 3
    pairs = width // LANES
    vm = pl.BlockSpec(memory_space=pltpu.VMEM)
    return pl.pallas_call(
        functools.partial(attend_kernel, pairs, HEAD**-0.5),
        in_specs=[pl.BlockSpec(memory_space=pltpu.SMEM), vm, vm],
        out_specs=[vm, vm],
        out_shape=[
            jax.ShapeDtypeStruct((items, length, width), bf),
            jax.ShapeDtypeStruct((2 * pairs, items * length), f32),
        ],
        scratch_shapes=[pltpu.VMEM((2, length, length), f32), pltpu.VMEM((2, length, length), bf)],
        compiler_params=pltpu.CompilerParams(vmem_limit_bytes=40 * 2**20),
        cost_estimate=pl.CostEstimate(
            flops=8 * items * length * length * width,
            bytes_accessed=items * length * width * 12,
            transcendentals=items * length * length * width // HEAD,
        ),
        name="attend",
    )(lengths, lines, qkv)


def attend_back_kernel(
    pairs, scale, lens_ref, line_ref, qkv_ref, lse_ref, dmix_ref, dqkv_ref, dline_ref, probs, dprobs, low, diag
):
    items, length, _ = dmix_ref.shape
    blocks = length // BLOCK
    first = lax.broadcasted_iota(jnp.int32, (1, LANES), 1) < HEAD
    key = lax.broadcasted_iota(jnp.int32, (BLOCK, 1), 0)

    def one_pair(pair, carry):
        at = lambda part: pl.ds(pl.multiple_of((part * pairs + pair) * LANES, LANES), LANES)
        biases = [toeplitz(line_ref[pl.ds(2 * pair + head, 1), :], BLOCK) for head in range(2)]
        diag[...] = jnp.zeros_like(diag)
        for item in range(items):
            keys = qkv_ref[item, :, at(1)]
            values = qkv_ref[item, :, at(2)]
            queries = qkv_ref[item, :, at(0)] * scale
            given = dmix_ref[item, :, at(0)]
            dquery, dkeys, dvals = [], [], []
            for head, (mine, pulled) in enumerate(zip(head_halves(queries), head_halves(given))):
                stats = lse_ref[pl.ds(2 * pair + head, 1), item * length : (item + 1) * length]
                inner = jnp.zeros((1, length), f32)
                for block in range(blocks):
                    rows = slice(block * BLOCK, (block + 1) * BLOCK)
                    start = length - block * BLOCK
                    part = lax.dot_general(keys[rows], mine, NT, preferred_element_type=f32)
                    part = jnp.exp(part + biases[head][:, start : start + length] - stats)
                    part = jnp.where(key < lens_ref[item] - block * BLOCK, part, 0.0)
                    back = lax.dot_general(values[rows], pulled, NT, preferred_element_type=f32)
                    probs[head, rows, :] = part
                    dprobs[head, rows, :] = back
                    low[head, rows, :] = part.astype(bf)
                    inner += jnp.sum(part * back, axis=0, keepdims=True)
                dvals.append(jnp.dot(low[head], given, preferred_element_type=f32))
                for block in range(blocks):
                    rows = slice(block * BLOCK, (block + 1) * BLOCK)
                    start = length - block * BLOCK
                    part = probs[head, rows, :] * (dprobs[head, rows, :] - inner)
                    diag[head, :, start : start + length] += part
                    low[head, rows, :] = part.astype(bf)
                dkeys.append(jnp.dot(low[head], queries, preferred_element_type=f32))
                dquery.append(lax.dot_general(low[head], keys, TN, preferred_element_type=f32))
            dqkv_ref[item, :, at(0)] = (jnp.where(first, dquery[0], dquery[1]) * scale).astype(bf)
            dqkv_ref[item, :, at(1)] = jnp.where(first, dkeys[0], dkeys[1]).astype(bf)
            dqkv_ref[item, :, at(2)] = jnp.where(first, dvals[0], dvals[1]).astype(bf)
        for head in range(2):
            dline_ref[pl.ds(2 * pair + head, 1), :] = diagonal_sums(diag[head])
        return carry

    lax.fori_loop(0, pairs, one_pair, 0)


def attend_back(qkv, lines, lengths, lse, dmixed):
    items, length, width = dmixed.shape
    pairs = width // LANES
    vm = pl.BlockSpec(memory_space=pltpu.VMEM)
    square = (2, length, length)
    return pl.pallas_call(
        functools.partial(attend_back_kernel, pairs, HEAD**-0.5),
        in_specs=[pl.BlockSpec(memory_space=pltpu.SMEM), vm, vm, vm, vm],
        out_specs=[vm, vm],
        out_shape=[jax.ShapeDtypeStruct(qkv.shape, bf), jax.ShapeDtypeStruct(lines.shape, f32)],
        scratch_shapes=[
            pltpu.VMEM(square, f32),
            pltpu.VMEM(square, f32),
            pltpu.VMEM(square, bf),
            pltpu.VMEM((2, BLOCK, 2 * length), f32),
        ],
        compiler_params=pltpu.CompilerParams(vmem_limit_bytes=40 * 2**20),
        cost_estimate=pl.CostEstimate(
            flops=20 * items * length * length * width,
            bytes_accessed=items * length * width * 20,
            transcendentals=items * length * length * width // HEAD,
        ),
        name="attend_back",
    )(lengths, lines, qkv, lse, dmixed)


def split_features(features):
    whole = features // LANES * LANES
    return whole, features - whole


def tile_count(features):
    whole, rest = split_features(features)
    return whole // LANES + (rest > 0)


def first_of_pair(packed, features):
    return packed[..., :features]


def second_of_pair(packed, features):
    whole, rest = split_features(features)
    tail = packed[..., features : features + rest]
    return jnp.concatenate([packed[..., features + rest :], tail], axis=-1) if whole else tail


def pack_pair(first, second):
    whole, _ = split_features(first.shape[-1])
    parts = [first, second[..., whole:], second[..., :whole]] if whole else [first, second]
    return jnp.concatenate(parts, axis=-1)


def packed_starts(features, half):
    whole, rest = split_features(features)
    base = 0 if half == 0 else features + rest
    return [base + low for low in range(0, whole, LANES)] + ([whole] if rest else [])


def gather_kernel(features, load_steps, batch, table_ref, ids_ref, out_ref, *scratch):
    step = pl.program_id(0)
    width = table_ref.shape[1]
    tiles = tile_count(features)
    whole, rest = split_features(features)
    stash = scratch[:tiles]
    rows = [scratch[tiles : 2 * tiles], scratch[2 * tiles :]]

    @pl.when(step < load_steps)
    def _():
        base = pl.multiple_of(step * width, width)
        for tile in range(tiles):
            low = tile * LANES
            part = table_ref[low : min(features, low + LANES), :].astype(bf).astype(f32)
            if low == whole:
                blank = [jnp.zeros((LANES - 2 * rest, width), f32)] if 2 * rest < LANES else []
                part = jnp.concatenate([part, part, *blank], axis=0)
            stash[tile][pl.ds(base, width), :] = part.T

    @pl.when(step >= load_steps)
    def _():
        count = out_ref.shape[0]
        for half in range(2):
            def take(index, carry):
                start = pl.multiple_of(index * batch, batch)
                tokens = [ids_ref[0, half, start + inner] for inner in range(batch)]
                for tile in range(tiles):
                    for inner in range(batch):
                        rows[half][tile][pl.ds(start + inner, 1), :] = stash[tile][pl.ds(tokens[inner], 1), :]
                return carry
            lax.fori_loop(0, count // batch, take, 0, unroll=2)
        for half in range(2):
            for tile in range(whole // LANES):
                low = packed_starts(features, half)[tile]
                out_ref[:, low : low + LANES] = rows[half][tile][...].astype(bf)
        if rest:
            lane = lax.broadcasted_iota(jnp.int32, (1, LANES), 1)
            shared = jnp.where(lane < rest, rows[0][-1][...], rows[1][-1][...]).astype(bf)
            out_ref[:, whole : whole + 2 * rest] = shared[:, : 2 * rest]


def gather_rows(table, ids, width=4096, batch=16):
    features, vocab = table.shape
    steps, _, chunk = ids.shape
    tiles = tile_count(features)
    load_steps = pl.cdiv(vocab, width)
    return pl.pallas_call(
        functools.partial(gather_kernel, features, load_steps, batch),
        grid=(load_steps + steps,),
        in_specs=[
            pl.BlockSpec((features, width), lambda s: (0, jnp.minimum(s, load_steps - 1))),
            pl.BlockSpec((1, 2, chunk), lambda s: (jnp.maximum(s - load_steps, 0), 0, 0), memory_space=pltpu.SMEM),
        ],
        out_specs=pl.BlockSpec((chunk, 2 * features), lambda s: (jnp.maximum(s - load_steps, 0), 0)),
        out_shape=jax.ShapeDtypeStruct((steps * chunk, 2 * features), bf),
        scratch_shapes=[pltpu.VMEM((load_steps * width, LANES), f32)] * tiles + [pltpu.VMEM((chunk, LANES), f32)] * (2 * tiles),
        compiler_params=pltpu.CompilerParams(vmem_limit_bytes=60 * 2**20),
        cost_estimate=pl.CostEstimate(flops=0, bytes_accessed=80 * 2**20, transcendentals=0),
        name="gather_rows",
    )(table, ids)


def stage_ids_kernel(batch, order, place_ref, ids_ref, out_ref, flags_ref, flat):
    lane = lax.broadcasted_iota(jnp.int32, (1, LANES), 1)
    count, _, chunk = ids_ref.shape[2:]
    flat[...] = jnp.zeros_like(flat)
    for at, (slot, other) in enumerate(order):
        core = lax.rem(place_ref[0] + other, ids_ref.shape[0])
        for step in range(count):
            index = at * count + step
            ids = ids_ref[core, place_ref[1 + slot], step]
            out_ref[index] = ids
            flat[2 * index : 2 * index + 2, :] = ids
    flags = jnp.zeros((flat.shape[0], LANES), jnp.int32)
    for block in range(chunk // LANES):
        part = flat[:, block * LANES : (block + 1) * LANES]
        found = jnp.zeros(part.shape, jnp.int32)
        for shift in range(1, batch):
            again = (part == pltpu.roll(part, shift, 1)) & (lane % batch >= shift)
            found = jnp.where(again, 1, found)
        flags = jnp.where(lane == block, jnp.max(found, axis=1, keepdims=True), flags)
    for index in range(out_ref.shape[0]):
        flags_ref[index] = flags[2 * index : 2 * index + 2]


def stage_ids(place, ids, order, batch=4):
    *_, count, _, chunk = ids.shape
    vm = pl.BlockSpec(memory_space=pltpu.VMEM)
    total = len(order) * count
    return pl.pallas_call(
        functools.partial(stage_ids_kernel, batch, order),
        in_specs=[pl.BlockSpec(memory_space=pltpu.SMEM), vm],
        out_specs=[vm, vm],
        out_shape=[
            jax.ShapeDtypeStruct((total, 2, chunk), jnp.int32),
            jax.ShapeDtypeStruct((total, 2, LANES), jnp.int32),
        ],
        scratch_shapes=[pltpu.VMEM((2 * total + -2 * total % 8, chunk), jnp.int32)],
        name="stage_ids",
    )(place, ids)


def spread_rows(features, rows_ref, summed):
    whole, rest = split_features(features)
    lane = lax.broadcasted_iota(jnp.int32, (1, LANES), 1)
    for half in range(2):
        for tile, start in enumerate(packed_starts(features, half)):
            if start == whole:
                part = rows_ref[:, start : start + 2 * rest].astype(f32)
                if 2 * rest < LANES:
                    part = jnp.concatenate([part, jnp.zeros((part.shape[0], LANES - 2 * rest), f32)], axis=1)
                mine = lane < rest if half == 0 else (lane >= rest) & (lane < 2 * rest)
                part = jnp.where(mine, part, 0.0)
            else:
                part = rows_ref[:, start : start + LANES].astype(f32)
            summed[half][tile][...] = part


def merge_rows(batch, ids_row_ref, flags_ref, summed):
    count = summed[0][0].shape[0]
    for half in range(2):
        for at in range(count // LANES):
            block = slice(at * LANES, (at + 1) * LANES)

            @pl.when(flags_ref[0, half, at] > 0)
            def _():
                place = lax.broadcasted_iota(jnp.int32, (LANES, LANES), 0) // batch
                same_batch = place == lax.broadcasted_iota(jnp.int32, (LANES, LANES), 1) // batch
                across = jnp.broadcast_to(ids_row_ref[0, half : half + 1, block], (LANES, LANES))
                match = jnp.where((across == across.T) & same_batch, 1.0, 0.0).astype(bf)
                for rows in summed[half]:
                    rows[block, :] = jnp.dot(match, rows[block, :].astype(bf), preferred_element_type=f32)


def add_rows(batch, ids_ref, totals, summed):
    count = summed[0][0].shape[0]

    def add(index, carry):
        start = pl.multiple_of(index * batch, batch)
        for half in range(2):
            tokens = [ids_ref[0, half, start + inner] for inner in range(batch)]
            fresh = [
                [total[pl.ds(tokens[inner], 1), :] + rows[pl.ds(start + inner, 1), :] for inner in range(batch)]
                for total, rows in zip(totals, summed[half])
            ]
            for total, new in zip(totals, fresh):
                for inner in range(batch):
                    total[pl.ds(tokens[inner], 1), :] = new[inner]
        return carry

    lax.fori_loop(0, count // batch, add, 0, unroll=4)


def table_columns(features, totals, base, width):
    whole, rest = split_features(features)
    pieces = [total[pl.ds(base, width), :].T for total in totals]
    if rest:
        pieces[-1] = pieces[-1][:rest] + pieces[-1][rest : 2 * rest]
    return pieces


class Stage:
    def __init__(self, segments, choices, ids, flags, first, blocks, features):
        self.first = first
        first = first * blocks
        self.arrays = [array for candidates in segments for array in candidates]
        self.segments = [len(candidates) for candidates in segments]
        self.chunk = ids.shape[2]
        self.each = segments[0][0].shape[0] // self.chunk
        self.steps = self.each * len(segments)
        self.operands = [choices, ids, ids, flags, *self.arrays]
        at = lambda s: first + jnp.minimum(s, self.steps - 1)
        self.in_specs = [
            pl.BlockSpec(memory_space=pltpu.SMEM),
            pl.BlockSpec((1, 2, self.chunk), lambda s: (at(s), 0, 0), memory_space=pltpu.SMEM),
            pl.BlockSpec((1, 2, self.chunk), lambda s: (at(s), 0, 0)),
            pl.BlockSpec((1, 2, LANES), lambda s: (at(s), 0, 0), memory_space=pltpu.SMEM),
        ]
        for segment, candidates in enumerate(segments):
            for _ in candidates:
                low = segment * self.each
                self.in_specs.append(
                    pl.BlockSpec(
                        (self.chunk, 2 * features), lambda s, low=low: (jnp.clip(s - low, 0, self.each - 1), 0)
                    )
                )
        self.features = features

    def scratch(self, vocab):
        tiles = tile_count(self.features)
        return [pltpu.VMEM((vocab, LANES), f32)] * tiles + [pltpu.VMEM((self.chunk, LANES), f32)] * (2 * tiles)

    def add(self, batch, refs, scratch):
        choice_ref, ids_ref, ids_row_ref, flags_ref, *rows_refs = refs
        step = pl.program_id(0)
        tiles = tile_count(self.features)
        totals = scratch[:tiles]
        summed = [scratch[tiles : 2 * tiles], scratch[2 * tiles :]]

        @pl.when(step == 0)
        def _():
            for total in totals:
                total[...] = jnp.zeros_like(total)

        for segment, candidates in enumerate(self.segments):
            now = (step >= segment * self.each) & (step < (segment + 1) * self.each)
            for candidate in range(candidates):
                rows_ref, rows_refs = rows_refs[0], rows_refs[1:]

                @pl.when(now & (choice_ref[self.first + segment] == candidate))
                def _():
                    spread_rows(self.features, rows_ref, summed)

        @pl.when(step < self.steps)
        def _():
            merge_rows(batch, ids_row_ref, flags_ref, summed)
            add_rows(batch, ids_ref, totals, summed)

        return totals


def scatter_kernel(stage, batch, dense, *refs):
    count = len(stage.operands)
    dense_refs = refs[count : count + dense]
    out_ref = refs[count + dense]
    totals = stage.add(batch, refs[:count], refs[count + dense + 1 :])
    step = pl.program_id(0)
    width = out_ref.shape[1]

    @pl.when(step >= stage.steps)
    def _():
        base = pl.multiple_of((step - stage.steps) * width, width)
        low = 0
        for piece in table_columns(stage.features, totals, base, width):
            cut = slice(low, low + piece.shape[0])
            low += piece.shape[0]
            for dense_ref in dense_refs:
                piece = piece + dense_ref[cut, :].astype(f32)
            out_ref[cut, :] = piece.astype(bf)


def scatter_rows(stage, vocab, dense=(), width=2048, batch=4):
    flush = pl.cdiv(vocab, width)
    block = pl.BlockSpec((stage.features, width), lambda s: (0, jnp.maximum(s - stage.steps, 0)))
    return pl.pallas_call(
        functools.partial(scatter_kernel, stage, batch, len(dense)),
        grid=(stage.steps + flush,),
        in_specs=stage.in_specs + [block] * len(dense),
        out_specs=block,
        out_shape=jax.ShapeDtypeStruct((stage.features, vocab), bf),
        scratch_shapes=stage.scratch(flush * width),
        compiler_params=pltpu.CompilerParams(vmem_limit_bytes=127 * 2**19),
        cost_estimate=pl.CostEstimate(flops=0, bytes_accessed=100 * 2**20, transcendentals=0),
        name="scatter_rows",
    )(*stage.operands, *dense)


def assemble_kernel(features, spread_ref, gain_ref, embedded_ref, normed_ref):
    for half, take in enumerate((first_of_pair, second_of_pair)):
        row = jnp.concatenate([take(spread_ref[part], features) for part in range(spread_ref.shape[0])], axis=1)
        embedded_ref[half] = row
        stream = row.astype(f32)
        scale = lax.rsqrt(jnp.mean(stream * stream, axis=1, keepdims=True) + NORM_EPS)
        normed_ref[half] = (stream * scale * gain_ref[...]).astype(bf)


def assemble(spread, gain, block=128):
    parts, count, features = spread.shape
    features //= 2
    width = parts * features
    block = min(block, count)
    out = jax.ShapeDtypeStruct((2, count, width), bf)
    whole_block = pl.BlockSpec((2, block, width), lambda s: (0, s, 0))
    embedded, normed = pl.pallas_call(
        functools.partial(assemble_kernel, features),
        grid=(count // block,),
        in_specs=[
            pl.BlockSpec((parts, block, 2 * features), lambda s: (0, s, 0)),
            pl.BlockSpec((1, width), lambda s: (0, 0)),
        ],
        out_specs=[whole_block, whole_block],
        out_shape=[out, out],
        compiler_params=pltpu.CompilerParams(vmem_limit_bytes=30 * 2**20),
        name="assemble",
    )(spread, gain.reshape(1, width))
    return embedded.reshape(2 * count, width), normed.reshape(2 * count, width)


def pack_back_kernel(features, back_ref, embedded_ref, passed_ref, gain_ref, packed_ref, grad_gain_ref):
    gain = gain_ref[...]
    halves = []
    grad_gain = jnp.zeros_like(gain)
    for half in range(2):
        stream = embedded_ref[half].astype(f32)
        back = back_ref[half]
        scale = lax.rsqrt(jnp.mean(stream * stream, axis=1, keepdims=True) + NORM_EPS)
        unit = stream * scale
        grad_gain += jnp.sum(back * unit, axis=0, keepdims=True)
        pulled = back * gain
        along = jnp.mean(pulled * unit, axis=1, keepdims=True)
        halves.append((passed_ref[half] + scale * (pulled - unit * along)).astype(bf))
    for part in range(packed_ref.shape[0]):
        cut = slice(part * features, (part + 1) * features)
        packed_ref[part] = pack_pair(halves[0][:, cut], halves[1][:, cut])

    @pl.when(pl.program_id(0) == 0)
    def _():
        grad_gain_ref[...] = jnp.zeros_like(grad_gain_ref)

    grad_gain_ref[...] += grad_gain


def pack_back(back, embedded, passed, gain, features, block=128):
    rows, width = back.shape
    count, parts = rows // 2, width // features
    block = min(block, count)
    pair = pl.BlockSpec((2, block, width), lambda s: (0, s, 0))
    line = pl.BlockSpec((1, width), lambda s: (0, 0))
    packed, grad_gain = pl.pallas_call(
        functools.partial(pack_back_kernel, features),
        grid=(count // block,),
        in_specs=[pair, pair, pair, line],
        out_specs=[pl.BlockSpec((parts, block, 2 * features), lambda s: (0, s, 0)), line],
        out_shape=[jax.ShapeDtypeStruct((parts, count, 2 * features), bf), jax.ShapeDtypeStruct((1, width), f32)],
        compiler_params=pltpu.CompilerParams(vmem_limit_bytes=30 * 2**20),
        name="pack_back",
    )(back.reshape(2, count, width), embedded.reshape(2, count, width), passed.reshape(2, count, width), gain.reshape(1, width))
    return packed, grad_gain[0]


def finish_kernel(stage, vocab, batch, dense, *refs):
    count = len(stage.operands)
    weight_ref, first_ref, second_ref, *dense_refs = refs[count : count + 3 + dense]
    refs, scratch = refs[: count + 7 + dense], refs[count + 7 + dense :]
    momentum_ref, variance_ref, direction_ref, squares_ref = refs[-4:]
    totals = stage.add(batch, refs[:count], scratch)
    step = pl.program_id(0)

    @pl.when(step == 0)
    def _():
        squares_ref[...] = jnp.zeros_like(squares_ref)

    @pl.when(step >= stage.steps)
    def _():
        width = weight_ref.shape[1]
        base = pl.multiple_of((step - stage.steps) * width, width)
        inside = base + lax.broadcasted_iota(jnp.int32, (1, width), 1) < vocab
        low = 0
        for piece in table_columns(stage.features, totals, base, width):
            cut = slice(low, low + piece.shape[0])
            low += piece.shape[0]
            weight = weight_ref[cut, :]
            gradient = piece
            for dense_ref in dense_refs:
                gradient = gradient + dense_ref[cut, :].astype(f32)
            momentum, variance, direction = lamb_direction(weight, gradient, first_ref[cut, :], second_ref[cut, :])
            momentum_ref[cut, :] = momentum
            variance_ref[cut, :] = variance
            direction_ref[cut, :] = direction.astype(bf)
            for line, value in enumerate((weight, direction)):
                value = jnp.where(inside, value, 0.0)
                squares_ref[line : line + 1, :] += jnp.sum(value * value, axis=0, keepdims=True)


def finish(stage, weight, first, second, dense, width=1024, batch=4, mode=None):
    features, vocab = weight.shape
    columns = pl.cdiv(vocab, width)
    block = pl.BlockSpec((features, width), lambda s: (0, jnp.maximum(s - stage.steps, 0)))
    ahead = pl.BlockSpec(block.block_shape, block.index_map, pipeline_mode=mode)
    full = jax.ShapeDtypeStruct(weight.shape, f32)
    return pl.pallas_call(
        functools.partial(finish_kernel, stage, vocab, batch, len(dense)),
        grid=(stage.steps + columns,),
        in_specs=stage.in_specs + [ahead] * (3 + len(dense)),
        out_specs=[block, block, block, pl.BlockSpec((8, width), lambda s: (0, 0))],
        out_shape=[full, full, jax.ShapeDtypeStruct(weight.shape, bf), jax.ShapeDtypeStruct((8, width), f32)],
        scratch_shapes=stage.scratch(columns * width),
        compiler_params=pltpu.CompilerParams(vmem_limit_bytes=127 * 2**19),
        cost_estimate=pl.CostEstimate(flops=0, bytes_accessed=300 * 2**20, transcendentals=0),
        name="finish",
    )(*stage.operands, weight, first, second, *dense)


MESH = pl.DeviceIdType.MESH


def exchange(value_ref, out_ref, mine, peers, send, received, slot):
    copies = []
    for peer in peers:
        copy = pltpu.make_async_remote_copy(
            src_ref=value_ref,
            dst_ref=out_ref.at[mine],
            send_sem=send.at[slot],
            recv_sem=received.at[slot],
            device_id=peer,
            device_id_type=MESH,
        )
        copy.start()
        copies.append(copy)
        slot += 1
    return copies


def line_peers(axis):
    place, size = lax.axis_index(axis), lax.axis_size(axis)
    return place, [{axis: lax.rem(place + step, size)} for step in range(1, size)]


def plane_peers(axes):
    places = [lax.axis_index(axis) for axis in axes]
    sizes = [lax.axis_size(axis) for axis in axes]
    count = sizes[0] * sizes[1]
    mine = places[0] * sizes[1] + places[1]
    peers = []
    for step in range(1, count):
        peer = lax.rem(mine + step, count)
        peers.append({axes[0]: peer // sizes[1], axes[1]: lax.rem(peer, sizes[1])})
    return mine, peers


def greet(peers):
    barrier = pltpu.get_barrier_semaphore()
    for peer in peers:
        pl.semaphore_signal(barrier, inc=1, device_id=peer, device_id_type=MESH)
    pl.semaphore_wait(barrier, len(peers))


def share_kernel(axis, value_ref, out_ref, send, received):
    mine, peers = line_peers(axis)
    greet(peers)
    out_ref[mine] = value_ref[...]
    for copy in exchange(value_ref, out_ref, mine, peers, send, received, 0):
        copy.wait()


def share(value, axis, size):
    return pl.pallas_call(
        functools.partial(share_kernel, axis),
        in_specs=[pl.BlockSpec(memory_space=pltpu.VMEM)],
        out_specs=pl.BlockSpec(memory_space=pltpu.VMEM),
        out_shape=jax.ShapeDtypeStruct((size, *value.shape), value.dtype),
        scratch_shapes=[pltpu.SemaphoreType.DMA((size - 1,)), pltpu.SemaphoreType.DMA((size - 1,))],
        compiler_params=pltpu.CompilerParams(collective_id=0, has_side_effects=True),
        name="share",
    )(value)


def sum_squares_kernel(axes, rows_ref, table_ref, out_ref, slots, send, received):
    places = [lax.axis_index(axis) for axis in axes]
    sizes = [lax.axis_size(axis) for axis in axes]
    count = sizes[0] * sizes[1]
    mine = places[0] * sizes[1] + places[1]
    barrier = pltpu.get_barrier_semaphore()
    peers = []
    for step in range(1, count):
        peer = lax.rem(mine + step, count)
        peers.append({axes[0]: peer // sizes[1], axes[1]: lax.rem(peer, sizes[1])})
    for peer in peers:
        pl.semaphore_signal(barrier, inc=1, device_id=peer, device_id_type=MESH)
    pl.semaphore_wait(barrier, count - 1)
    lane = lax.broadcasted_iota(jnp.int32, (1, LANES), 1)
    sums = jnp.sum(rows_ref[...], axis=1, keepdims=True)
    slots[mine] = table_ref[...]
    slots[mine, 0:1, :] = jnp.where(lane == 0, sums[0:1], jnp.where(lane == 1, sums[1:2], 0.0)) * table_ref[0:1, :]
    copies = []
    for step, peer in enumerate(peers):
        copy = pltpu.make_async_remote_copy(
            src_ref=slots.at[mine],
            dst_ref=slots.at[mine],
            send_sem=send.at[step],
            recv_sem=received.at[step],
            device_id=peer,
            device_id_type=MESH,
        )
        copy.start()
        copies.append(copy)
    for copy in copies:
        copy.wait()
    total = slots[0]
    for other in range(1, count):
        total = total + slots[other]
    out_ref[...] = total


def sum_over(rows, table, axes, sizes):
    count = sizes[0] * sizes[1]
    return pl.pallas_call(
        functools.partial(sum_squares_kernel, axes),
        in_specs=[pl.BlockSpec(memory_space=pltpu.VMEM)] * 2,
        out_specs=pl.BlockSpec(memory_space=pltpu.VMEM),
        out_shape=jax.ShapeDtypeStruct(table.shape, f32),
        scratch_shapes=[
            pltpu.VMEM((count, *table.shape), f32),
            pltpu.SemaphoreType.DMA((count - 1,)),
            pltpu.SemaphoreType.DMA((count - 1,)),
        ],
        compiler_params=pltpu.CompilerParams(collective_id=1, has_side_effects=True),
        name="sum_over",
    )(rows, table)


def sum_all_kernel(near, far, value_ref, out_ref, near_slots, far_slots, send, received):
    places = [lax.axis_index(axis) for axis in (*near, far)]
    sizes = [lax.axis_size(axis) for axis in (*near, far)]
    count = sizes[0] * sizes[1]
    mine = places[0] * sizes[1] + places[1]
    barrier = pltpu.get_barrier_semaphore()
    plane, line = [], []
    for step in range(1, count):
        peer = lax.rem(mine + step, count)
        plane.append({near[0]: peer // sizes[1], near[1]: lax.rem(peer, sizes[1])})
    for step in range(1, sizes[2]):
        line.append({far: lax.rem(places[2] + step, sizes[2])})
    for peer in plane + line:
        pl.semaphore_signal(barrier, inc=1, device_id=peer, device_id_type=MESH)
    pl.semaphore_wait(barrier, len(plane) + len(line))
    slot = 0
    value = value_ref[...]
    for peers, slots, at in ((plane, near_slots, mine), (line, far_slots, places[2])):
        slots[at] = value
        copies = []
        for peer in peers:
            copy = pltpu.make_async_remote_copy(
                src_ref=slots.at[at],
                dst_ref=slots.at[at],
                send_sem=send.at[slot],
                recv_sem=received.at[slot],
                device_id=peer,
                device_id_type=MESH,
            )
            copy.start()
            copies.append(copy)
            slot += 1
        for copy in copies:
            copy.wait()
        value = slots[0]
        for other in range(1, slots.shape[0]):
            value = value + slots[other]
    out_ref[...] = value


def sum_all(value, near, far, sizes):
    count = sizes[0] * sizes[1]
    slots = count - 1 + sizes[2] - 1
    return pl.pallas_call(
        functools.partial(sum_all_kernel, near, far),
        in_specs=[pl.BlockSpec(memory_space=pltpu.VMEM)],
        out_specs=pl.BlockSpec(memory_space=pltpu.VMEM),
        out_shape=jax.ShapeDtypeStruct(value.shape, f32),
        scratch_shapes=[
            pltpu.VMEM((count, *value.shape), f32),
            pltpu.VMEM((sizes[2], *value.shape), f32),
            pltpu.SemaphoreType.DMA((slots,)),
            pltpu.SemaphoreType.DMA((slots,)),
        ],
        compiler_params=pltpu.CompilerParams(collective_id=2, has_side_effects=True),
        name="sum_all",
    )(value)


def share_both_kernel(plane, line, vectors_ref, ids_ref, all_vectors_ref, all_ids_ref, send, received):
    mine, near = plane_peers(plane)
    place, far = line_peers(line)
    greet(near + far)
    all_vectors_ref[mine] = vectors_ref[...]
    all_ids_ref[place] = ids_ref[...]
    copies = exchange(vectors_ref, all_vectors_ref, mine, near, send, received, 0)
    copies += exchange(ids_ref, all_ids_ref, place, far, send, received, len(near))
    for copy in copies:
        copy.wait()


def share_both(vectors, ids, plane, line, sizes):
    count = sizes[0] * sizes[1]
    slots = count - 1 + sizes[2] - 1
    vm = pl.BlockSpec(memory_space=pltpu.VMEM)
    return pl.pallas_call(
        functools.partial(share_both_kernel, plane, line),
        in_specs=[vm, vm],
        out_specs=[vm, vm],
        out_shape=[
            jax.ShapeDtypeStruct((count, *vectors.shape), vectors.dtype),
            jax.ShapeDtypeStruct((sizes[2], *ids.shape), ids.dtype),
        ],
        scratch_shapes=[pltpu.SemaphoreType.DMA((slots,)), pltpu.SemaphoreType.DMA((slots,))],
        compiler_params=pltpu.CompilerParams(collective_id=3, has_side_effects=True),
        name="share_both",
    )(vectors, ids)


def lamb_direction(weight, gradient, moment_one, moment_two):
    momentum = BETA_ONE * moment_one + (1.0 - BETA_ONE) * gradient
    variance = BETA_TWO * moment_two + (1.0 - BETA_TWO) * gradient * gradient
    direction = (
        momentum / (1.0 - BETA_ONE**STEP) / (jnp.sqrt(variance / (1.0 - BETA_TWO**STEP)) + ADAM_EPS)
        + WEIGHT_DECAY * weight
    )
    return (momentum, variance, direction)


def total_of(value):
    while value.ndim > 2:
        value = jnp.sum(value, axis=1)
    return jnp.sum(jnp.sum(value, axis=1, keepdims=True), axis=0, keepdims=True)


def small_moments_kernel(live_ref, ffn_ref, rest_ref, small_ref, *refs):
    inputs, outputs, squares_ref, loss_ref = refs[:18], refs[18:-2], refs[-2], refs[-1]
    parts, _, width = inputs[0].shape
    half = ffn_ref.shape[1] // 2
    heads, buckets = inputs[12].shape
    gains, model = inputs[15].shape
    lines = model // LANES
    first_mdl, first_dat = lax.axis_index("mdl") == 0, lax.axis_index("dat") == 0

    def bias_gradient():
        start = gains * lines
        own = [small_ref[start + core * heads : start + (core + 1) * heads, :buckets] for core in range(HEADS // heads)]
        return functools.reduce(
            lambda kept, at: jnp.where(lax.axis_index("mdl") == at, own[at], kept), range(1, len(own)), own[0]
        )

    def gain_gradient():
        rows = [[small_ref[gain * lines + at : gain * lines + at + 1, :] for at in range(lines)] for gain in range(gains)]
        return jnp.concatenate([jnp.concatenate(row, axis=1) for row in rows], axis=0)

    gradient_of = (
        lambda: jnp.stack([rest_ref[:, part * width : (part + 1) * width] for part in range(parts)]),
        lambda: rest_ref[:, parts * width :],
        lambda: ffn_ref[:, half:],
        lambda: ffn_ref[:, :half],
        bias_gradient,
        gain_gradient,
    )
    lane = lax.broadcasted_iota(jnp.int32, (1, LANES), 1)
    counted = [first_mdl, True, True, True, True, first_dat] + [first_mdl & first_dat] * 3

    @pl.when(pl.program_id(0) == 0)
    def _():
        squares_ref[...] = jnp.zeros_like(squares_ref)
        squares_ref[0:1, :] = jnp.where(counted[0], jnp.ones((1, LANES), f32), 0.0)
        loss_line = gains * lines + HEADS
        loss_ref[0] = jnp.max(small_ref[loss_line : loss_line + 1, :])
        loss_ref[1] = live_ref[0]

    def update(place):
        weight_ref, first_ref, second_ref = inputs[3 * place : 3 * place + 3]
        weight = weight_ref[...]
        results = lamb_direction(weight, gradient_of[place]().astype(f32), first_ref[...], second_ref[...])
        for ref, value in zip(outputs[3 * place : 3 * place + 3], results):
            ref[...] = value
        return weight * weight, results[2] * results[2]

    def add(line, weight_square, direction_square):
        both = jnp.where(lane == 0, weight_square, jnp.where(lane == 1, direction_square, 0.0))
        squares_ref[line : line + 1, :] += jnp.where(counted[line], both, 0.0)

    for place in range(4):
        weight_square, direction_square = update(place)
        add(place + 1, total_of(weight_square), total_of(direction_square))

    @pl.when(pl.program_id(0) == 0)
    def _():
        weight_square, direction_square = update(4)
        add(5, total_of(weight_square), total_of(direction_square))
        weight_square, direction_square = update(5)
        for row in range(weight_square.shape[0]):
            add(6 + row, total_of(weight_square[row : row + 1]), total_of(direction_square[row : row + 1]))


def row_block(value, steps):
    if value.ndim == 3:
        return pl.BlockSpec((value.shape[0], value.shape[1] // steps, value.shape[2]), lambda s: (0, s, 0))
    return pl.BlockSpec((value.shape[0] // steps, value.shape[1]), lambda s: (s, 0))


def whole_block(value):
    return pl.BlockSpec(value.shape, lambda s: (0,) * value.ndim)


def small_moments(live_total, weights, gradients, moments, steps):
    operands = [live_total.reshape(1), *gradients]
    scalars = pl.BlockSpec(memory_space=pltpu.SMEM)
    in_specs = [scalars] + [row_block(value, steps) for value in gradients[:2]] + [whole_block(gradients[2])]
    out_specs, out_shape = [], []
    for place, (weight, states) in enumerate(zip(weights, moments)):
        spec = row_block(weight, steps) if place < 4 else whole_block(weight)
        operands += [weight, *states]
        in_specs += [spec] * 3
        out_specs += [spec] * 3
        out_shape += [jax.ShapeDtypeStruct(weight.shape, f32)] * 3
    return pl.pallas_call(
        small_moments_kernel,
        grid=(steps,),
        in_specs=in_specs,
        out_specs=out_specs + [pl.BlockSpec((16, LANES), lambda s: (0, 0)), scalars],
        out_shape=out_shape + [jax.ShapeDtypeStruct((16, LANES), f32), jax.ShapeDtypeStruct((2,), f32)],
        compiler_params=pltpu.CompilerParams(vmem_limit_bytes=127 * 2**19),
        name="small_moments",
    )(*operands)


def update_all_kernel(squares_ref, *refs):
    norms = jnp.sqrt(squares_ref[...])
    rates = LEARN_RATE * norms[:, 0:1] / norms[:, 1:2]
    count = len(refs) // 3
    norms_ref = refs[-1]
    norms_ref[...] = norms[: norms_ref.shape[0], :2]
    for place in range(count):
        weight_ref, direction_ref, updated_ref = refs[2 * place], refs[2 * place + 1], refs[2 * count + place]
        rate = rates[6:9] if place == 6 else rates[place : place + 1]
        weight = weight_ref[...]
        if weight.ndim == 3:
            rate = rate[:, :, None]
        updated_ref[...] = weight - rate * direction_ref[...].astype(f32)


def update_all(squares, weights, directions, steps):
    operands, in_specs, out_specs, out_shape = [squares], [whole_block(squares)], [], []
    for place, (weight, direction) in enumerate(zip(weights, directions)):
        spec = row_block(weight, steps) if place < 5 else whole_block(weight)
        operands += [weight, direction]
        in_specs += [spec] * 2
        out_specs += [spec]
        out_shape += [jax.ShapeDtypeStruct(weight.shape, f32)]
    return pl.pallas_call(
        update_all_kernel,
        grid=(steps,),
        in_specs=in_specs,
        out_specs=out_specs + [pl.BlockSpec((9, 2), lambda s: (0, 0))],
        out_shape=out_shape + [jax.ShapeDtypeStruct((9, 2), f32)],
        compiler_params=pltpu.CompilerParams(vmem_limit_bytes=127 * 2**19),
        name="update_all",
    )(*operands)


def norm_scale(stream, gain_row):
    return (
        stream * lax.rsqrt(jnp.mean(stream * stream, axis=-1, keepdims=True) + NORM_EPS) * gain_row
    )


def gelu_tanh(pre_act):
    return jax.nn.gelu(pre_act, approximate=True)


def dot(left, right, dims=((1,), (0,))):
    return lax.dot_general(left, right, (dims, ((), ())), preferred_element_type=f32)


def bucket_onehot(length):
    relative = length - jnp.arange(2 * length, dtype=jnp.int32)
    distance = jnp.abs(relative)
    far_bucket = 8 + sum(((distance >= threshold).astype(jnp.int32) for threshold in BUCKET_EDGES))
    bucket = jnp.where(distance < 8, distance, far_bucket) + jnp.where(relative > 0, 16, 0)
    return (bucket[:, None] == jnp.arange(BUCKETS)).astype(f32)


def after(value, *others):
    return lax.optimization_barrier((value, *others))[0]


def arrivals(groups):
    found = []
    for group in range(groups):
        found.append([])
        for hop in range(1, groups):
            for source, way in ((group - hop, 0), (group + hop, 1)):
                if 0 <= source < groups:
                    found[-1].append((source, way, hop))
    return found


def swap_cores(value):
    size = lax.axis_size("mdl")
    return lax.ppermute(value, "mdl", [(core, (core + 1) % size) for core in range(size)])


def shards(
    token_ids,
    item_lengths,
    prefix_lengths,
    group_live,
    partner,
    embedding,
    qkv_weight,
    out_weight,
    up_weight,
    down_weight,
    bias_table,
    norm_gains,
    embedding_first,
    embedding_second,
    qkv_first,
    qkv_second,
    out_first,
    out_second,
    up_first,
    up_second,
    down_first,
    down_second,
    bias_first,
    bias_second,
    gains_first,
    gains_second,
):
    item_count, length = token_ids.shape
    features, vocab = embedding.shape
    grp_size, dat_size, mdl_size = lax.axis_size("grp"), lax.axis_size("dat"), lax.axis_size("mdl")
    group_index, dat_index, mdl_index = lax.axis_index("grp"), lax.axis_index("dat"), lax.axis_index("mdl")
    mine = item_count // mdl_size
    rows = mine * length
    pair_rows = rows // 2
    chunk = min(512, pair_rows)
    chunks = pair_rows // chunk
    group_items = item_count * dat_size
    width = features * dat_size
    first_slot = dat_index * item_count + mdl_index * mine

    tn = ((0,), (0,))
    nt = ((1,), (1,))

    group_ids = share(token_ids, "dat", dat_size)

    def of_core(table, core):
        return lax.dynamic_index_in_dim(table, core % mdl_size, 0, keepdims=False)

    def by_core(ids):
        lead = ids.shape[:-3]
        ids = ids.reshape(-1, dat_size, mdl_size, 2, chunks, chunk).transpose(2, 0, 1, 4, 3, 5)
        return ids.reshape(mdl_size, *lead, dat_size * chunks, 2, chunk)

    def gathered(*shards):
        return lax.all_gather(
            jnp.concatenate([shard.astype(bf) for shard in shards], axis=1), "dat", axis=0, tiled=True
        )

    def halves(own, *widths):
        both = (own, swap_cores(own))
        edges = [0]
        for part in widths:
            edges.append(edges[-1] + part)
        return [[part[:, low:high] for part in both] for low, high in zip(edges, edges[1:])]

    flat_qkv = qkv_weight.reshape(features, -1)
    first_own = gathered(flat_qkv, out_weight.T)
    onehot = bucket_onehot(length)
    line_halves = [
        jnp.einsum("rb,bh->hr", onehot, table, precision=MAX_PRECISION)
        for table in (bias_table, swap_cores(bias_table))
    ]

    looked_up = gather_rows(embedding, of_core(by_core(group_ids), mdl_index))
    spread = lax.all_to_all(
        looked_up.reshape(dat_size, pair_rows, 2 * features), "dat", split_axis=0, concat_axis=0, tiled=True
    )
    second_own = gathered(after(up_weight, looked_up), after(down_weight, looked_up))
    item_lengths, prefix_lengths, partner = after((item_lengths, prefix_lengths, partner), looked_up)
    my_lengths, my_prefixes, my_partner = [
        lax.dynamic_slice_in_dim(value, mdl_index * mine, mine) for value in (item_lengths, prefix_lengths, partner)
    ]
    embedded_low, normed_one = assemble(spread, norm_gains[0])
    embedded = embedded_low.astype(f32)
    qkv_halves, out_halves = halves(after(first_own, spread), flat_qkv.shape[1], out_weight.shape[0])
    qkv_rows = [dot(normed_one, weight).astype(bf).reshape(mine, length, -1) for weight in qkv_halves]
    mixed, log_totals = zip(*[attend(item_qkv, lines, my_lengths) for item_qkv, lines in zip(qkv_rows, line_halves)])
    mixed_rows = [heads.reshape(rows, -1) for heads in mixed]
    up_halves, down_halves = halves(after(second_own, *mixed), up_weight.shape[1], down_weight.shape[1])
    after_attn = embedded + (dot(mixed_rows[0], out_halves[0], nt) + dot(mixed_rows[1], out_halves[1], nt))
    normed_two_f, norm_two_back = jax.vjp(norm_scale, after_attn, norm_gains[1])
    normed_two = normed_two_f.astype(bf)
    gate_acts, gelu_backs = zip(*[jax.vjp(gelu_tanh, dot(normed_two, weight)) for weight in up_halves])
    activated = [act.astype(bf) for act in gate_acts]
    after_ffn = after_attn + (
        dot(activated[0], down_halves[0], nt) + dot(activated[1], down_halves[1], nt)
    )
    positions = jnp.arange(length)
    pool_mask = (
        (positions[None, :] >= my_prefixes[:, None]) & (positions[None, :] < my_lengths[:, None])
    ).astype(f32)

    def pool_tail(stream, gain_row):
        normed_three = norm_scale(stream, gain_row).reshape(mine, length, -1)
        pooled = jnp.sum(normed_three * pool_mask[:, :, None], axis=1) / jnp.sum(pool_mask, axis=1, keepdims=True)
        return pooled * lax.rsqrt(jnp.sum(pooled * pooled, axis=1, keepdims=True) + NORM_EPS)

    vectors, tail_back = jax.vjp(pool_tail, after_ffn, norm_gains[2])

    partner_row = jnp.pad(my_partner.astype(f32), (0, width - mine))[None]
    plane_facts = jnp.concatenate([vectors, partner_row, jnp.zeros((-(mine + 1) % 8, width), f32)], axis=0)
    plane_facts, all_ids = share_both(
        plane_facts, group_ids.reshape(-1, length), ("dat", "mdl"), "grp", (dat_size, mdl_size, grp_size)
    )
    group_vectors = plane_facts[:, :mine].reshape(group_items, width)
    group_partner = plane_facts[:, mine, :mine].reshape(group_items).astype(jnp.int32)
    all_ids = by_core(all_ids.reshape(grp_size, dat_size, item_count, length))
    live_count = jnp.sum(jnp.where(jnp.arange(grp_size) == group_index, group_live, 0))
    live_total = jnp.sum(group_live).astype(f32)
    slots = jnp.arange(group_items)
    live_rows = slots < live_count
    logits = jnp.dot(group_vectors, group_vectors.T, precision=MAX_PRECISION) / SOFTMAX_WARMTH
    allowed = live_rows[None, :] & (slots[None, :] != slots[:, None])
    masked = jnp.where(allowed, logits, MASK_FILL)
    row_top = jnp.max(masked, axis=1, keepdims=True)
    log_total = row_top[:, 0] + jnp.log(jnp.sum(jnp.exp(masked - row_top), axis=1))
    mate_hits = slots[None, :] == group_partner[:, None]
    target = jnp.sum(jnp.where(mate_hits, logits, 0.0), axis=1)
    loss_part = jnp.sum(jnp.where(live_rows, log_total - target, 0.0))
    row_weight = jnp.where(live_rows, 1.0 / live_total, 0.0)
    grad_logits = (
        row_weight[:, None] * (jnp.exp(masked - log_total[:, None]) - mate_hits.astype(f32)) / SOFTMAX_WARMTH
    )
    my_pulls = lax.dynamic_slice_in_dim(grad_logits + grad_logits.T, first_slot, mine)
    grad_vectors = jnp.dot(my_pulls, group_vectors, precision=MAX_PRECISION)

    def both_cores(own, other):
        return (own + swap_cores(other.astype(bf)).astype(f32)).astype(bf)

    def scattered(total):
        return lax.psum_scatter(total, "dat", scatter_dimension=0, tiled=True)

    grad_after_ffn, grad_gain_three = tail_back(grad_vectors)
    grad_ffn = grad_after_ffn.astype(bf)
    total_down = both_cores(*[dot(grad_ffn, act, tn) for act in activated])
    grad_gates = [
        back(dot(grad_ffn, weight))[0].astype(bf) for back, weight in zip(gelu_backs, down_halves)
    ]
    total_up = both_cores(*[dot(normed_two, grad_gate, tn) for grad_gate in grad_gates])
    part_ffn = scattered(jnp.concatenate([total_down, total_up], axis=1))
    two_back = dot(grad_gates[0], up_halves[0], nt) + dot(grad_gates[1], up_halves[1], nt)
    grad_after_attn, grad_gain_two = norm_two_back(two_back)
    grad_after_attn = grad_after_attn + grad_after_ffn
    grad_attn = grad_after_attn.astype(bf)
    total_out = both_cores(*[dot(grad_attn, heads, tn) for heads in mixed_rows])
    grad_mixed = [dot(grad_attn, weight).astype(bf).reshape(mine, length, -1) for weight in out_halves]
    grad_qkv_items, grad_lines = zip(
        *[
            attend_back(item_qkv, lines, my_lengths, stats, grad)
            for item_qkv, lines, stats, grad in zip(qkv_rows, line_halves, log_totals, grad_mixed)
        ]
    )
    grad_qkv_rows = [grad.reshape(rows, -1) for grad in grad_qkv_items]
    one_back = dot(grad_qkv_rows[0], qkv_halves[0], nt) + dot(grad_qkv_rows[1], qkv_halves[1], nt)
    outgoing, grad_gain_one = pack_back(one_back, embedded_low, grad_after_attn, norm_gains[0], features)
    total_qkv = both_cores(*[dot(normed_one, grad, tn) for grad in grad_qkv_rows])
    total_rest = jnp.concatenate([total_qkv, total_out], axis=1)

    grad_bias_own, grad_bias_other = [
        jnp.einsum("rb,hr->hb", onehot, grad, precision=MAX_PRECISION) for grad in grad_lines
    ]
    grad_bias_all = jnp.where(
        mdl_index == 0,
        jnp.concatenate([grad_bias_own, grad_bias_other], axis=0),
        jnp.concatenate([grad_bias_other, grad_bias_own], axis=0),
    )
    leader = ((dat_index == 0) & (mdl_index == 0)).astype(f32)
    gain_lines = jnp.stack([grad_gain_one, grad_gain_two, grad_gain_three]).reshape(-1, LANES)
    loss_line = jnp.full((1, LANES), loss_part * leader)
    small = jnp.concatenate(
        [gain_lines, jnp.pad(grad_bias_all, ((0, 0), (0, LANES - BUCKETS))), loss_line], axis=0
    )
    small = jnp.pad(small, ((0, -small.shape[0] % 8), (0, 0)))

    by_group = arrivals(grp_size)
    sources = jnp.array([[group] + [found[0] for found in by_group[group]] for group in range(grp_size)], jnp.int32)
    sources = lax.dynamic_index_in_dim(sources, group_index, 0, keepdims=False)
    place = jnp.concatenate([mdl_index[None].astype(jnp.int32), sources])
    order = [(slot, 0) for slot in range(grp_size)]
    order[-1:] = [(grp_size - 2, 1), (grp_size - 1, 0), (grp_size - 1, 1)]
    staged_ids, staged_flags = stage_ids(place, after(all_ids, outgoing), order)

    outgoing = after(outgoing, part_ffn)
    own_rows = lax.all_to_all(outgoing, "dat", split_axis=0, concat_axis=0, tiled=True)
    own_rows = own_rows.reshape(dat_size * pair_rows, 2 * features)
    part_rest = scattered(after(total_rest, own_rows))
    moving = [[own_rows], [own_rows]]
    swapped = [[None], [None]]

    def swap(hop, *waits):
        for way in range(2):
            both = way == 1 and moving[0][hop] is moving[1][hop]
            swapped[way].append(swapped[0][hop] if both else swap_cores(after(moving[way][hop], *waits)))

    def move(hop, *waits):
        senders = range(hop - 1, grp_size - 1)
        upward = [(group, group + 1) for group in senders]
        downward = [(grp_size - 1 - group, grp_size - 2 - group) for group in senders]
        if {group for group, _ in upward} & {group for group, _ in downward}:
            for way, pairs in enumerate((upward, downward)):
                moving[way].append(lax.ppermute(after(moving[way][-1], *waits), "grp", pairs))
        else:
            rising = group_index >= hop - 1
            moved = lax.ppermute(after(jnp.where(rising, moving[0][-1], moving[1][-1]), *waits), "grp", upward + downward)
            moving[0].append(moved)
            moving[1].append(moved)

    def candidates(slot):
        found = [by_group[group][slot - 1][1:] for group in range(grp_size)]
        kinds = sorted(set(found))
        return kinds, [kinds.index(kind) for kind in found]

    picks = [[0] * grp_size if slot == 0 else candidates(slot)[1] for slot, _ in order]
    choices = lax.dynamic_index_in_dim(jnp.array(picks, jnp.int32).T, group_index, 0, keepdims=False)
    choices = after(choices, outgoing)

    def stage(first, count):
        segments = []
        for slot, other in order[first : first + count]:
            buffers = swapped if other else moving
            segments.append([own_rows] if slot == 0 else [buffers[way][hop] for way, hop in candidates(slot)[0]])
        return Stage(segments, choices, staged_ids, staged_flags, first, dat_size * chunks, features)

    move(1)
    first_table = scatter_rows(stage(0, 1), vocab)
    small = sum_all(after(small, first_table), ("dat", "mdl"), "grp", (dat_size, mdl_size, grp_size))
    for hop in range(2, grp_size - 1):
        move(hop, small)
        swap(hop - 1)
    early = stage(1, grp_size - 3)
    early.operands[0] = after(early.operands[0], part_rest)
    own_table = scatter_rows(early, vocab, (first_table,))
    swap(grp_size - 2, own_table)
    move(grp_size - 1, own_table)
    other_table = swap_cores(after(own_table, *[kept for way in swapped for kept in way[1:]]))
    late_table = scatter_rows(stage(grp_size - 2, 2), vocab)
    swap(grp_size - 1, late_table)
    last = stage(grp_size, 2)
    full_ffn, full_rest = lax.psum((after(part_ffn, late_table), part_rest), "grp")
    table_momentum, table_variance, table_direction, table_squares = finish(
        last,
        embedding,
        embedding_first,
        embedding_second,
        (own_table, other_table, late_table),
    )
    full_ffn, full_rest = after(full_ffn, table_squares), after(full_rest, table_squares)
    by_part = lambda value: value.transpose(1, 0, 2)
    weights = (by_part(qkv_weight), out_weight.T, up_weight, down_weight, bias_table.T, norm_gains)
    gradients = (full_ffn, full_rest, small)
    moments = (
        (by_part(qkv_first), by_part(qkv_second)),
        (out_first.T, out_second.T),
        (up_first, up_second),
        (down_first, down_second),
        (bias_first.T, bias_second.T),
        (gains_first, gains_second),
    )
    *results, square_table, loss_pair = small_moments(live_total, weights, gradients, moments, max(1, features // 48))
    squares = sum_over(table_squares, square_table, ("dat", "mdl"), (dat_size, mdl_size))
    updated = update_all(squares, (embedding, *weights), (table_direction, *results[2::3]), features // 16)
    outputs = [
        loss_pair,
        updated[-1],
        table_momentum,
        table_variance,
        updated[0],
    ]
    outputs.extend(by_part(value) for value in (results[0], results[1], updated[1]))
    outputs.extend(value.T for value in (results[3], results[4], updated[2]))
    for position in range(2, 6):
        three = (results[3 * position], results[3 * position + 1], updated[position + 1])
        outputs.extend(value.T if position == 4 else value for value in three)
    return tuple(outputs)


def solution(mesh):
    state = [
        P("dat", None),
        P("dat", None, "mdl"),
        P("mdl", "dat"),
        P("dat", "mdl"),
        P("dat", "mdl"),
        P(None, "mdl"),
        P(),
    ]
    placed = [P(("grp", "dat"), None), P(("grp", "dat")), P(("grp", "dat")), P(), P(("grp", "dat"))]
    placed += state + [spec for spec in state for _ in range(2)]
    return jax.shard_map(
        shards,
        mesh=mesh,
        in_specs=tuple(placed),
        out_specs=(P(), P(), *[spec for spec in state for _ in range(3)]),
        check_vma=False,
    )
```

```python
import functools

import jax
import jax.numpy as jnp
from jax import lax
from jax.experimental import pallas as pl
from jax.experimental.pallas import tpu as pltpu
from jax.sharding import PartitionSpec as P

HEADS = 12
HEAD = 64
BUCKETS = 32
STEP = 10


SOFTMAX_WARMTH = 0.01
NORM_EPS = 1e-06
BUCKET_EDGES = (12, 16, 23, 32, 46, 64, 91)
BETA_ONE = 0.9
BETA_TWO = 0.999
ADAM_EPS = 1e-06
WEIGHT_DECAY = 0.01
LEARN_RATE = 0.5
MASK_FILL = -1000000000.0
MAX_PRECISION = lax.Precision.HIGHEST
LANES = 128
bf = jnp.bfloat16
f32 = jnp.float32


BLOCK = 128
NT = (((1,), (1,)), ((), ()))
TN = (((0,), (0,)), ((), ()))


def toeplitz(line, rows):
    out = line
    size = 1
    while size < rows:
        out = jnp.concatenate([out, pltpu.roll(out, size, 1)], axis=0)
        size *= 2
    return out


def diagonal_sums(square):
    rows, width = square.shape
    while rows > 8:
        rows //= 2
        square = square[:rows] + pltpu.roll(square[rows:], width - rows, 1)
    for shift in (4, 2, 1):
        square = square + pltpu.roll(pltpu.roll(square, width - shift, 1), 8 - shift, 0)
    return square[:1]


def head_halves(pair):
    first = lax.broadcasted_iota(jnp.int32, (1, LANES), 1) < HEAD
    return jnp.where(first, pair, 0), jnp.where(first, 0, pair)


def attend_kernel(pairs, scale, lens_ref, line_ref, qkv_ref, mixed_ref, lse_ref, scores, probs):
    items, length, _ = mixed_ref.shape
    blocks = length // BLOCK
    first = lax.broadcasted_iota(jnp.int32, (1, LANES), 1) < HEAD
    key = lax.broadcasted_iota(jnp.int32, (BLOCK, 1), 0)

    def one_pair(pair, carry):
        at = lambda part: pl.ds(pl.multiple_of((part * pairs + pair) * LANES, LANES), LANES)
        biases = [toeplitz(line_ref[pl.ds(2 * pair + head, 1), :], BLOCK) for head in range(2)]
        for item in range(items):
            keys = qkv_ref[item, :, at(1)]
            values = qkv_ref[item, :, at(2)]
            mixed = []
            for head, queries in enumerate(head_halves(qkv_ref[item, :, at(0)] * scale)):
                top = jnp.full((1, length), MASK_FILL, f32)
                for block in range(blocks):
                    rows = slice(block * BLOCK, (block + 1) * BLOCK)
                    low = length - block * BLOCK
                    part = lax.dot_general(keys[rows], queries, NT, preferred_element_type=f32)
                    part = part + biases[head][:, low : low + length]
                    part = jnp.where(key < lens_ref[item] - block * BLOCK, part, MASK_FILL)
                    scores[head, rows, :] = part
                    top = jnp.maximum(top, jnp.max(part, axis=0, keepdims=True))
                whole = jnp.zeros((1, length), f32)
                for block in range(blocks):
                    rows = slice(block * BLOCK, (block + 1) * BLOCK)
                    part = jnp.exp(scores[head, rows, :] - top)
                    scores[head, rows, :] = part
                    whole += jnp.sum(part, axis=0, keepdims=True)
                share = 1.0 / whole
                for block in range(blocks):
                    rows = slice(block * BLOCK, (block + 1) * BLOCK)
                    probs[head, rows, :] = (scores[head, rows, :] * share).astype(bf)
                lse_ref[pl.ds(2 * pair + head, 1), item * length : (item + 1) * length] = top + jnp.log(whole)
                mixed.append(lax.dot_general(probs[head], values, TN, preferred_element_type=f32))
            mixed_ref[item, :, at(0)] = jnp.where(first, mixed[0], mixed[1]).astype(bf)
        return carry

    lax.fori_loop(0, pairs, one_pair, 0)


def attend(qkv, lines, lengths):
    items, length, width = qkv.shape
    width //= 3
    pairs = width // LANES
    vm = pl.BlockSpec(memory_space=pltpu.VMEM)
    return pl.pallas_call(
        functools.partial(attend_kernel, pairs, HEAD**-0.5),
        in_specs=[pl.BlockSpec(memory_space=pltpu.SMEM), vm, vm],
        out_specs=[vm, vm],
        out_shape=[
            jax.ShapeDtypeStruct((items, length, width), bf),
            jax.ShapeDtypeStruct((2 * pairs, items * length), f32),
        ],
        scratch_shapes=[pltpu.VMEM((2, length, length), f32), pltpu.VMEM((2, length, length), bf)],
        compiler_params=pltpu.CompilerParams(vmem_limit_bytes=40 * 2**20),
        cost_estimate=pl.CostEstimate(
            flops=8 * items * length * length * width,
            bytes_accessed=items * length * width * 12,
            transcendentals=items * length * length * width // HEAD,
        ),
        name="attend",
    )(lengths, lines, qkv)


def attend_back_kernel(
    pairs, scale, lens_ref, line_ref, qkv_ref, lse_ref, dmix_ref, dqkv_ref, dline_ref, probs, dprobs, low, diag
):
    items, length, _ = dmix_ref.shape
    blocks = length // BLOCK
    first = lax.broadcasted_iota(jnp.int32, (1, LANES), 1) < HEAD
    key = lax.broadcasted_iota(jnp.int32, (BLOCK, 1), 0)

    def one_pair(pair, carry):
        at = lambda part: pl.ds(pl.multiple_of((part * pairs + pair) * LANES, LANES), LANES)
        biases = [toeplitz(line_ref[pl.ds(2 * pair + head, 1), :], BLOCK) for head in range(2)]
        diag[...] = jnp.zeros_like(diag)
        for item in range(items):
            keys = qkv_ref[item, :, at(1)]
            values = qkv_ref[item, :, at(2)]
            queries = qkv_ref[item, :, at(0)] * scale
            given = dmix_ref[item, :, at(0)]
            dquery, dkeys, dvals = [], [], []
            for head, (mine, pulled) in enumerate(zip(head_halves(queries), head_halves(given))):
                stats = lse_ref[pl.ds(2 * pair + head, 1), item * length : (item + 1) * length]
                inner = jnp.zeros((1, length), f32)
                for block in range(blocks):
                    rows = slice(block * BLOCK, (block + 1) * BLOCK)
                    start = length - block * BLOCK
                    part = lax.dot_general(keys[rows], mine, NT, preferred_element_type=f32)
                    part = jnp.exp(part + biases[head][:, start : start + length] - stats)
                    part = jnp.where(key < lens_ref[item] - block * BLOCK, part, 0.0)
                    back = lax.dot_general(values[rows], pulled, NT, preferred_element_type=f32)
                    probs[head, rows, :] = part
                    dprobs[head, rows, :] = back
                    low[head, rows, :] = part.astype(bf)
                    inner += jnp.sum(part * back, axis=0, keepdims=True)
                dvals.append(jnp.dot(low[head], given, preferred_element_type=f32))
                for block in range(blocks):
                    rows = slice(block * BLOCK, (block + 1) * BLOCK)
                    start = length - block * BLOCK
                    part = probs[head, rows, :] * (dprobs[head, rows, :] - inner)
                    diag[head, :, start : start + length] += part
                    low[head, rows, :] = part.astype(bf)
                dkeys.append(jnp.dot(low[head], queries, preferred_element_type=f32))
                dquery.append(lax.dot_general(low[head], keys, TN, preferred_element_type=f32))
            dqkv_ref[item, :, at(0)] = (jnp.where(first, dquery[0], dquery[1]) * scale).astype(bf)
            dqkv_ref[item, :, at(1)] = jnp.where(first, dkeys[0], dkeys[1]).astype(bf)
            dqkv_ref[item, :, at(2)] = jnp.where(first, dvals[0], dvals[1]).astype(bf)
        for head in range(2):
            dline_ref[pl.ds(2 * pair + head, 1), :] = diagonal_sums(diag[head])
        return carry

    lax.fori_loop(0, pairs, one_pair, 0)


def attend_back(qkv, lines, lengths, lse, dmixed):
    items, length, width = dmixed.shape
    pairs = width // LANES
    vm = pl.BlockSpec(memory_space=pltpu.VMEM)
    square = (2, length, length)
    return pl.pallas_call(
        functools.partial(attend_back_kernel, pairs, HEAD**-0.5),
        in_specs=[pl.BlockSpec(memory_space=pltpu.SMEM), vm, vm, vm, vm],
        out_specs=[vm, vm],
        out_shape=[jax.ShapeDtypeStruct(qkv.shape, bf), jax.ShapeDtypeStruct(lines.shape, f32)],
        scratch_shapes=[
            pltpu.VMEM(square, f32),
            pltpu.VMEM(square, f32),
            pltpu.VMEM(square, bf),
            pltpu.VMEM((2, BLOCK, 2 * length), f32),
        ],
        compiler_params=pltpu.CompilerParams(vmem_limit_bytes=40 * 2**20),
        cost_estimate=pl.CostEstimate(
            flops=20 * items * length * length * width,
            bytes_accessed=items * length * width * 20,
            transcendentals=items * length * length * width // HEAD,
        ),
        name="attend_back",
    )(lengths, lines, qkv, lse, dmixed)


def split_features(features):
    whole = features // LANES * LANES
    return whole, features - whole


def tile_count(features):
    whole, rest = split_features(features)
    return whole // LANES + (rest > 0)


def first_of_pair(packed, features):
    return packed[..., :features]


def second_of_pair(packed, features):
    whole, rest = split_features(features)
    tail = packed[..., features : features + rest]
    return jnp.concatenate([packed[..., features + rest :], tail], axis=-1) if whole else tail


def pack_pair(first, second):
    whole, _ = split_features(first.shape[-1])
    parts = [first, second[..., whole:], second[..., :whole]] if whole else [first, second]
    return jnp.concatenate(parts, axis=-1)


def packed_starts(features, half):
    whole, rest = split_features(features)
    base = 0 if half == 0 else features + rest
    return [base + low for low in range(0, whole, LANES)] + ([whole] if rest else [])


def gather_kernel(features, load_steps, batch, table_ref, ids_ref, out_ref, *scratch):
    step = pl.program_id(0)
    width = table_ref.shape[1]
    tiles = tile_count(features)
    whole, rest = split_features(features)
    stash = scratch[:tiles]
    rows = [scratch[tiles : 2 * tiles], scratch[2 * tiles :]]

    @pl.when(step < load_steps)
    def _():
        base = pl.multiple_of(step * width, width)
        for tile in range(tiles):
            low = tile * LANES
            part = table_ref[low : min(features, low + LANES), :].astype(bf).astype(f32)
            if low == whole:
                blank = [jnp.zeros((LANES - 2 * rest, width), f32)] if 2 * rest < LANES else []
                part = jnp.concatenate([part, part, *blank], axis=0)
            stash[tile][pl.ds(base, width), :] = part.T

    @pl.when(step >= load_steps)
    def _():
        count = out_ref.shape[0]
        for half in range(2):
            def take(index, carry):
                start = pl.multiple_of(index * batch, batch)
                tokens = [ids_ref[0, half, start + inner] for inner in range(batch)]
                for tile in range(tiles):
                    for inner in range(batch):
                        rows[half][tile][pl.ds(start + inner, 1), :] = stash[tile][pl.ds(tokens[inner], 1), :]
                return carry
            lax.fori_loop(0, count // batch, take, 0, unroll=2)
        for half in range(2):
            for tile in range(whole // LANES):
                low = packed_starts(features, half)[tile]
                out_ref[:, low : low + LANES] = rows[half][tile][...].astype(bf)
        if rest:
            lane = lax.broadcasted_iota(jnp.int32, (1, LANES), 1)
            shared = jnp.where(lane < rest, rows[0][-1][...], rows[1][-1][...]).astype(bf)
            out_ref[:, whole : whole + 2 * rest] = shared[:, : 2 * rest]


def gather_rows(table, ids, width=4096, batch=16):
    features, vocab = table.shape
    steps, _, chunk = ids.shape
    tiles = tile_count(features)
    load_steps = pl.cdiv(vocab, width)
    return pl.pallas_call(
        functools.partial(gather_kernel, features, load_steps, batch),
        grid=(load_steps + steps,),
        in_specs=[
            pl.BlockSpec((features, width), lambda s: (0, jnp.minimum(s, load_steps - 1))),
            pl.BlockSpec((1, 2, chunk), lambda s: (jnp.maximum(s - load_steps, 0), 0, 0), memory_space=pltpu.SMEM),
        ],
        out_specs=pl.BlockSpec((chunk, 2 * features), lambda s: (jnp.maximum(s - load_steps, 0), 0)),
        out_shape=jax.ShapeDtypeStruct((steps * chunk, 2 * features), bf),
        scratch_shapes=[pltpu.VMEM((load_steps * width, LANES), f32)] * tiles + [pltpu.VMEM((chunk, LANES), f32)] * (2 * tiles),
        compiler_params=pltpu.CompilerParams(vmem_limit_bytes=60 * 2**20),
        cost_estimate=pl.CostEstimate(flops=0, bytes_accessed=80 * 2**20, transcendentals=0),
        name="gather_rows",
    )(table, ids)


def stage_ids_kernel(batch, order, sources, picks, ids_ref, out_ref, flags_ref, choices_ref, flat):
    lane = lax.broadcasted_iota(jnp.int32, (1, LANES), 1)
    count, _, chunk = ids_ref.shape[2:]
    group = lax.axis_index("grp")

    def of_group(values):
        found = jnp.int32(values[0])
        for at, value in enumerate(values[1:], 1):
            found = jnp.where(group == at, value, found)
        return found

    flat[...] = jnp.zeros_like(flat)
    for at, (slot, other) in enumerate(order):
        choices_ref[at] = of_group(picks[at])
        core = lax.rem(lax.axis_index("mdl") + other, ids_ref.shape[0])
        source = of_group(sources[slot])
        for step in range(count):
            index = at * count + step
            ids = ids_ref[core, source, step]
            out_ref[index] = ids
            flat[2 * index : 2 * index + 2, :] = ids
    flags = jnp.zeros((flat.shape[0], LANES), jnp.int32)
    for block in range(chunk // LANES):
        part = flat[:, block * LANES : (block + 1) * LANES]
        found = jnp.zeros(part.shape, jnp.int32)
        for shift in range(1, batch):
            again = (part == pltpu.roll(part, shift, 1)) & (lane % batch >= shift)
            found = jnp.where(again, 1, found)
        flags = jnp.where(lane == block, jnp.max(found, axis=1, keepdims=True), flags)
    for index in range(out_ref.shape[0]):
        flags_ref[index] = flags[2 * index : 2 * index + 2]


def stage_ids(ids, order, sources, picks, batch=4):
    *_, count, _, chunk = ids.shape
    vm = pl.BlockSpec(memory_space=pltpu.VMEM)
    total = len(order) * count
    return pl.pallas_call(
        functools.partial(stage_ids_kernel, batch, order, sources, picks),
        in_specs=[vm],
        out_specs=[vm, vm, pl.BlockSpec(memory_space=pltpu.SMEM)],
        out_shape=[
            jax.ShapeDtypeStruct((total, 2, chunk), jnp.int32),
            jax.ShapeDtypeStruct((total, 2, LANES), jnp.int32),
            jax.ShapeDtypeStruct((len(order),), jnp.int32),
        ],
        scratch_shapes=[pltpu.VMEM((2 * total + -2 * total % 8, chunk), jnp.int32)],
        name="stage_ids",
    )(ids)


def spread_rows(features, rows_ref, summed):
    whole, rest = split_features(features)
    lane = lax.broadcasted_iota(jnp.int32, (1, LANES), 1)
    for half in range(2):
        for tile, start in enumerate(packed_starts(features, half)):
            if start == whole:
                part = rows_ref[:, start : start + 2 * rest].astype(f32)
                if 2 * rest < LANES:
                    part = jnp.concatenate([part, jnp.zeros((part.shape[0], LANES - 2 * rest), f32)], axis=1)
                mine = lane < rest if half == 0 else (lane >= rest) & (lane < 2 * rest)
                part = jnp.where(mine, part, 0.0)
            else:
                part = rows_ref[:, start : start + LANES].astype(f32)
            summed[half][tile][...] = part


def merge_rows(batch, ids_row_ref, flags_ref, summed):
    count = summed[0][0].shape[0]
    for half in range(2):
        for at in range(count // LANES):
            block = slice(at * LANES, (at + 1) * LANES)

            @pl.when(flags_ref[0, half, at] > 0)
            def _():
                place = lax.broadcasted_iota(jnp.int32, (LANES, LANES), 0) // batch
                same_batch = place == lax.broadcasted_iota(jnp.int32, (LANES, LANES), 1) // batch
                across = jnp.broadcast_to(ids_row_ref[0, half : half + 1, block], (LANES, LANES))
                match = jnp.where((across == across.T) & same_batch, 1.0, 0.0).astype(bf)
                for rows in summed[half]:
                    rows[block, :] = jnp.dot(match, rows[block, :].astype(bf), preferred_element_type=f32)


def add_rows(batch, ids_ref, totals, summed):
    count = summed[0][0].shape[0]

    def add(index, carry):
        start = pl.multiple_of(index * batch, batch)
        for half in range(2):
            tokens = [ids_ref[0, half, start + inner] for inner in range(batch)]
            fresh = [
                [total[pl.ds(tokens[inner], 1), :] + rows[pl.ds(start + inner, 1), :] for inner in range(batch)]
                for total, rows in zip(totals, summed[half])
            ]
            for total, new in zip(totals, fresh):
                for inner in range(batch):
                    total[pl.ds(tokens[inner], 1), :] = new[inner]
        return carry

    lax.fori_loop(0, count // batch, add, 0, unroll=4)


def table_columns(features, totals, base, width):
    whole, rest = split_features(features)
    pieces = [total[pl.ds(base, width), :].T for total in totals]
    if rest:
        pieces[-1] = pieces[-1][:rest] + pieces[-1][rest : 2 * rest]
    return pieces


class Stage:
    def __init__(self, segments, choices, ids, flags, first, blocks, features):
        self.first = first
        first = first * blocks
        self.arrays = [array for candidates in segments for array in candidates]
        self.segments = [len(candidates) for candidates in segments]
        self.chunk = ids.shape[2]
        self.each = segments[0][0].shape[0] // self.chunk
        self.steps = self.each * len(segments)
        self.operands = [choices, ids, ids, flags, *self.arrays]
        at = lambda s: first + jnp.minimum(s, self.steps - 1)
        self.in_specs = [
            pl.BlockSpec(memory_space=pltpu.SMEM),
            pl.BlockSpec((1, 2, self.chunk), lambda s: (at(s), 0, 0), memory_space=pltpu.SMEM),
            pl.BlockSpec((1, 2, self.chunk), lambda s: (at(s), 0, 0)),
            pl.BlockSpec((1, 2, LANES), lambda s: (at(s), 0, 0), memory_space=pltpu.SMEM),
        ]
        for segment, candidates in enumerate(segments):
            for _ in candidates:
                low = segment * self.each
                self.in_specs.append(
                    pl.BlockSpec(
                        (self.chunk, 2 * features), lambda s, low=low: (jnp.clip(s - low, 0, self.each - 1), 0)
                    )
                )
        self.features = features

    def scratch(self, vocab):
        tiles = tile_count(self.features)
        return [pltpu.VMEM((vocab, LANES), f32)] * tiles + [pltpu.VMEM((self.chunk, LANES), f32)] * (2 * tiles)

    def add(self, batch, refs, scratch):
        choice_ref, ids_ref, ids_row_ref, flags_ref, *rows_refs = refs
        step = pl.program_id(0)
        tiles = tile_count(self.features)
        totals = scratch[:tiles]
        summed = [scratch[tiles : 2 * tiles], scratch[2 * tiles :]]

        @pl.when(step == 0)
        def _():
            for total in totals:
                total[...] = jnp.zeros_like(total)

        for segment, candidates in enumerate(self.segments):
            now = (step >= segment * self.each) & (step < (segment + 1) * self.each)
            for candidate in range(candidates):
                rows_ref, rows_refs = rows_refs[0], rows_refs[1:]

                @pl.when(now & (choice_ref[self.first + segment] == candidate))
                def _():
                    spread_rows(self.features, rows_ref, summed)

        @pl.when(step < self.steps)
        def _():
            merge_rows(batch, ids_row_ref, flags_ref, summed)
            add_rows(batch, ids_ref, totals, summed)

        return totals


def scatter_kernel(stage, batch, dense, *refs):
    count = len(stage.operands)
    dense_refs = refs[count : count + dense]
    out_ref = refs[count + dense]
    totals = stage.add(batch, refs[:count], refs[count + dense + 1 :])
    step = pl.program_id(0)
    width = out_ref.shape[1]

    @pl.when(step >= stage.steps)
    def _():
        base = pl.multiple_of((step - stage.steps) * width, width)
        low = 0
        for piece in table_columns(stage.features, totals, base, width):
            cut = slice(low, low + piece.shape[0])
            low += piece.shape[0]
            for dense_ref in dense_refs:
                piece = piece + dense_ref[cut, :].astype(f32)
            out_ref[cut, :] = piece.astype(bf)


def scatter_rows(stage, vocab, dense=(), width=4096, batch=4):
    flush = pl.cdiv(vocab, width)
    block = pl.BlockSpec((stage.features, width), lambda s: (0, jnp.maximum(s - stage.steps, 0)))
    return pl.pallas_call(
        functools.partial(scatter_kernel, stage, batch, len(dense)),
        grid=(stage.steps + flush,),
        in_specs=stage.in_specs + [block] * len(dense),
        out_specs=block,
        out_shape=jax.ShapeDtypeStruct((stage.features, vocab), bf),
        scratch_shapes=stage.scratch(flush * width),
        compiler_params=pltpu.CompilerParams(vmem_limit_bytes=127 * 2**19),
        cost_estimate=pl.CostEstimate(flops=0, bytes_accessed=100 * 2**20, transcendentals=0),
        name="scatter_rows",
    )(*stage.operands, *dense)


def assemble_kernel(features, spread_ref, gain_ref, embedded_ref, normed_ref):
    for half, take in enumerate((first_of_pair, second_of_pair)):
        row = jnp.concatenate([take(spread_ref[part], features) for part in range(spread_ref.shape[0])], axis=1)
        embedded_ref[half] = row
        stream = row.astype(f32)
        scale = lax.rsqrt(jnp.mean(stream * stream, axis=1, keepdims=True) + NORM_EPS)
        normed_ref[half] = (stream * scale * gain_ref[...]).astype(bf)


def assemble(spread, gain, block=128):
    parts, count, features = spread.shape
    features //= 2
    width = parts * features
    block = min(block, count)
    out = jax.ShapeDtypeStruct((2, count, width), bf)
    whole_block = pl.BlockSpec((2, block, width), lambda s: (0, s, 0))
    embedded, normed = pl.pallas_call(
        functools.partial(assemble_kernel, features),
        grid=(count // block,),
        in_specs=[
            pl.BlockSpec((parts, block, 2 * features), lambda s: (0, s, 0)),
            pl.BlockSpec((1, width), lambda s: (0, 0)),
        ],
        out_specs=[whole_block, whole_block],
        out_shape=[out, out],
        compiler_params=pltpu.CompilerParams(vmem_limit_bytes=30 * 2**20),
        name="assemble",
    )(spread, gain.reshape(1, width))
    return embedded.reshape(2 * count, width), normed.reshape(2 * count, width)


def pack_back_kernel(features, back_ref, embedded_ref, passed_ref, gain_ref, packed_ref, grad_gain_ref):
    gain = gain_ref[...]
    halves = []
    grad_gain = jnp.zeros_like(gain)
    for half in range(2):
        stream = embedded_ref[half].astype(f32)
        back = back_ref[half]
        scale = lax.rsqrt(jnp.mean(stream * stream, axis=1, keepdims=True) + NORM_EPS)
        unit = stream * scale
        grad_gain += jnp.sum(back * unit, axis=0, keepdims=True)
        pulled = back * gain
        along = jnp.mean(pulled * unit, axis=1, keepdims=True)
        halves.append((passed_ref[half] + scale * (pulled - unit * along)).astype(bf))
    for part in range(packed_ref.shape[0]):
        cut = slice(part * features, (part + 1) * features)
        packed_ref[part] = pack_pair(halves[0][:, cut], halves[1][:, cut])

    @pl.when(pl.program_id(0) == 0)
    def _():
        grad_gain_ref[...] = jnp.zeros_like(grad_gain_ref)

    grad_gain_ref[...] += grad_gain


def pack_back(back, embedded, passed, gain, features, block=128):
    rows, width = back.shape
    count, parts = rows // 2, width // features
    block = min(block, count)
    pair = pl.BlockSpec((2, block, width), lambda s: (0, s, 0))
    line = pl.BlockSpec((1, width), lambda s: (0, 0))
    packed, grad_gain = pl.pallas_call(
        functools.partial(pack_back_kernel, features),
        grid=(count // block,),
        in_specs=[pair, pair, pair, line],
        out_specs=[pl.BlockSpec((parts, block, 2 * features), lambda s: (0, s, 0)), line],
        out_shape=[jax.ShapeDtypeStruct((parts, count, 2 * features), bf), jax.ShapeDtypeStruct((1, width), f32)],
        compiler_params=pltpu.CompilerParams(vmem_limit_bytes=30 * 2**20),
        name="pack_back",
    )(back.reshape(2, count, width), embedded.reshape(2, count, width), passed.reshape(2, count, width), gain.reshape(1, width))
    return packed, grad_gain[0]


def finish_kernel(stage, vocab, batch, dense, *refs):
    count = len(stage.operands)
    weight_ref, first_ref, second_ref, *dense_refs = refs[count : count + 3 + dense]
    refs, scratch = refs[: count + 7 + dense], refs[count + 7 + dense :]
    momentum_ref, variance_ref, direction_ref, squares_ref = refs[-4:]
    totals = stage.add(batch, refs[:count], scratch)
    step = pl.program_id(0)

    @pl.when(step == 0)
    def _():
        squares_ref[...] = jnp.zeros_like(squares_ref)

    @pl.when(step >= stage.steps)
    def _():
        width = weight_ref.shape[1]
        base = pl.multiple_of((step - stage.steps) * width, width)
        inside = base + lax.broadcasted_iota(jnp.int32, (1, width), 1) < vocab
        low = 0
        for piece in table_columns(stage.features, totals, base, width):
            cut = slice(low, low + piece.shape[0])
            low += piece.shape[0]
            weight = weight_ref[cut, :]
            gradient = piece
            for dense_ref in dense_refs:
                gradient = gradient + dense_ref[cut, :].astype(f32)
            momentum, variance, direction = lamb_direction(weight, gradient, first_ref[cut, :], second_ref[cut, :])
            momentum_ref[cut, :] = momentum
            variance_ref[cut, :] = variance
            direction_ref[cut, :] = direction.astype(bf)
            for line, value in enumerate((weight, direction)):
                value = jnp.where(inside, value, 0.0)
                squares_ref[line : line + 1, :] += jnp.sum(value * value, axis=0, keepdims=True)


def finish(stage, weight, first, second, dense, width=1024, batch=4, mode=None):
    features, vocab = weight.shape
    columns = pl.cdiv(vocab, width)
    block = pl.BlockSpec((features, width), lambda s: (0, jnp.maximum(s - stage.steps, 0)))
    ahead = pl.BlockSpec(block.block_shape, block.index_map, pipeline_mode=mode)
    full = jax.ShapeDtypeStruct(weight.shape, f32)
    return pl.pallas_call(
        functools.partial(finish_kernel, stage, vocab, batch, len(dense)),
        grid=(stage.steps + columns,),
        in_specs=stage.in_specs + [ahead] * (3 + len(dense)),
        out_specs=[block, block, block, pl.BlockSpec((8, width), lambda s: (0, 0))],
        out_shape=[full, full, jax.ShapeDtypeStruct(weight.shape, bf), jax.ShapeDtypeStruct((8, width), f32)],
        scratch_shapes=stage.scratch(columns * width),
        compiler_params=pltpu.CompilerParams(vmem_limit_bytes=127 * 2**19),
        cost_estimate=pl.CostEstimate(flops=0, bytes_accessed=300 * 2**20, transcendentals=0),
        name="finish",
    )(*stage.operands, weight, first, second, *dense)


MESH = pl.DeviceIdType.MESH


def exchange(value_ref, out_ref, mine, peers, send, received, slot):
    copies = []
    for peer in peers:
        copy = pltpu.make_async_remote_copy(
            src_ref=value_ref,
            dst_ref=out_ref.at[mine],
            send_sem=send.at[slot],
            recv_sem=received.at[slot],
            device_id=peer,
            device_id_type=MESH,
        )
        copy.start()
        copies.append(copy)
        slot += 1
    return copies


def line_peers(axis):
    place, size = lax.axis_index(axis), lax.axis_size(axis)
    return place, [{axis: lax.rem(place + step, size)} for step in range(1, size)]


def plane_peers(axes):
    places = [lax.axis_index(axis) for axis in axes]
    sizes = [lax.axis_size(axis) for axis in axes]
    count = sizes[0] * sizes[1]
    mine = places[0] * sizes[1] + places[1]
    peers = []
    for step in range(1, count):
        peer = lax.rem(mine + step, count)
        peers.append({axes[0]: peer // sizes[1], axes[1]: lax.rem(peer, sizes[1])})
    return mine, peers


def greet(peers):
    barrier = pltpu.get_barrier_semaphore()
    for peer in peers:
        pl.semaphore_signal(barrier, inc=1, device_id=peer, device_id_type=MESH)
    pl.semaphore_wait(barrier, len(peers))


def share_kernel(axis, value_ref, out_ref, send, received):
    mine, peers = line_peers(axis)
    greet(peers)
    out_ref[mine] = value_ref[...]
    for copy in exchange(value_ref, out_ref, mine, peers, send, received, 0):
        copy.wait()


def share(value, axis, size):
    return pl.pallas_call(
        functools.partial(share_kernel, axis),
        in_specs=[pl.BlockSpec(memory_space=pltpu.VMEM)],
        out_specs=pl.BlockSpec(memory_space=pltpu.VMEM),
        out_shape=jax.ShapeDtypeStruct((size, *value.shape), value.dtype),
        scratch_shapes=[pltpu.SemaphoreType.DMA((size - 1,)), pltpu.SemaphoreType.DMA((size - 1,))],
        compiler_params=pltpu.CompilerParams(collective_id=0, has_side_effects=True),
        name="share",
    )(value)


def sum_squares_kernel(axes, rows_ref, table_ref, out_ref, slots, send, received):
    places = [lax.axis_index(axis) for axis in axes]
    sizes = [lax.axis_size(axis) for axis in axes]
    count = sizes[0] * sizes[1]
    mine = places[0] * sizes[1] + places[1]
    barrier = pltpu.get_barrier_semaphore()
    peers = []
    for step in range(1, count):
        peer = lax.rem(mine + step, count)
        peers.append({axes[0]: peer // sizes[1], axes[1]: lax.rem(peer, sizes[1])})
    for peer in peers:
        pl.semaphore_signal(barrier, inc=1, device_id=peer, device_id_type=MESH)
    pl.semaphore_wait(barrier, count - 1)
    lane = lax.broadcasted_iota(jnp.int32, (1, LANES), 1)
    sums = jnp.sum(rows_ref[...], axis=1, keepdims=True)
    slots[mine] = table_ref[...]
    slots[mine, 0:1, :] = jnp.where(lane == 0, sums[0:1], jnp.where(lane == 1, sums[1:2], 0.0)) * table_ref[0:1, :]
    copies = []
    for step, peer in enumerate(peers):
        copy = pltpu.make_async_remote_copy(
            src_ref=slots.at[mine],
            dst_ref=slots.at[mine],
            send_sem=send.at[step],
            recv_sem=received.at[step],
            device_id=peer,
            device_id_type=MESH,
        )
        copy.start()
        copies.append(copy)
    for copy in copies:
        copy.wait()
    total = slots[0]
    for other in range(1, count):
        total = total + slots[other]
    out_ref[...] = total


def sum_over(rows, table, axes, sizes):
    count = sizes[0] * sizes[1]
    return pl.pallas_call(
        functools.partial(sum_squares_kernel, axes),
        in_specs=[pl.BlockSpec(memory_space=pltpu.VMEM)] * 2,
        out_specs=pl.BlockSpec(memory_space=pltpu.VMEM),
        out_shape=jax.ShapeDtypeStruct(table.shape, f32),
        scratch_shapes=[
            pltpu.VMEM((count, *table.shape), f32),
            pltpu.SemaphoreType.DMA((count - 1,)),
            pltpu.SemaphoreType.DMA((count - 1,)),
        ],
        compiler_params=pltpu.CompilerParams(collective_id=1, has_side_effects=True),
        name="sum_over",
    )(rows, table)


def sum_all_kernel(near, far, value_ref, out_ref, near_slots, far_slots, send, received):
    places = [lax.axis_index(axis) for axis in (*near, far)]
    sizes = [lax.axis_size(axis) for axis in (*near, far)]
    count = sizes[0] * sizes[1]
    mine = places[0] * sizes[1] + places[1]
    barrier = pltpu.get_barrier_semaphore()
    plane, line = [], []
    for step in range(1, count):
        peer = lax.rem(mine + step, count)
        plane.append({near[0]: peer // sizes[1], near[1]: lax.rem(peer, sizes[1])})
    for step in range(1, sizes[2]):
        line.append({far: lax.rem(places[2] + step, sizes[2])})
    for peer in plane + line:
        pl.semaphore_signal(barrier, inc=1, device_id=peer, device_id_type=MESH)
    pl.semaphore_wait(barrier, len(plane) + len(line))
    slot = 0
    value = value_ref[...]
    for peers, slots, at in ((plane, near_slots, mine), (line, far_slots, places[2])):
        slots[at] = value
        copies = []
        for peer in peers:
            copy = pltpu.make_async_remote_copy(
                src_ref=slots.at[at],
                dst_ref=slots.at[at],
                send_sem=send.at[slot],
                recv_sem=received.at[slot],
                device_id=peer,
                device_id_type=MESH,
            )
            copy.start()
            copies.append(copy)
            slot += 1
        for copy in copies:
            copy.wait()
        value = slots[0]
        for other in range(1, slots.shape[0]):
            value = value + slots[other]
    out_ref[...] = value


def sum_all(value, near, far, sizes):
    count = sizes[0] * sizes[1]
    slots = count - 1 + sizes[2] - 1
    return pl.pallas_call(
        functools.partial(sum_all_kernel, near, far),
        in_specs=[pl.BlockSpec(memory_space=pltpu.VMEM)],
        out_specs=pl.BlockSpec(memory_space=pltpu.VMEM),
        out_shape=jax.ShapeDtypeStruct(value.shape, f32),
        scratch_shapes=[
            pltpu.VMEM((count, *value.shape), f32),
            pltpu.VMEM((sizes[2], *value.shape), f32),
            pltpu.SemaphoreType.DMA((slots,)),
            pltpu.SemaphoreType.DMA((slots,)),
        ],
        compiler_params=pltpu.CompilerParams(collective_id=2, has_side_effects=True),
        name="sum_all",
    )(value)


def share_both_kernel(plane, line, vectors_ref, ids_ref, all_vectors_ref, all_ids_ref, send, received):
    mine, near = plane_peers(plane)
    place, far = line_peers(line)
    greet(near + far)
    all_vectors_ref[mine] = vectors_ref[...]
    all_ids_ref[place] = ids_ref[...]
    copies = exchange(vectors_ref, all_vectors_ref, mine, near, send, received, 0)
    copies += exchange(ids_ref, all_ids_ref, place, far, send, received, len(near))
    for copy in copies:
        copy.wait()


def share_both(vectors, ids, plane, line, sizes):
    count = sizes[0] * sizes[1]
    slots = count - 1 + sizes[2] - 1
    vm = pl.BlockSpec(memory_space=pltpu.VMEM)
    return pl.pallas_call(
        functools.partial(share_both_kernel, plane, line),
        in_specs=[vm, vm],
        out_specs=[vm, vm],
        out_shape=[
            jax.ShapeDtypeStruct((count, *vectors.shape), vectors.dtype),
            jax.ShapeDtypeStruct((sizes[2], *ids.shape), ids.dtype),
        ],
        scratch_shapes=[pltpu.SemaphoreType.DMA((slots,)), pltpu.SemaphoreType.DMA((slots,))],
        compiler_params=pltpu.CompilerParams(collective_id=3, has_side_effects=True),
        name="share_both",
    )(vectors, ids)


def lamb_direction(weight, gradient, moment_one, moment_two):
    momentum = BETA_ONE * moment_one + (1.0 - BETA_ONE) * gradient
    variance = BETA_TWO * moment_two + (1.0 - BETA_TWO) * gradient * gradient
    direction = (
        momentum / (1.0 - BETA_ONE**STEP) / (jnp.sqrt(variance / (1.0 - BETA_TWO**STEP)) + ADAM_EPS)
        + WEIGHT_DECAY * weight
    )
    return (momentum, variance, direction)


def total_of(value):
    while value.ndim > 2:
        value = jnp.sum(value, axis=1)
    return jnp.sum(jnp.sum(value, axis=1, keepdims=True), axis=0, keepdims=True)


def small_moments_kernel(live_ref, ffn_ref, rest_ref, small_ref, *refs):
    inputs, outputs, squares_ref, loss_ref = refs[:18], refs[18:-2], refs[-2], refs[-1]
    parts, _, width = inputs[0].shape
    half = ffn_ref.shape[1] // 2
    heads, buckets = inputs[12].shape
    gains, model = inputs[15].shape
    lines = model // LANES
    first_mdl, first_dat = lax.axis_index("mdl") == 0, lax.axis_index("dat") == 0

    def bias_gradient():
        start = gains * lines
        own = [small_ref[start + core * heads : start + (core + 1) * heads, :buckets] for core in range(HEADS // heads)]
        return functools.reduce(
            lambda kept, at: jnp.where(lax.axis_index("mdl") == at, own[at], kept), range(1, len(own)), own[0]
        )

    def gain_gradient():
        rows = [[small_ref[gain * lines + at : gain * lines + at + 1, :] for at in range(lines)] for gain in range(gains)]
        return jnp.concatenate([jnp.concatenate(row, axis=1) for row in rows], axis=0)

    gradient_of = (
        lambda: jnp.stack([rest_ref[:, part * width : (part + 1) * width] for part in range(parts)]),
        lambda: rest_ref[:, parts * width :],
        lambda: ffn_ref[:, half:],
        lambda: ffn_ref[:, :half],
        bias_gradient,
        gain_gradient,
    )
    lane = lax.broadcasted_iota(jnp.int32, (1, LANES), 1)
    counted = [first_mdl, True, True, True, True, first_dat] + [first_mdl & first_dat] * 3

    @pl.when(pl.program_id(0) == 0)
    def _():
        squares_ref[...] = jnp.zeros_like(squares_ref)
        squares_ref[0:1, :] = jnp.where(counted[0], jnp.ones((1, LANES), f32), 0.0)
        loss_line = gains * lines + HEADS
        loss_ref[0] = jnp.max(small_ref[loss_line : loss_line + 1, :])
        loss_ref[1] = live_ref[0]

    def update(place):
        weight_ref, first_ref, second_ref = inputs[3 * place : 3 * place + 3]
        weight = weight_ref[...]
        results = lamb_direction(weight, gradient_of[place]().astype(f32), first_ref[...], second_ref[...])
        for ref, value in zip(outputs[3 * place : 3 * place + 3], results):
            ref[...] = value
        return weight * weight, results[2] * results[2]

    def add(line, weight_square, direction_square):
        both = jnp.where(lane == 0, weight_square, jnp.where(lane == 1, direction_square, 0.0))
        squares_ref[line : line + 1, :] += jnp.where(counted[line], both, 0.0)

    for place in range(4):
        weight_square, direction_square = update(place)
        add(place + 1, total_of(weight_square), total_of(direction_square))

    @pl.when(pl.program_id(0) == 0)
    def _():
        weight_square, direction_square = update(4)
        add(5, total_of(weight_square), total_of(direction_square))
        weight_square, direction_square = update(5)
        for row in range(weight_square.shape[0]):
            add(6 + row, total_of(weight_square[row : row + 1]), total_of(direction_square[row : row + 1]))


def row_block(value, steps):
    if value.ndim == 3:
        return pl.BlockSpec((value.shape[0], value.shape[1] // steps, value.shape[2]), lambda s: (0, s, 0))
    return pl.BlockSpec((value.shape[0] // steps, value.shape[1]), lambda s: (s, 0))


def whole_block(value):
    return pl.BlockSpec(value.shape, lambda s: (0,) * value.ndim)


def small_moments(live_total, weights, gradients, moments, steps):
    operands = [live_total.reshape(1), *gradients]
    scalars = pl.BlockSpec(memory_space=pltpu.SMEM)
    in_specs = [scalars] + [row_block(value, steps) for value in gradients[:2]] + [whole_block(gradients[2])]
    out_specs, out_shape = [], []
    for place, (weight, states) in enumerate(zip(weights, moments)):
        spec = row_block(weight, steps) if place < 4 else whole_block(weight)
        operands += [weight, *states]
        in_specs += [spec] * 3
        out_specs += [spec] * 3
        out_shape += [jax.ShapeDtypeStruct(weight.shape, f32)] * 3
    return pl.pallas_call(
        small_moments_kernel,
        grid=(steps,),
        in_specs=in_specs,
        out_specs=out_specs + [pl.BlockSpec((16, LANES), lambda s: (0, 0)), scalars],
        out_shape=out_shape + [jax.ShapeDtypeStruct((16, LANES), f32), jax.ShapeDtypeStruct((2,), f32)],
        compiler_params=pltpu.CompilerParams(vmem_limit_bytes=127 * 2**19),
        name="small_moments",
    )(*operands)


def update_all_kernel(squares_ref, *refs):
    norms = jnp.sqrt(squares_ref[...])
    rates = LEARN_RATE * norms[:, 0:1] / norms[:, 1:2]
    count = len(refs) // 3
    norms_ref = refs[-1]
    norms_ref[...] = norms[: norms_ref.shape[0], :2]
    for place in range(count):
        weight_ref, direction_ref, updated_ref = refs[2 * place], refs[2 * place + 1], refs[2 * count + place]
        rate = rates[6:9] if place == 6 else rates[place : place + 1]
        weight = weight_ref[...]
        if weight.ndim == 3:
            rate = rate[:, :, None]
        updated_ref[...] = weight - rate * direction_ref[...].astype(f32)


def update_all(squares, weights, directions, steps):
    operands, in_specs, out_specs, out_shape = [squares], [whole_block(squares)], [], []
    for place, (weight, direction) in enumerate(zip(weights, directions)):
        spec = row_block(weight, steps) if place < 5 else whole_block(weight)
        operands += [weight, direction]
        in_specs += [spec] * 2
        out_specs += [spec]
        out_shape += [jax.ShapeDtypeStruct(weight.shape, f32)]
    return pl.pallas_call(
        update_all_kernel,
        grid=(steps,),
        in_specs=in_specs,
        out_specs=out_specs + [pl.BlockSpec((9, 2), lambda s: (0, 0))],
        out_shape=out_shape + [jax.ShapeDtypeStruct((9, 2), f32)],
        compiler_params=pltpu.CompilerParams(vmem_limit_bytes=127 * 2**19),
        name="update_all",
    )(*operands)


def norm_scale(stream, gain_row):
    return (
        stream * lax.rsqrt(jnp.mean(stream * stream, axis=-1, keepdims=True) + NORM_EPS) * gain_row
    )


def gelu_tanh(pre_act):
    return jax.nn.gelu(pre_act, approximate=True)


def dot(left, right, dims=((1,), (0,))):
    return lax.dot_general(left, right, (dims, ((), ())), preferred_element_type=f32)


def bucket_onehot(length):
    relative = length - jnp.arange(2 * length, dtype=jnp.int32)
    distance = jnp.abs(relative)
    far_bucket = 8 + sum(((distance >= threshold).astype(jnp.int32) for threshold in BUCKET_EDGES))
    bucket = jnp.where(distance < 8, distance, far_bucket) + jnp.where(relative > 0, 16, 0)
    return (bucket[:, None] == jnp.arange(BUCKETS)).astype(f32)


def after(value, *others):
    return lax.optimization_barrier((value, *others))[0]


def arrivals(groups):
    found = []
    for group in range(groups):
        found.append([])
        for hop in range(1, groups):
            for source, way in ((group - hop, 0), (group + hop, 1)):
                if 0 <= source < groups:
                    found[-1].append((source, way, hop))
    return found


def swap_cores(value):
    size = lax.axis_size("mdl")
    return lax.ppermute(value, "mdl", [(core, (core + 1) % size) for core in range(size)])


def shards(
    token_ids,
    item_lengths,
    prefix_lengths,
    group_live,
    partner,
    embedding,
    qkv_weight,
    out_weight,
    up_weight,
    down_weight,
    bias_table,
    norm_gains,
    embedding_first,
    embedding_second,
    qkv_first,
    qkv_second,
    out_first,
    out_second,
    up_first,
    up_second,
    down_first,
    down_second,
    bias_first,
    bias_second,
    gains_first,
    gains_second,
):
    item_count, length = token_ids.shape
    features, vocab = embedding.shape
    grp_size, dat_size, mdl_size = lax.axis_size("grp"), lax.axis_size("dat"), lax.axis_size("mdl")
    group_index, dat_index, mdl_index = lax.axis_index("grp"), lax.axis_index("dat"), lax.axis_index("mdl")
    mine = item_count // mdl_size
    rows = mine * length
    pair_rows = rows // 2
    chunk = min(512, pair_rows)
    chunks = pair_rows // chunk
    group_items = item_count * dat_size
    width = features * dat_size
    first_slot = dat_index * item_count + mdl_index * mine

    tn = ((0,), (0,))
    nt = ((1,), (1,))

    group_ids = share(token_ids, "dat", dat_size)

    def of_core(table, core):
        return lax.dynamic_index_in_dim(table, core % mdl_size, 0, keepdims=False)

    def by_core(ids):
        lead = ids.shape[:-3]
        ids = ids.reshape(-1, dat_size, mdl_size, 2, chunks, chunk).transpose(2, 0, 1, 4, 3, 5)
        return ids.reshape(mdl_size, *lead, dat_size * chunks, 2, chunk)

    def gathered(*shards):
        return lax.all_gather(
            jnp.concatenate([shard.astype(bf) for shard in shards], axis=1), "dat", axis=0, tiled=True
        )

    def halves(own, *widths):
        both = (own, swap_cores(own))
        edges = [0]
        for part in widths:
            edges.append(edges[-1] + part)
        return [[part[:, low:high] for part in both] for low, high in zip(edges, edges[1:])]

    flat_qkv = qkv_weight.reshape(features, -1)
    first_own = gathered(flat_qkv, out_weight.T)
    onehot = bucket_onehot(length)
    line_halves = [
        jnp.einsum("rb,bh->hr", onehot, table, precision=MAX_PRECISION)
        for table in (bias_table, swap_cores(bias_table))
    ]

    looked_up = gather_rows(embedding, of_core(by_core(group_ids), mdl_index))
    spread = lax.all_to_all(
        looked_up.reshape(dat_size, pair_rows, 2 * features), "dat", split_axis=0, concat_axis=0, tiled=True
    )
    second_own = gathered(after(up_weight, looked_up), after(down_weight, looked_up))
    item_lengths, prefix_lengths, partner = after((item_lengths, prefix_lengths, partner), looked_up)
    my_lengths, my_prefixes, my_partner = [
        lax.dynamic_slice_in_dim(value, mdl_index * mine, mine) for value in (item_lengths, prefix_lengths, partner)
    ]
    embedded_low, normed_one = assemble(spread, norm_gains[0])
    embedded = embedded_low.astype(f32)
    qkv_halves, out_halves = halves(after(first_own, spread), flat_qkv.shape[1], out_weight.shape[0])
    qkv_rows = [dot(normed_one, weight).astype(bf).reshape(mine, length, -1) for weight in qkv_halves]
    mixed, log_totals = zip(*[attend(item_qkv, lines, my_lengths) for item_qkv, lines in zip(qkv_rows, line_halves)])
    mixed_rows = [heads.reshape(rows, -1) for heads in mixed]
    up_halves, down_halves = halves(after(second_own, *mixed), up_weight.shape[1], down_weight.shape[1])
    after_attn = embedded + (dot(mixed_rows[0], out_halves[0], nt) + dot(mixed_rows[1], out_halves[1], nt))
    normed_two_f, norm_two_back = jax.vjp(norm_scale, after_attn, norm_gains[1])
    normed_two = normed_two_f.astype(bf)
    gate_acts, gelu_backs = zip(*[jax.vjp(gelu_tanh, dot(normed_two, weight)) for weight in up_halves])
    activated = [act.astype(bf) for act in gate_acts]
    after_ffn = after_attn + (
        dot(activated[0], down_halves[0], nt) + dot(activated[1], down_halves[1], nt)
    )
    positions = jnp.arange(length)
    pool_mask = (
        (positions[None, :] >= my_prefixes[:, None]) & (positions[None, :] < my_lengths[:, None])
    ).astype(f32)

    def pool_tail(stream, gain_row):
        normed_three = norm_scale(stream, gain_row).reshape(mine, length, -1)
        pooled = jnp.sum(normed_three * pool_mask[:, :, None], axis=1) / jnp.sum(pool_mask, axis=1, keepdims=True)
        return pooled * lax.rsqrt(jnp.sum(pooled * pooled, axis=1, keepdims=True) + NORM_EPS)

    vectors, tail_back = jax.vjp(pool_tail, after_ffn, norm_gains[2])

    partner_row = jnp.pad(my_partner.astype(f32), (0, width - mine))[None]
    plane_facts = jnp.concatenate([vectors, partner_row, jnp.zeros((-(mine + 1) % 8, width), f32)], axis=0)
    plane_facts, all_ids = share_both(
        plane_facts, group_ids.reshape(-1, length), ("dat", "mdl"), "grp", (dat_size, mdl_size, grp_size)
    )
    group_vectors = plane_facts[:, :mine].reshape(group_items, width)
    group_partner = plane_facts[:, mine, :mine].reshape(group_items).astype(jnp.int32)
    all_ids = by_core(all_ids.reshape(grp_size, dat_size, item_count, length))
    live_count = jnp.sum(jnp.where(jnp.arange(grp_size) == group_index, group_live, 0))
    live_total = jnp.sum(group_live).astype(f32)
    slots = jnp.arange(group_items)
    live_rows = slots < live_count
    logits = jnp.dot(group_vectors, group_vectors.T, precision=MAX_PRECISION) / SOFTMAX_WARMTH
    allowed = live_rows[None, :] & (slots[None, :] != slots[:, None])
    masked = jnp.where(allowed, logits, MASK_FILL)
    row_top = jnp.max(masked, axis=1, keepdims=True)
    log_total = row_top[:, 0] + jnp.log(jnp.sum(jnp.exp(masked - row_top), axis=1))
    mate_hits = slots[None, :] == group_partner[:, None]
    target = jnp.sum(jnp.where(mate_hits, logits, 0.0), axis=1)
    loss_part = jnp.sum(jnp.where(live_rows, log_total - target, 0.0))
    row_weight = jnp.where(live_rows, 1.0 / live_total, 0.0)
    grad_logits = (
        row_weight[:, None] * (jnp.exp(masked - log_total[:, None]) - mate_hits.astype(f32)) / SOFTMAX_WARMTH
    )
    my_pulls = lax.dynamic_slice_in_dim(grad_logits + grad_logits.T, first_slot, mine)
    grad_vectors = jnp.dot(my_pulls, group_vectors, precision=MAX_PRECISION)

    def both_cores(own, other):
        return (own + swap_cores(other.astype(bf)).astype(f32)).astype(bf)

    def scattered(total):
        return lax.psum_scatter(total, "dat", scatter_dimension=0, tiled=True)

    grad_after_ffn, grad_gain_three = tail_back(grad_vectors)
    grad_ffn = grad_after_ffn.astype(bf)
    total_down = both_cores(*[dot(grad_ffn, act, tn) for act in activated])
    grad_gates = [
        back(dot(grad_ffn, weight))[0].astype(bf) for back, weight in zip(gelu_backs, down_halves)
    ]
    total_up = both_cores(*[dot(normed_two, grad_gate, tn) for grad_gate in grad_gates])
    part_ffn = scattered(jnp.concatenate([total_down, total_up], axis=1))
    two_back = dot(grad_gates[0], up_halves[0], nt) + dot(grad_gates[1], up_halves[1], nt)
    grad_after_attn, grad_gain_two = norm_two_back(two_back)
    grad_after_attn = grad_after_attn + grad_after_ffn
    grad_attn = grad_after_attn.astype(bf)
    total_out = both_cores(*[dot(grad_attn, heads, tn) for heads in mixed_rows])
    grad_mixed = [dot(grad_attn, weight).astype(bf).reshape(mine, length, -1) for weight in out_halves]
    grad_qkv_items, grad_lines = zip(
        *[
            attend_back(item_qkv, lines, my_lengths, stats, grad)
            for item_qkv, lines, stats, grad in zip(qkv_rows, line_halves, log_totals, grad_mixed)
        ]
    )
    grad_qkv_rows = [grad.reshape(rows, -1) for grad in grad_qkv_items]
    one_back = dot(grad_qkv_rows[0], qkv_halves[0], nt) + dot(grad_qkv_rows[1], qkv_halves[1], nt)
    outgoing, grad_gain_one = pack_back(one_back, embedded_low, grad_after_attn, norm_gains[0], features)
    total_qkv = both_cores(*[dot(normed_one, grad, tn) for grad in grad_qkv_rows])
    total_rest = jnp.concatenate([total_qkv, total_out], axis=1)

    grad_bias_own, grad_bias_other = [
        jnp.einsum("rb,hr->hb", onehot, grad, precision=MAX_PRECISION) for grad in grad_lines
    ]
    grad_bias_all = jnp.where(
        mdl_index == 0,
        jnp.concatenate([grad_bias_own, grad_bias_other], axis=0),
        jnp.concatenate([grad_bias_other, grad_bias_own], axis=0),
    )
    leader = ((dat_index == 0) & (mdl_index == 0)).astype(f32)
    gain_lines = jnp.stack([grad_gain_one, grad_gain_two, grad_gain_three]).reshape(-1, LANES)
    loss_line = jnp.full((1, LANES), loss_part * leader)
    small = jnp.concatenate(
        [gain_lines, jnp.pad(grad_bias_all, ((0, 0), (0, LANES - BUCKETS))), loss_line], axis=0
    )
    small = jnp.pad(small, ((0, -small.shape[0] % 8), (0, 0)))

    by_group = arrivals(grp_size)
    sources = [list(range(grp_size))] + [[found[slot][0] for found in by_group] for slot in range(grp_size - 1)]
    order = [(slot, 0) for slot in range(grp_size)]
    order[-1:] = [(grp_size - 2, 1), (grp_size - 1, 0), (grp_size - 1, 1)]

    def candidates(slot):
        found = [by_group[group][slot - 1][1:] for group in range(grp_size)]
        kinds = sorted(set(found))
        return kinds, [kinds.index(kind) for kind in found]

    picks = [[0] * grp_size if slot == 0 else candidates(slot)[1] for slot, _ in order]
    staged_ids, staged_flags, choices = stage_ids(after(all_ids, outgoing), order, sources, picks)

    outgoing = after(outgoing, part_ffn)
    own_rows = lax.all_to_all(outgoing, "dat", split_axis=0, concat_axis=0, tiled=True)
    own_rows = own_rows.reshape(dat_size * pair_rows, 2 * features)
    part_rest = scattered(after(total_rest, own_rows))
    moving = [[own_rows], [own_rows]]
    swapped = [[None], [None]]

    def swap(hop, *waits):
        for way in range(2):
            both = way == 1 and moving[0][hop] is moving[1][hop]
            swapped[way].append(swapped[0][hop] if both else swap_cores(after(moving[way][hop], *waits)))

    def move(hop, *waits):
        senders = range(hop - 1, grp_size - 1)
        upward = [(group, group + 1) for group in senders]
        downward = [(grp_size - 1 - group, grp_size - 2 - group) for group in senders]
        if {group for group, _ in upward} & {group for group, _ in downward}:
            for way, pairs in enumerate((upward, downward)):
                moving[way].append(lax.ppermute(after(moving[way][-1], *waits), "grp", pairs))
        else:
            rising = group_index >= hop - 1
            moved = lax.ppermute(after(jnp.where(rising, moving[0][-1], moving[1][-1]), *waits), "grp", upward + downward)
            moving[0].append(moved)
            moving[1].append(moved)

    def stage(first, count):
        segments = []
        for slot, other in order[first : first + count]:
            buffers = swapped if other else moving
            segments.append([own_rows] if slot == 0 else [buffers[way][hop] for way, hop in candidates(slot)[0]])
        return Stage(segments, choices, staged_ids, staged_flags, first, dat_size * chunks, features)

    move(1)
    first_table = scatter_rows(stage(0, 1), vocab)
    small = sum_all(after(small, first_table), ("dat", "mdl"), "grp", (dat_size, mdl_size, grp_size))
    for hop in range(2, grp_size - 1):
        move(hop, small)
        swap(hop - 1)
    early = stage(1, grp_size - 3)
    early.operands[0] = after(early.operands[0], part_rest)
    own_table = scatter_rows(early, vocab, (first_table,))
    swap(grp_size - 2, own_table)
    move(grp_size - 1, own_table)
    other_table = swap_cores(after(own_table, *[kept for way in swapped for kept in way[1:]]))
    late_table = scatter_rows(stage(grp_size - 2, 2), vocab)
    swap(grp_size - 1, late_table)
    last = stage(grp_size, 2)
    full_ffn, full_rest = lax.psum((after(part_ffn, late_table), part_rest), "grp")
    table_momentum, table_variance, table_direction, table_squares = finish(
        last,
        embedding,
        embedding_first,
        embedding_second,
        (own_table, other_table, late_table),
    )
    full_ffn, full_rest = after(full_ffn, table_squares), after(full_rest, table_squares)
    by_part = lambda value: value.transpose(1, 0, 2)
    weights = (by_part(qkv_weight), out_weight.T, up_weight, down_weight, bias_table.T, norm_gains)
    gradients = (full_ffn, full_rest, small)
    moments = (
        (by_part(qkv_first), by_part(qkv_second)),
        (out_first.T, out_second.T),
        (up_first, up_second),
        (down_first, down_second),
        (bias_first.T, bias_second.T),
        (gains_first, gains_second),
    )
    *results, square_table, loss_pair = small_moments(live_total, weights, gradients, moments, max(1, features // 48))
    squares = sum_over(table_squares, square_table, ("dat", "mdl"), (dat_size, mdl_size))
    updated = update_all(squares, (embedding, *weights), (table_direction, *results[2::3]), features // 16)
    outputs = [
        loss_pair,
        updated[-1],
        table_momentum,
        table_variance,
        updated[0],
    ]
    outputs.extend(by_part(value) for value in (results[0], results[1], updated[1]))
    outputs.extend(value.T for value in (results[3], results[4], updated[2]))
    for position in range(2, 6):
        three = (results[3 * position], results[3 * position + 1], updated[position + 1])
        outputs.extend(value.T if position == 4 else value for value in three)
    return tuple(outputs)


def solution(mesh):
    state = [
        P("dat", None),
        P("dat", None, "mdl"),
        P("mdl", "dat"),
        P("dat", "mdl"),
        P("dat", "mdl"),
        P(None, "mdl"),
        P(),
    ]
    placed = [P(("grp", "dat"), None), P(("grp", "dat")), P(("grp", "dat")), P(), P(("grp", "dat"))]
    placed += state + [spec for spec in state for _ in range(2)]
    return jax.shard_map(
        shards,
        mesh=mesh,
        in_specs=tuple(placed),
        out_specs=(P(), P(), *[spec for spec in state for _ in range(3)]),
        check_vma=False,
    )
```
